32 devices in a mesh: pipe: 4 (over z), dp: 4 (over y, x), tensor: 2 (over core).
Axes of the slice: x: 2, y: 2, z: 4, core: 2. Of those that a mesh axis runs over, the one named last changes fastest.
Arguments:
- up_weight: bfloat16 [4, 2048, 4096], P('pipe', None, 'tensor'), may hold values from -0.125 to 0.125
- down_weight: bfloat16 [4, 2048, 4096], P('pipe', None, 'tensor'), may hold values from -0.09375 to 0.09375
- gate_act: bfloat16 [4, 512, 4096], P('pipe', 'dp', 'tensor'), may hold values from -0.27734375 to 2.5
- hidden: bfloat16 [4, 512, 4096], P('pipe', 'dp', 'tensor'), may hold values from -6 to 6
- block_input: bfloat16 [4, 512, 2048], P('pipe', ('dp', 'tensor')), may hold values from -6 to 6
- norm_gain: float32 [4, 2048], P('pipe'), may hold values from 0.1 to 1.9
- loss_grad: bfloat16 [512, 2048], P(('dp', 'tensor')), may hold values from -0.796875 to 0.796875
- moment_one: float32 [4, 2048, 4096], P('pipe', 'dp', 'tensor'), may hold values from -6 to 6
- moment_two: float32 [4, 2048, 4096], P('pipe', 'dp', 'tensor'), may hold values from 1 to 30
Outputs:
- input_grad: bfloat16 [4, 512, 2048], P('pipe', ('dp', 'tensor'))
- new_moment_one: float32 [4, 2048, 4096], P('pipe', 'dp', 'tensor')
- new_moment_two: float32 [4, 2048, 4096], P('pipe', 'dp', 'tensor')
- new_down_weight: float32 [4, 2048, 4096], P('pipe', 'dp', 'tensor')
The draws below stay inside these ranges and needn't reach their ends.
All inputs are finite; a program needn't handle non-finite values.
Results may differ from the reference program's by a relative error of at most 0.028.
Values may be sent and summed in bfloat16 or wider, within the bound.
No kernel may reach another device: no remote copies, remote signals or barrier semaphores. Data moves between devices by JAX's collectives and lax.ppermute only.
A program may use at most 128 MiB of HBM per device.

```python
import math
import jax
import jax.numpy as jnp
from jax import lax

D = 2048
FF = 4096
TOK = 128
TOKENS = 512
N_PIPE = 4
N_DP = 4
N_TENSOR = 2


def raised(drawn, stream_key, source, target, shards_of, factor):
    def block_of(axis_at):
        return (jnp.arange(drawn.shape[axis_at]) // (drawn.shape[axis_at] // shards_of)).reshape((-1,) + (1,) * (drawn.ndim - 1 - axis_at))

    one_side = jax.random.permutation(stream_key, shards_of)[block_of(target)]
    other_side = (block_of(target) + shards_of // 2) % shards_of
    return jnp.where((block_of(source) == one_side) | (block_of(source) == other_side), factor * drawn, drawn)


def shard_levels(stream_key, shape, pieces, smallest, largest):
    level, own = 1.0, jax.random.fold_in(stream_key, 6)
    for position, blocks in pieces:
        steps = jnp.exp(jax.random.uniform(jax.random.fold_in(own, position), (blocks,), jnp.float32, smallest / len(pieces), largest / len(pieces)))
        level = level * jnp.repeat(steps, shape[position] // blocks).reshape([-1 if axis == position else 1 for axis in range(len(shape))])
    return level


def noise(rng, extent, spread, most, split=(), held_as=jnp.bfloat16):
    drawn = spread * jax.random.normal(rng, extent, jnp.float32)
    if split:
        drawn = drawn * shard_levels(rng, extent, split, -0.22, 0.18)
    return jnp.clip(drawn, -most, most).astype(held_as)


def heavy_noise(stream_key, extent, scale, most, shards, heavy, held_as=jnp.bfloat16):
    entries = scale * jax.random.normal(stream_key, extent, jnp.float32)
    if shards:
        entries = entries * shard_levels(stream_key, extent, shards, -0.22, 0.18)
    return jnp.clip(raised(entries, jax.random.fold_in(stream_key, 3), *heavy), -most, most).astype(held_as)


def setup_inputs(seed: int = 0) -> dict:
    key_list = jax.random.split(jax.random.key(seed), 10)
    return {
        "up_weight": noise(key_list[0], (N_PIPE, D, FF), D ** -0.5, 0.125, ((0, 4), (2, 2))),
        "down_weight": noise(key_list[1], (N_PIPE, D, FF), FF ** -0.5, 0.09375, ((0, 4), (2, 2))),
        "gate_act": jnp.clip(-0.27734375 + 2.7773438 * jax.random.uniform(key_list[2], (N_PIPE, TOKENS, FF), jnp.float32) ** shard_levels(key_list[2], (N_PIPE, TOKENS, FF), ((0, 4), (1, 4), (2, 2)), -0.2, 0.2), -0.27734375, 2.5).astype(jnp.bfloat16),
        "hidden": noise(key_list[3], (N_PIPE, TOKENS, FF), 1.0, 6.0, ((0, 4), (1, 4), (2, 2))),
        "block_input": noise(key_list[4], (N_PIPE, TOKENS, D), 1.0, 6.0, ((0, 4), (1, 8))),
        "norm_gain": jnp.clip(1.0 + 0.18 * jax.random.normal(key_list[5], (N_PIPE, D), jnp.float32), 0.1, 1.9),
        "loss_grad": heavy_noise(key_list[6], (TOKENS, D), 0.1, 0.796875, ((0, 8),), (0, 1, 8, 2.0)),
        "moment_one": noise(key_list[7], (N_PIPE, D, FF), 1.0, 6.0, ((0, 4), (1, 4), (2, 2)), jnp.float32),
        "moment_two": jnp.clip(jnp.exp(math.log(30.0) - 3.4011974 * jax.random.uniform(key_list[8], (N_PIPE, D, FF), jnp.float32) ** shard_levels(key_list[8], (N_PIPE, D, FF), ((0, 4), (1, 4), (2, 2)), -0.2, 0.2)), 1.0, 30.0),
    }


EPS_NORM = 1e-05
EPS_ADAM = 1e-08
BETA_ONE = 0.9
BETA_TWO = 0.95
RATE = 0.01
DECAY = 0.1
CORRECT_ONE = 1.0 - 0.9 ** 10
CORRECT_TWO = 1.0 - 0.95 ** 10

def rounded(value):
    return lax.optimization_barrier(value.astype(jnp.bfloat16)).astype(jnp.float32)

def reference(up_weight, down_weight, gate_act, hidden, block_input, norm_gain, loss_grad, moment_one, moment_two):
    upstream = loss_grad
    width = FF // N_TENSOR
    grads_out = []
    firsts = []
    seconds = []
    weights = []
    for layer in reversed(range(N_PIPE)):
        unit_grad = (jnp.dot(upstream, down_weight[layer], preferred_element_type=jnp.float32) * gate_act[layer].astype(jnp.float32)).astype(jnp.bfloat16)
        normed = jnp.zeros((TOKENS, D), jnp.float32)
        for block in range(N_TENSOR):
            left = unit_grad[:, block * width:(block + 1) * width]
            right = up_weight[layer][:, block * width:(block + 1) * width]
            term = lax.dot_general(left, right, (((1,), (1,)), ((), ())), preferred_element_type=jnp.float32)
            normed = normed + rounded(term)
        rows_in = block_input[layer].astype(jnp.float32)
        inverse_rms = lax.rsqrt(lax.optimization_barrier(jnp.mean(rows_in * rows_in, axis=-1, keepdims=True)) + EPS_NORM)
        scaled = normed * norm_gain[layer][None, :]
        mean_term = lax.optimization_barrier(jnp.mean(rows_in * scaled, axis=-1, keepdims=True))
        input_grad = (upstream.astype(jnp.float32) + inverse_rms * scaled - rows_in * inverse_rms ** 3 * mean_term).astype(jnp.bfloat16)
        upstream_blocks = upstream.reshape(N_DP, TOK, D)
        hidden_blocks = hidden[layer].reshape(N_DP, TOK, FF)

        def add_block(carry, pair):
            term = jnp.dot(pair[0].T, pair[1], preferred_element_type=jnp.float32)
            return (carry + rounded(term), None)
        gradient, _ = lax.scan(add_block, jnp.zeros((D, FF), jnp.float32), (upstream_blocks, hidden_blocks))
        first = BETA_ONE * moment_one[layer] + (1.0 - BETA_ONE) * gradient
        second = BETA_TWO * moment_two[layer] + (1.0 - BETA_TWO) * gradient * gradient
        current = down_weight[layer].astype(jnp.float32)
        direction = first / CORRECT_ONE / (jnp.sqrt(second / CORRECT_TWO) + EPS_ADAM) + DECAY * current
        grads_out.append(input_grad)
        firsts.append(first)
        seconds.append(second)
        weights.append(current - RATE * direction)
        upstream = input_grad
    grads_out = grads_out[::-1]
    firsts = firsts[::-1]
    seconds = seconds[::-1]
    weights = weights[::-1]
    return (jnp.stack(grads_out), jnp.stack(firsts), jnp.stack(seconds), jnp.stack(weights))
```

```python
import functools
import jax
import jax.numpy as jnp
from jax import lax
from jax.experimental import pallas as pl
from jax.experimental.pallas import tpu as pltpu
from jax.sharding import PartitionSpec as P

EPS_NORM = 1e-05
EPS_ADAM = 1e-08
BETA_ONE = 0.9
BETA_TWO = 0.95
RATE = 0.01
DECAY = 0.1
CORRECT_ONE = 1.0 - 0.9**10
CORRECT_TWO = 1.0 - 0.95**10

MIB = 2**20
VMEM = pl.BlockSpec(memory_space=pltpu.VMEM)
F32 = jnp.float32
BF16 = jnp.bfloat16


def tile_of(extent, most):
    tile = min(extent, most)
    while extent % tile:
        tile //= 2
    return tile


def step_kernel(layer, sizes, own_ref, *refs):
    parts, share, width, units = sizes
    peer_refs = refs[: parts - 1]
    down_ref, up_ref, gate_ref, kept_ref = refs[parts - 1 : parts + 3]
    sent_refs = refs[parts + 3 : 2 * parts + 2]
    rows_ref, unit_ref = refs[2 * parts + 2 :]
    me = lax.axis_index("tensor")

    @pl.when(lax.axis_index("pipe") == layer)
    def _():
        rows_ref[0:share, :] = own_ref[...]
        for k in range(1, parts):
            rows_ref[k * share : (k + 1) * share, :] = peer_refs[k - 1][...]
        tile = tile_of(units, 1024)

        @pl.loop(0, units // tile)
        def _(j):
            cols = pl.ds(pl.multiple_of(j * tile, tile), tile)
            term = jnp.dot(rows_ref[...], down_ref[:, cols], preferred_element_type=F32)
            for k in range(parts):
                at = pl.multiple_of(lax.rem(me + k, parts) * share, share)
                gates = gate_ref[pl.ds(at, share), cols].astype(F32)
                unit_ref[k * share : (k + 1) * share, cols] = (
                    term[k * share : (k + 1) * share] * gates
                ).astype(BF16)

        tile = tile_of(width, 1024)

        @pl.loop(0, width // tile)
        def _(j):
            cols = pl.ds(pl.multiple_of(j * tile, tile), tile)
            term = lax.dot_general(
                unit_ref[...], up_ref[cols, :], (((1,), (1,)), ((), ())), preferred_element_type=F32
            )
            kept_ref[:, cols] = term[0:share]
            for k in range(1, parts):
                sent_refs[k - 1][:, cols] = term[k * share : (k + 1) * share].astype(BF16)


def section_step(layer, own, peers, w_down, w_up, gates):
    share, width = own.shape
    units = w_down.shape[1]
    parts = len(peers) + 1
    rows = share * parts
    outs = pl.pallas_call(
        functools.partial(step_kernel, layer, (parts, share, width, units)),
        out_shape=[jax.ShapeDtypeStruct((share, width), F32)]
        + [jax.ShapeDtypeStruct((share, width), BF16)] * (parts - 1),
        in_specs=[VMEM] * (parts + 3),
        out_specs=[VMEM] * parts,
        scratch_shapes=[pltpu.VMEM((rows, width), BF16), pltpu.VMEM((rows, units), BF16)],
        compiler_params=pltpu.CompilerParams(vmem_limit_bytes=8 * MIB),
        cost_estimate=pl.CostEstimate(
            flops=4 * rows * width * units, bytes_accessed=4 * width * units, transcendentals=0
        ),
        name="section_step",
    )(own, *peers, w_down, w_up, gates)
    return outs[0], outs[1:]


def norm_kernel(layer, parts, kept_ref, *refs):
    arrived = refs[: parts - 1]
    up_ref, in_ref, gain_ref = refs[parts - 1 : parts + 2]
    earlier = refs[parts + 2 : -1]
    out_ref = refs[-1]
    segment = lax.axis_index("pipe")

    @pl.when(segment == layer)
    def _():
        normed = kept_ref[...]
        for ref in arrived:
            normed = normed + ref[...].astype(F32)
        rows_in = in_ref[...].astype(F32)
        inverse_rms = lax.rsqrt(jnp.mean(rows_in * rows_in, axis=-1, keepdims=True) + EPS_NORM)
        scaled = normed * gain_ref[...]
        mean_term = jnp.mean(rows_in * scaled, axis=-1, keepdims=True)
        out_ref[...] = (
            up_ref[...].astype(F32)
            + inverse_rms * scaled
            - rows_in * (inverse_rms * inverse_rms * inverse_rms * mean_term)
        ).astype(BF16)

    for above, ref in enumerate(earlier):

        @pl.when(segment == layer + len(earlier) - above)
        def _(ref=ref):
            out_ref[...] = ref[...]


def norm_step(layer, kept, arrived, upstream, rows_in, gain, earlier=()):
    parts = len(arrived) + 1
    return pl.pallas_call(
        functools.partial(norm_kernel, layer, parts),
        out_shape=jax.ShapeDtypeStruct(upstream.shape, BF16),
        in_specs=[VMEM] * (parts + 3 + len(earlier)),
        out_specs=VMEM,
        compiler_params=pltpu.CompilerParams(vmem_limit_bytes=8 * MIB),
        name="norm_step",
    )(kept, *arrived, upstream, rows_in, gain, *earlier)


def split_kernel(owners, *refs):
    sections = len(refs) - owners
    share = refs[sections].shape[1]
    me = lax.axis_index("dp")
    for s in range(sections):

        @pl.when(lax.axis_index("pipe") == sections - 1 - s)
        def _(s=s):
            for k in range(owners):
                at = pl.multiple_of((me ^ k) * share, share)
                refs[sections + k][...] = refs[s][:, pl.ds(at, share)]


def split_for_owners(upstreams, owners):
    tokens, width = upstreams[0].shape
    return pl.pallas_call(
        functools.partial(split_kernel, owners),
        out_shape=[jax.ShapeDtypeStruct((tokens, width // owners), BF16)] * owners,
        in_specs=[VMEM] * len(upstreams),
        out_specs=[VMEM] * owners,
        compiler_params=pltpu.CompilerParams(vmem_limit_bytes=4 * MIB),
        name="split_for_owners",
    )(*upstreams)


def adam_update(gradient, current, moment_one, moment_two):
    first = BETA_ONE * moment_one + (1.0 - BETA_ONE) * gradient
    second = BETA_TWO * moment_two + (1.0 - BETA_TWO) * gradient * gradient
    direction = (first / CORRECT_ONE) / (jnp.sqrt(second / CORRECT_TWO) + EPS_ADAM) + DECAY * current
    return first, second, current - RATE * direction


def adam_kernel(grad_refs, sizes, *refs):
    owners, parts, share, rows, tile = sizes
    up_refs = refs[:grad_refs]
    hidden_ref, down_ref, one_ref, two_ref, first_ref, second_ref, updated_ref, turned_ref = refs[grad_refs:]
    me = lax.axis_index("dp")
    part = lax.axis_index("tensor")

    @pl.when(pl.program_id(0) == 0)
    def _():
        for p in range(parts):
            for k in range(owners):
                at = (me ^ k) * parts + lax.rem(part + p, parts)
                turned_ref[pl.ds(pl.multiple_of(at * share, share), share), :] = up_refs[p * owners + k][...]

    gradient = lax.dot_general(
        turned_ref[...], hidden_ref[...], (((0,), (0,)), ((), ())), preferred_element_type=F32
    )
    cols = pl.ds(pl.multiple_of(pl.program_id(0) * tile, tile), tile)
    current = down_ref[pl.ds(pl.multiple_of(me * rows, rows), rows), cols].astype(F32)
    first_ref[...], second_ref[...], updated_ref[...] = adam_update(
        gradient, current, one_ref[:, cols], two_ref[:, cols]
    )


def adam_step(blocks, hidden_all, w_down, moment_one, moment_two, owners, parts):
    rows, units = moment_one.shape
    share = blocks[0].shape[0]
    tokens = hidden_all.shape[0]
    tile = tile_of(units, 256)
    out = pl.BlockSpec((rows, tile), lambda j: (0, j))
    return pl.pallas_call(
        functools.partial(adam_kernel, len(blocks), (owners, parts, share, rows, tile)),
        out_shape=[jax.ShapeDtypeStruct((rows, units), F32)] * 3,
        grid=(units // tile,),
        in_specs=[VMEM] * len(blocks)
        + [pl.BlockSpec((tokens, tile), lambda j: (0, j)), VMEM, VMEM, VMEM],
        out_specs=[out] * 3,
        scratch_shapes=[pltpu.VMEM((tokens, rows), BF16)],
        compiler_params=pltpu.CompilerParams(vmem_limit_bytes=24 * MIB),
        name="adam_step",
    )(*blocks, hidden_all, w_down, moment_one, moment_two)


def adam_general(upstreams, hidden_all, w_down, moment_one, moment_two):
    owners = lax.axis_size("dp")
    sections = len(upstreams)
    segment = lax.axis_index("pipe")
    own = upstreams[0]
    for s in range(1, sections):
        own = jnp.where(segment == sections - 1 - s, upstreams[s], own)
    mine = lax.all_to_all(own, "dp", split_axis=1, concat_axis=0, tiled=True)
    share, rows = own.shape[0], mine.shape[1]
    turned = lax.all_gather(mine.reshape(owners, share, rows), "tensor", axis=1, tiled=True)
    gradient = lax.dot_general(
        turned.reshape(-1, rows), hidden_all, (((0,), (0,)), ((), ())), preferred_element_type=F32
    )
    at = lax.axis_index("dp") * rows
    current = lax.dynamic_slice_in_dim(w_down, at, rows, 0).astype(F32)
    return adam_update(gradient, current, moment_one, moment_two)


def from_peers(value, axis):
    size = lax.axis_size(axis)
    return [lax.ppermute(value, axis, [((i + k) % size, i) for i in range(size)]) for k in range(1, size)]


def to_peers(values, axis):
    size = lax.axis_size(axis)
    return [
        lax.ppermute(value, axis, [(i, (i + k) % size) for i in range(size)])
        for k, value in enumerate(values, 1)
    ]


def on_device(
    up_weight,
    down_weight,
    gate_act,
    hidden,
    block_input,
    norm_gain,
    loss_grad,
    moment_one,
    moment_two,
):
    w_up, w_down, gates, rows_in = up_weight[0], down_weight[0], gate_act[0], block_input[0]
    sections = lax.axis_size("pipe")
    owners = lax.axis_size("dp")
    parts = lax.axis_size("tensor")
    hidden_all = lax.all_gather(hidden[0], "dp", axis=0, tiled=True)
    by_blocks = owners <= 8 and owners & (owners - 1) == 0 and rows_in.shape[1] // owners % 128 == 0
    upstreams = [loss_grad]
    grads = []
    for layer in reversed(range(sections)):
        upstream = upstreams[-1]
        peers = from_peers(upstream, "tensor")
        if layer == 0 and by_blocks:
            blocks = split_for_owners(upstreams, owners)
            blocks = [blocks[0]] + [
                lax.ppermute(blocks[k], "dp", [(i, i ^ k) for i in range(owners)])
                for k in range(1, owners)
            ]
            blocks = blocks + [
                block for turn in zip(*[from_peers(b, "tensor") for b in blocks]) for block in turn
            ]
        kept, sent = section_step(layer, upstream, peers, w_down, w_up, gates)
        arrived = to_peers(sent, "tensor")
        grad = norm_step(
            layer, kept, arrived, upstream, rows_in, norm_gain, grads if layer == 0 else ()
        )
        grads.append(grad)
        if layer:
            upstreams.append(lax.ppermute(grad, "pipe", [(layer, layer - 1)]))
    if by_blocks:
        first, second, updated = adam_step(
            blocks, hidden_all, w_down, moment_one[0], moment_two[0], owners, parts
        )
    else:
        first, second, updated = adam_general(
            upstreams, hidden_all, w_down, moment_one[0], moment_two[0]
        )
    return (grads[-1][None], first[None], second[None], updated[None])


def solution(mesh):
    in_specs = (
        P("pipe", None, "tensor"),
        P("pipe", None, "tensor"),
        P("pipe", "dp", "tensor"),
        P("pipe", "dp", "tensor"),
        P("pipe", ("dp", "tensor"), None),
        P("pipe", None),
        P(("dp", "tensor"), None),
        P("pipe", "dp", "tensor"),
        P("pipe", "dp", "tensor"),
    )
    out_specs = (
        P("pipe", ("dp", "tensor"), None),
        P("pipe", "dp", "tensor"),
        P("pipe", "dp", "tensor"),
        P("pipe", "dp", "tensor"),
    )
    return jax.shard_map(
        on_device, mesh=mesh, in_specs=in_specs, out_specs=out_specs, check_vma=False
    )
```

```python
import functools
import jax
import jax.numpy as jnp
from jax import lax
from jax.experimental import pallas as pl
from jax.experimental.pallas import tpu as pltpu
from jax.sharding import PartitionSpec as P

EPS_NORM = 1e-05
EPS_ADAM = 1e-08
BETA_ONE = 0.9
BETA_TWO = 0.95
RATE = 0.01
DECAY = 0.1
CORRECT_ONE = 1.0 - 0.9**10
CORRECT_TWO = 1.0 - 0.95**10

MIB = 2**20
VMEM = pl.BlockSpec(memory_space=pltpu.VMEM)
CHEAP = pl.CostEstimate(flops=0, bytes_accessed=0, transcendentals=0)
F32 = jnp.float32
BF16 = jnp.bfloat16


def tile_of(extent, most):
    tile = min(extent, most)
    while extent % tile:
        tile //= 2
    return tile


def copies(pairs, sem, chunks):
    started = []
    for n, (source, target) in enumerate(pairs):
        rows = source.shape[0] // chunks
        cut = [slice(c * rows, (c + 1) * rows) for c in range(chunks)]
        started.append(
            [pltpu.make_async_copy(source.at[r], target.at[r], sem.at[n, c]) for c, r in enumerate(cut)]
        )
    for array in started:
        for copy in array:
            copy.start()
    return started


def stage(arrays, split=(), after=()):
    pieces = [(n, slice(None)) for n in range(len(arrays))]
    for n, array in enumerate(split, len(arrays)):
        half = array.shape[0] // 2
        pieces += [(n, slice(0, half)), (n, slice(half, 2 * half))]
    arrays = [*arrays, *split]
    shapes = [(arrays[n][rows].shape if rows.start is not None else arrays[n].shape) for n, rows in pieces]
    count = len(arrays)

    def kernel(*refs):
        sources, targets, sem = refs[:count], refs[count + len(after) : -1], refs[-1]
        pairs = [(sources[n].at[rows], target) for (n, rows), target in zip(pieces, targets)]
        for array in copies(pairs, sem, 2):
            for copy in array:
                copy.wait()

    return pl.pallas_call(
        kernel,
        out_shape=[pltpu.VMEM(shape, arrays[n].dtype) for (n, _), shape in zip(pieces, shapes)],
        in_specs=[pl.BlockSpec(memory_space=pltpu.HBM)] * count
        + [pl.BlockSpec(memory_space=pl.ANY)] * len(after),
        out_specs=[VMEM] * len(pieces),
        scratch_shapes=[pltpu.SemaphoreType.DMA((len(pieces), 2))],
        compiler_params=pltpu.CompilerParams(vmem_limit_bytes=4 * MIB),
        cost_estimate=pl.CostEstimate(
            flops=0, bytes_accessed=sum(2 * a.size * a.dtype.itemsize for a in arrays), transcendentals=0
        ),
        name="stage",
    )(*[pltpu.with_memory_space_constraint(a, pltpu.HBM) for a in arrays], *after)


def stage_in_section(arrays, wanted, held, after):
    count = len(arrays)

    def kernel(*refs):
        sources, targets, sem = refs[:count], refs[count + len(held) + len(after) : -1], refs[-1]

        @pl.when(wanted(lax.axis_index("pipe")))
        def _():
            for array in copies(list(zip(sources, targets)), sem, 2):
                for copy in array:
                    copy.wait()

    return pl.pallas_call(
        kernel,
        out_shape=[pltpu.VMEM(a.shape, a.dtype) for a in arrays],
        in_specs=[pl.BlockSpec(memory_space=pltpu.HBM)] * count
        + [VMEM] * len(held)
        + [pl.BlockSpec(memory_space=pl.ANY)] * len(after),
        out_specs=[VMEM] * count,
        input_output_aliases={count + n: n for n in range(len(held))},
        scratch_shapes=[pltpu.SemaphoreType.DMA((count, 2))],
        compiler_params=pltpu.CompilerParams(vmem_limit_bytes=4 * MIB),
        cost_estimate=CHEAP,
        name="stage_in_section",
    )(*[pltpu.with_memory_space_constraint(a, pltpu.HBM) for a in arrays], *held, *after)


def unit_grads(parts, share, rows_ref, down_ref, gate_ref, unit_ref):
    me = lax.axis_index("tensor")
    term = jnp.dot(rows_ref[...], down_ref[...], preferred_element_type=F32)
    for k in range(parts):
        at = pl.multiple_of(lax.rem(me + k, parts) * share, share)
        gates = gate_ref[pl.ds(at, share), :].astype(F32)
        unit_ref[k * share : (k + 1) * share, :] = (term[k * share : (k + 1) * share] * gates).astype(BF16)


def hand_out(share, term, cols, kept_ref, sent_refs):
    kept_ref[:, cols] = term[0:share]
    for k, ref in enumerate(sent_refs, 1):
        ref[:, cols] = term[k * share : (k + 1) * share].astype(BF16)


def fill_rows(share, rows_ref, own_ref, peer_refs):
    rows_ref[0:share, :] = own_ref[...]
    at, row = 0, share
    for ref in peer_refs:
        rows_ref[row : row + share, at : at + ref.shape[1]] = ref[...]
        at += ref.shape[1]
        if at == rows_ref.shape[1]:
            at, row = 0, row + share


def step_kernel(layer, parts, pieces, own_ref, *refs):
    peer_refs, refs = refs[:pieces], refs[pieces:]
    down_ref, turned_ref, gate_ref, kept_ref = refs[:4]
    sent_refs = refs[4 : parts + 3]
    rows_ref, unit_ref = refs[parts + 3 :]
    share = own_ref.shape[0]

    @pl.when(lax.axis_index("pipe") == layer)
    def _():
        fill_rows(share, rows_ref, own_ref, peer_refs)
        unit_grads(parts, share, rows_ref, down_ref, gate_ref, unit_ref)
        term = jnp.dot(unit_ref[...], turned_ref[...], preferred_element_type=F32)
        hand_out(share, term, slice(None), kept_ref, sent_refs)


def first_kernel(layer, parts, pieces, own_ref, *refs):
    peer_refs, refs = refs[:pieces], refs[pieces:]
    down_ref, up_ref, gate_ref, turned_ref, kept_ref = refs[:5]
    sent_refs = refs[5 : parts + 4]
    rows_ref, unit_ref, held_ref, sem = refs[parts + 4 :]
    share = own_ref.shape[0]
    chunks = sem.shape[1]
    size = held_ref.shape[0] // chunks
    (arriving,) = copies([(up_ref, held_ref)], sem, chunks)
    starts = lax.axis_index("pipe") == layer

    @pl.when(starts)
    def _():
        fill_rows(share, rows_ref, own_ref, peer_refs)
        unit_grads(parts, share, rows_ref, down_ref, gate_ref, unit_ref)

    for c in range(chunks):
        cols = slice(c * size, (c + 1) * size)
        arriving[c].wait()

        @pl.when(starts)
        def _(cols=cols):
            term = lax.dot_general(
                unit_ref[...], held_ref[cols, :], (((1,), (1,)), ((), ())), preferred_element_type=F32
            )
            hand_out(share, term, cols, kept_ref, sent_refs)

        @pl.when(jnp.logical_not(starts))
        def _(cols=cols):
            turned_ref[:, cols] = held_ref[cols, :].T


def section_step(layer, own, peers, w_down, turned, gates, w_up=None, after=()):
    share, width = own.shape
    units = w_down.shape[1]
    pieces = len(peers)
    parts = sum(p.size for p in peers) // own.size + 1
    rows = share * parts
    first = w_up is not None
    out_shape = [jax.ShapeDtypeStruct((share, width), F32)]
    out_shape += [jax.ShapeDtypeStruct((share, width), BF16)] * (parts - 1)
    scratch = [pltpu.VMEM((rows, width), BF16), pltpu.VMEM((rows, units), BF16)]
    in_specs = [VMEM] * (pieces + 4) + [pl.BlockSpec(memory_space=pl.ANY)] * len(after)
    body = functools.partial(first_kernel if first else step_kernel, layer, parts, pieces)

    def kernel(*refs):
        body(*refs[: pieces + 4], *refs[pieces + 4 + len(after) :])

    if first:
        out_shape = [pltpu.VMEM((units, width), BF16)] + out_shape
        scratch += [pltpu.VMEM((width, units), BF16), pltpu.SemaphoreType.DMA((1, 4))]
        in_specs[pieces + 2] = pl.BlockSpec(memory_space=pltpu.HBM)
        operand = pltpu.with_memory_space_constraint(w_up, pltpu.HBM)
    else:
        operand = turned
    outs = pl.pallas_call(
        kernel,
        out_shape=out_shape,
        in_specs=in_specs,
        out_specs=[VMEM] * len(out_shape),
        scratch_shapes=scratch,
        compiler_params=pltpu.CompilerParams(vmem_limit_bytes=(20 if first else 12) * MIB),
        cost_estimate=CHEAP,
        name="section_step",
    )(own, *peers, w_down, operand, gates, *after)
    return outs


def norm_kernel(layer, parts, earlier, owners, passed, handed, kept_ref, *refs):
    arrived = refs[: parts - 1]
    up_ref, in_ref, gain_ref = refs[parts - 1 : parts + 2]
    refs = refs[parts + 2 :]
    earlier_refs, refs = refs[:earlier], refs[earlier:]
    first_ref, pass_refs, refs = refs[0], refs[1 : 1 + passed], refs[1 + passed :]
    out_ref, block_refs, handed_refs = refs[0], refs[1 : len(refs) - handed], refs[len(refs) - handed :]
    segment = lax.axis_index("pipe")

    def cut(source):
        size = source.shape[1] // owners
        for k, ref in enumerate(block_refs, 1):
            at = pl.multiple_of((lax.axis_index("dp") ^ k) * size, size)
            ref[...] = source[:, pl.ds(at, size)]

    @pl.when(segment == layer)
    def _():
        normed = kept_ref[...]
        for ref in arrived:
            normed = normed + ref[...].astype(F32)
        rows_in = in_ref[...].astype(F32)
        inverse_rms = lax.rsqrt(jnp.mean(rows_in * rows_in, axis=-1, keepdims=True) + EPS_NORM)
        scaled = normed * gain_ref[...]
        mean_term = jnp.mean(rows_in * scaled, axis=-1, keepdims=True)
        out_ref[...] = (
            up_ref[...].astype(F32)
            + inverse_rms * scaled
            - rows_in * (inverse_rms * inverse_rms * inverse_rms * mean_term)
        ).astype(BF16)
        cut(out_ref)

    for above, ref in enumerate(earlier_refs):

        @pl.when(segment == layer + earlier - above)
        def _(ref=ref):
            cut(ref)
            if layer == 0:
                out_ref[...] = ref[...]

    if block_refs:

        @pl.when(segment == 0)
        def _():
            cut(first_ref)

    sources = list(pass_refs)
    for target in handed_refs:
        at = 0
        while at < target.shape[0]:
            source = sources.pop(0)
            target[at : at + source.shape[0], :] = source[...]
            at += source.shape[0]


def norm_step(layer, kept, arrived, upstream, rows_in, gain, first, earlier=(), owners=1, passed=()):
    parts = len(arrived) + 1
    share, width = upstream.shape
    block = jax.ShapeDtypeStruct((share, width // owners), BF16)
    handed = [
        jax.ShapeDtypeStruct((sum(p.shape[0] for p in group), group[0].shape[1]), BF16) for group in passed
    ]
    passed = [p for group in passed for p in group]
    outs = pl.pallas_call(
        functools.partial(norm_kernel, layer, parts, len(earlier), owners, len(passed), len(handed)),
        out_shape=[jax.ShapeDtypeStruct(upstream.shape, BF16)]
        + [block] * (owners - 1)
        + handed,
        in_specs=[VMEM] * (parts + 4 + len(earlier) + len(passed)),
        out_specs=[VMEM] * (owners + len(handed)),
        compiler_params=pltpu.CompilerParams(vmem_limit_bytes=8 * MIB),
        cost_estimate=CHEAP,
        name="norm_step",
    )(kept, *arrived, upstream, rows_in, gain, *earlier, first, *passed)
    return outs[0], outs[1:owners], outs[owners:]


def collect_kernel(sections, *refs):
    upstream_refs, block_refs, out_ref = refs[:sections], refs[sections:-1], refs[-1]
    share, size = block_refs[0].shape
    at = pl.multiple_of(lax.axis_index("dp") * size, size)
    for s, ref in enumerate(upstream_refs):

        @pl.when(lax.axis_index("pipe") == sections - 1 - s)
        def _(ref=ref):
            out_ref[0:share, :] = ref[:, pl.ds(at, size)]

    for k, ref in enumerate(block_refs, 1):
        out_ref[k * share : (k + 1) * share, :] = ref[...]


def collect(upstreams, blocks, after):
    sections = len(upstreams)
    owners = len(blocks) + 1
    share, size = blocks[0].shape
    count = sections + len(blocks)

    def kernel(*refs):
        collect_kernel(sections, *refs[:count], refs[-1])

    return pl.pallas_call(
        kernel,
        out_shape=jax.ShapeDtypeStruct((owners * share, size), BF16),
        in_specs=[VMEM] * count + [pl.BlockSpec(memory_space=pl.ANY)] * len(after),
        out_specs=VMEM,
        compiler_params=pltpu.CompilerParams(vmem_limit_bytes=4 * MIB),
        cost_estimate=CHEAP,
        name="collect",
    )(*upstreams, *blocks, *after)


def adam_update(gradient, current, moment_one, moment_two):
    first = BETA_ONE * moment_one + (1.0 - BETA_ONE) * gradient
    second = BETA_TWO * moment_two + (1.0 - BETA_TWO) * gradient * gradient
    scaled = second * (1.0 / CORRECT_TWO)
    root = scaled * lax.rsqrt(scaled)
    step = (first * (RATE / CORRECT_ONE)) / (root + EPS_ADAM)
    return first, second, (1.0 - RATE * DECAY) * current - step


def adam_kernel(sizes, *refs):
    owners, parts, share, tile = sizes
    up_refs = refs[:parts]
    hidden_ref, down_ref, one_ref, two_ref = refs[parts : parts + 4]
    outs = refs[parts + 4 : parts + 7]
    rows_ref, turned_ref, *results, sem = refs[parts + 7 :]
    rows = turned_ref.shape[0]
    me = lax.axis_index("dp")
    part = lax.axis_index("tensor")
    for p in range(parts):
        for k in range(owners):
            at = k * parts + lax.rem(part + p, parts)
            rows_ref[pl.ds(pl.multiple_of(at * share, share), share), :] = up_refs[p][
                k * share : (k + 1) * share, :
            ]
    turned_ref[...] = rows_ref[...].T
    writes = []
    for i in range(rows // tile):
        cut = slice(i * tile, (i + 1) * tile)
        gradient = jnp.dot(turned_ref[cut, :], hidden_ref[...], preferred_element_type=F32)
        current = down_ref[pl.ds(pl.multiple_of(me * rows + i * tile, tile), tile), :].astype(F32)
        updates = adam_update(gradient, current, one_ref[cut, :], two_ref[cut, :])
        for q, update in enumerate(updates):
            results[q][cut, :] = update
            writes.append(pltpu.make_async_copy(results[q].at[cut], outs[q].at[cut], sem.at[i, q]))
            writes[-1].start()
    for write in writes:
        write.wait()


def adam_step(blocks, hidden_all, w_down, moment_one, moment_two, owners, parts):
    rows, units = moment_one.shape
    tokens = hidden_all.shape[0]
    tile = tile_of(rows, 128)
    return pl.pallas_call(
        functools.partial(adam_kernel, (owners, parts, blocks[0].shape[0] // owners, tile)),
        out_shape=[jax.ShapeDtypeStruct((rows, units), F32)] * 3,
        in_specs=[VMEM] * (len(blocks) + 4),
        out_specs=[pl.BlockSpec(memory_space=pl.ANY)] * 3,
        scratch_shapes=[pltpu.VMEM((tokens, rows), BF16), pltpu.VMEM((rows, tokens), BF16)]
        + [pltpu.VMEM((rows, units), F32)] * 3
        + [pltpu.SemaphoreType.DMA((rows // tile, 3))],
        compiler_params=pltpu.CompilerParams(vmem_limit_bytes=18 * MIB),
        cost_estimate=CHEAP,
        name="adam_step",
    )(*blocks, hidden_all, w_down, moment_one, moment_two)


def columns(array, count):
    rows, cols = array.shape
    size = cols // count

    def kernel(source, *targets):
        for n, target in enumerate(targets):
            target[...] = source[:, n * size : (n + 1) * size]

    return pl.pallas_call(
        kernel,
        out_shape=[jax.ShapeDtypeStruct((rows, size), array.dtype)] * count,
        in_specs=[VMEM],
        out_specs=[VMEM] * count,
        compiler_params=pltpu.CompilerParams(vmem_limit_bytes=4 * MIB),
        cost_estimate=CHEAP,
        name="columns",
    )(array)


def stack(order, size):
    count = len(order)
    cols = order[0][0].shape[1]

    def kernel(*refs):
        out, sem = refs[-2:]
        started = [
            pltpu.make_async_copy(
                refs[n].at[at : at + size], out.at[n * size : (n + 1) * size], sem.at[n]
            )
            for n, (_, at) in enumerate(order)
        ]
        for copy in started:
            copy.start()
        for copy in started:
            copy.wait()

    return pl.pallas_call(
        kernel,
        out_shape=pltpu.VMEM((count * size, cols), BF16),
        in_specs=[pl.BlockSpec(memory_space=pl.ANY)] * count,
        out_specs=VMEM,
        scratch_shapes=[pltpu.SemaphoreType.DMA((count,))],
        compiler_params=pltpu.CompilerParams(vmem_limit_bytes=4 * MIB),
        cost_estimate=CHEAP,
        name="stack",
    )(*[array for array, _ in order])


def adam_general(upstreams, hidden_all, w_down, moment_one, moment_two):
    owners = lax.axis_size("dp")
    sections = len(upstreams)
    segment = lax.axis_index("pipe")
    own = upstreams[0]
    for s in range(1, sections):
        own = jnp.where(segment == sections - 1 - s, upstreams[s], own)
    mine = lax.all_to_all(own, "dp", split_axis=1, concat_axis=0, tiled=True)
    share, rows = own.shape[0], mine.shape[1]
    turned = lax.all_gather(mine.reshape(owners, share, rows), "tensor", axis=1, tiled=True)
    gradient = lax.dot_general(
        turned.reshape(-1, rows), hidden_all, (((0,), (0,)), ((), ())), preferred_element_type=F32
    )
    at = lax.axis_index("dp") * rows
    current = lax.dynamic_slice_in_dim(w_down, at, rows, 0).astype(F32)
    return adam_update(gradient, current, moment_one, moment_two)


def from_peers(value, axis):
    size = lax.axis_size(axis)
    return [lax.ppermute(value, axis, [((i + k) % size, i) for i in range(size)]) for k in range(1, size)]


def to_peers(values, axis):
    size = lax.axis_size(axis)
    return [
        lax.ppermute(value, axis, [(i, (i + k) % size) for i in range(size)])
        for k, value in enumerate(values, 1)
    ]


def on_device(
    up_weight,
    down_weight,
    gate_act,
    hidden,
    block_input,
    norm_gain,
    loss_grad,
    moment_one,
    moment_two,
):
    sections = lax.axis_size("pipe")
    owners = lax.axis_size("dp")
    parts = lax.axis_size("tensor")
    planned = sections == 4 and owners == 4 and block_input.shape[2] % (128 * owners) == 0
    share = loss_grad.shape[0]
    saved = hidden[0]
    w_down, gates, rows_in, loss, *halves = stage(
        [down_weight[0], gate_act[0], block_input[0], loss_grad], [saved] if planned else []
    )
    turned = None
    upstreams = [loss]
    grads = []
    blocks = []
    late = ()
    for layer in reversed(range(sections)):
        upstream = upstreams[-1]
        if planned and not layer:
            arrivals = [from_peers(piece, "tensor") for piece in columns(upstream, owners)]
            peers = [piece for peer in zip(*arrivals) for piece in peer]
        else:
            peers = from_peers(upstream if grads else loss_grad, "tensor")
        if not grads:
            turned, kept, *sent = section_step(layer, upstream, peers, w_down, None, gates, up_weight[0])
        else:
            kept, *sent = section_step(layer, upstream, peers, w_down, turned, gates, after=late)
        arrived = to_peers(sent, "tensor")
        window = len(grads)
        moving = ()
        if planned and window == 0:
            moving = [halves[:1], halves[1:]]
        elif planned and window == 1:
            moving = [(halves[1], side_lower), (halves[0], along_upper)]
        grad, cuts, handed = norm_step(
            layer,
            kept,
            arrived,
            upstream,
            rows_in,
            norm_gain,
            loss,
            earlier=grads if window >= sections - 2 else (),
            owners=owners if planned and layer == 1 else 1,
            passed=moving,
        )
        grads.append(grad)
        if layer:
            upstreams.append(lax.ppermute(grad, "pipe", [(layer, layer - 1)]))
        if planned and layer:
            for k, cut in enumerate(cuts, 1):
                pairs = [
                    (s * owners + i, (s - 1) % sections * owners + (i ^ k))
                    for s in range(sections)
                    for i in range(owners)
                ]
                blocks.append(lax.ppermute(cut, ("pipe", "dp"), pairs))
            if window < 2:
                exchange = [
                    lax.ppermute(piece, "dp", [(i, i ^ k) for i in range(owners)])
                    for k, piece in enumerate(handed, 1)
                ]
            if window == 0:
                along_upper, side_lower = exchange
                moments = stage_in_section(
                    [moment_one[0], moment_two[0]], lambda section: section != sections - 2, (), [grad]
                )
                late = [*exchange, *moments]
            elif window == 1:
                along_rest, side_rest = late = exchange
            else:
                late = moments = stage_in_section(
                    [moment_one[0], moment_two[0]], lambda section: section == sections - 2, moments, [grad]
                )
    if planned:
        half = saved.shape[0] // 2
        order = [
            (halves[0], 0),
            (halves[1], 0),
            (along_upper, 0),
            (along_rest, 0),
            (side_rest, 0),
            (side_lower, 0),
            (side_rest, half),
            (along_rest, half),
        ]
        hidden_all = stack(order, half)
        own = collect(upstreams, blocks, [kept, hidden_all])
        first, second, updated = adam_step(
            [own, *from_peers(own, "tensor")], hidden_all, w_down, *moments, owners, parts
        )
    else:
        hidden_all = lax.all_gather(saved, "dp", axis=0, tiled=True)
        first, second, updated = adam_general(
            upstreams, hidden_all, w_down, moment_one[0], moment_two[0]
        )
    return (grads[-1][None], first[None], second[None], updated[None])


def solution(mesh):
    in_specs = (
        P("pipe", None, "tensor"),
        P("pipe", None, "tensor"),
        P("pipe", "dp", "tensor"),
        P("pipe", "dp", "tensor"),
        P("pipe", ("dp", "tensor"), None),
        P("pipe", None),
        P(("dp", "tensor"), None),
        P("pipe", "dp", "tensor"),
        P("pipe", "dp", "tensor"),
    )
    out_specs = (
        P("pipe", ("dp", "tensor"), None),
        P("pipe", "dp", "tensor"),
        P("pipe", "dp", "tensor"),
        P("pipe", "dp", "tensor"),
    )
    return jax.shard_map(
        on_device, mesh=mesh, in_specs=in_specs, out_specs=out_specs, check_vma=False
    )
```

```python
import functools
import math
import jax
import jax.numpy as jnp
from jax import lax
from jax.experimental import pallas as pl
from jax.experimental.pallas import tpu as pltpu
from jax.sharding import PartitionSpec as P

EPS_NORM = 1e-05
EPS_ADAM = 1e-08
BETA_ONE = 0.9
BETA_TWO = 0.95
RATE = 0.01
DECAY = 0.1
CORRECT_ONE = 1.0 - 0.9**10
CORRECT_TWO = 1.0 - 0.95**10

MIB = 2**20
VMEM = pl.BlockSpec(memory_space=pltpu.VMEM)
CHEAP = pl.CostEstimate(flops=0, bytes_accessed=0, transcendentals=0)
F32 = jnp.float32
BF16 = jnp.bfloat16


def tile_of(extent, most):
    tile = min(extent, most)
    while extent % tile:
        tile //= 2
    return tile


def copies(pairs, sem, chunks):
    started = []
    for n, (source, target) in enumerate(pairs):
        rows = source.shape[0] // chunks
        cut = [slice(c * rows, (c + 1) * rows) for c in range(chunks)]
        started.append(
            [pltpu.make_async_copy(source.at[r], target.at[r], sem.at[n, c]) for c, r in enumerate(cut)]
        )
    for array in started:
        for copy in array:
            copy.start()
    return started


def stage(arrays, split=(), after=()):
    pieces = [(n, slice(None)) for n in range(len(arrays))]
    for n, array in enumerate(split, len(arrays)):
        half = array.shape[0] // 2
        pieces += [(n, slice(0, half)), (n, slice(half, 2 * half))]
    arrays = [*arrays, *split]
    shapes = [(arrays[n][rows].shape if rows.start is not None else arrays[n].shape) for n, rows in pieces]
    count = len(arrays)

    def kernel(*refs):
        sources, targets, sem = refs[:count], refs[count + len(after) : -1], refs[-1]
        pairs = [(sources[n].at[rows], target) for (n, rows), target in zip(pieces, targets)]
        for array in copies(pairs, sem, 2):
            for copy in array:
                copy.wait()

    return pl.pallas_call(
        kernel,
        out_shape=[pltpu.VMEM(shape, arrays[n].dtype) for (n, _), shape in zip(pieces, shapes)],
        in_specs=[pl.BlockSpec(memory_space=pltpu.HBM)] * count
        + [pl.BlockSpec(memory_space=pl.ANY)] * len(after),
        out_specs=[VMEM] * len(pieces),
        scratch_shapes=[pltpu.SemaphoreType.DMA((len(pieces), 2))],
        compiler_params=pltpu.CompilerParams(vmem_limit_bytes=4 * MIB),
        cost_estimate=pl.CostEstimate(
            flops=0, bytes_accessed=sum(2 * a.size * a.dtype.itemsize for a in arrays), transcendentals=0
        ),
        name="stage",
    )(*[pltpu.with_memory_space_constraint(a, pltpu.HBM) for a in arrays], *after)


def stage_in_section(arrays, wanted, held, after):
    count = len(arrays)

    def kernel(*refs):
        sources, targets, sem = refs[:count], refs[count + len(held) + len(after) : -1], refs[-1]

        @pl.when(wanted(lax.axis_index("pipe")))
        def _():
            for array in copies(list(zip(sources, targets)), sem, 2):
                for copy in array:
                    copy.wait()

    return pl.pallas_call(
        kernel,
        out_shape=[pltpu.VMEM(a.shape, a.dtype) for a in arrays],
        in_specs=[pl.BlockSpec(memory_space=pltpu.HBM)] * count
        + [VMEM] * len(held)
        + [pl.BlockSpec(memory_space=pl.ANY)] * len(after),
        out_specs=[VMEM] * count,
        input_output_aliases={count + n: n for n in range(len(held))},
        scratch_shapes=[pltpu.SemaphoreType.DMA((count, 2))],
        compiler_params=pltpu.CompilerParams(vmem_limit_bytes=4 * MIB),
        cost_estimate=CHEAP,
        name="stage_in_section",
    )(*[pltpu.with_memory_space_constraint(a, pltpu.HBM) for a in arrays], *held, *after)


def unit_grads(parts, share, rows_ref, down_ref, gate_ref, unit_ref):
    me = lax.axis_index("tensor")
    term = jnp.dot(rows_ref[...], down_ref[...], preferred_element_type=F32)
    for k in range(parts):
        at = pl.multiple_of(lax.rem(me + k, parts) * share, share)
        gates = gate_ref[pl.ds(at, share), :].astype(F32)
        unit_ref[k * share : (k + 1) * share, :] = (term[k * share : (k + 1) * share] * gates).astype(BF16)


def hand_out(share, term, cols, kept_ref, sent_refs):
    kept_ref[:, cols] = term[0:share]
    for k, ref in enumerate(sent_refs, 1):
        ref[:, cols] = term[k * share : (k + 1) * share].astype(BF16)


def fill_rows(share, rows_ref, own_ref, peer_refs):
    rows_ref[0:share, :] = own_ref[...]
    parts = rows_ref.shape[0] // share
    me = lax.axis_index("tensor")
    for k in range(1, parts):
        if peer_refs[0].shape[0] > share:
            at = pl.multiple_of(lax.rem(me + k, parts) * share, share)
            rows_ref[k * share : (k + 1) * share, :] = peer_refs[0][pl.ds(at, share), :]
        else:
            rows_ref[k * share : (k + 1) * share, :] = peer_refs[k - 1][...]


def step_kernel(layer, parts, pieces, own_ref, *refs):
    peer_refs, refs = refs[:pieces], refs[pieces:]
    down_ref, turned_ref, gate_ref, kept_ref = refs[:4]
    sent_refs = refs[4 : parts + 3]
    rows_ref, unit_ref = refs[parts + 3 :]
    share = own_ref.shape[0]

    @pl.when(lax.axis_index("pipe") == layer)
    def _():
        fill_rows(share, rows_ref, own_ref, peer_refs)
        unit_grads(parts, share, rows_ref, down_ref, gate_ref, unit_ref)
        term = jnp.dot(unit_ref[...], turned_ref[...], preferred_element_type=F32)
        hand_out(share, term, slice(None), kept_ref, sent_refs)


def unit_kernel(layer, parts, own_ref, *refs):
    peer_refs = refs[: parts - 1]
    down_ref, gate_ref, unit_ref, rows_ref = refs[parts - 1 :]
    share = own_ref.shape[0]

    @pl.when(lax.axis_index("pipe") == layer)
    def _():
        fill_rows(share, rows_ref, own_ref, peer_refs)
        unit_grads(parts, share, rows_ref, down_ref, gate_ref, unit_ref)


def unit_step(layer, own, peers, w_down, gates):
    parts = len(peers) + 1
    rows = own.shape[0] * parts
    return pl.pallas_call(
        functools.partial(unit_kernel, layer, parts),
        out_shape=jax.ShapeDtypeStruct((rows, w_down.shape[1]), BF16),
        in_specs=[VMEM] * (parts + 2),
        out_specs=VMEM,
        scratch_shapes=[pltpu.VMEM((rows, own.shape[1]), BF16)],
        compiler_params=pltpu.CompilerParams(vmem_limit_bytes=12 * MIB),
        cost_estimate=CHEAP,
        name="unit_step",
    )(own, *peers, w_down, gates)


def width_step(layer, unit_grad, turned, share, after):
    width = turned.shape[1]
    parts = unit_grad.shape[0] // share

    def kernel(unit_ref, turned_ref, *refs):
        kept_ref, *sent_refs = refs[len(after) :]

        @pl.when(lax.axis_index("pipe") == layer)
        def _():
            term = jnp.dot(unit_ref[...], turned_ref[...], preferred_element_type=F32)
            hand_out(share, term, slice(None), kept_ref, sent_refs)

    return pl.pallas_call(
        kernel,
        out_shape=[jax.ShapeDtypeStruct((share, width), F32)]
        + [jax.ShapeDtypeStruct((share, width), BF16)] * (parts - 1),
        in_specs=[VMEM, VMEM] + [pl.BlockSpec(memory_space=pl.ANY)] * len(after),
        out_specs=[VMEM] * parts,
        compiler_params=pltpu.CompilerParams(vmem_limit_bytes=12 * MIB),
        cost_estimate=CHEAP,
        name="width_step",
    )(unit_grad, turned, *after)


def first_kernel(layer, parts, pieces, own_ref, *refs):
    peer_refs, refs = refs[:pieces], refs[pieces:]
    down_ref, up_ref, gate_ref, turned_ref, kept_ref = refs[:5]
    sent_refs = refs[5 : parts + 4]
    rows_ref, unit_ref, held_ref, sem = refs[parts + 4 :]
    share = own_ref.shape[0]
    chunks = sem.shape[1]
    size = held_ref.shape[0] // chunks
    (arriving,) = copies([(up_ref, held_ref)], sem, chunks)
    starts = lax.axis_index("pipe") == layer

    @pl.when(starts)
    def _():
        fill_rows(share, rows_ref, own_ref, peer_refs)
        unit_grads(parts, share, rows_ref, down_ref, gate_ref, unit_ref)

    for c in range(chunks):
        cols = slice(c * size, (c + 1) * size)
        arriving[c].wait()

        @pl.when(starts)
        def _(cols=cols):
            term = lax.dot_general(
                unit_ref[...], held_ref[cols, :], (((1,), (1,)), ((), ())), preferred_element_type=F32
            )
            hand_out(share, term, cols, kept_ref, sent_refs)

        @pl.when(jnp.logical_not(starts))
        def _(cols=cols):
            turned_ref[:, cols] = held_ref[cols, :].T


def section_step(layer, own, peers, w_down, turned, gates, w_up=None, after=()):
    share, width = own.shape
    units = w_down.shape[1]
    pieces = len(peers)
    parts = lax.axis_size("tensor")
    rows = share * parts
    first = w_up is not None
    out_shape = [jax.ShapeDtypeStruct((share, width), F32)]
    out_shape += [jax.ShapeDtypeStruct((share, width), BF16)] * (parts - 1)
    scratch = [pltpu.VMEM((rows, width), BF16), pltpu.VMEM((rows, units), BF16)]
    in_specs = [VMEM] * (pieces + 4) + [pl.BlockSpec(memory_space=pl.ANY)] * len(after)
    body = functools.partial(first_kernel if first else step_kernel, layer, parts, pieces)

    def kernel(*refs):
        body(*refs[: pieces + 4], *refs[pieces + 4 + len(after) :])

    if first:
        out_shape = [pltpu.VMEM((units, width), BF16)] + out_shape
        scratch += [pltpu.VMEM((width, units), BF16), pltpu.SemaphoreType.DMA((1, 4))]
        in_specs[pieces + 2] = pl.BlockSpec(memory_space=pltpu.HBM)
        operand = pltpu.with_memory_space_constraint(w_up, pltpu.HBM)
    else:
        operand = turned
    outs = pl.pallas_call(
        kernel,
        out_shape=out_shape,
        in_specs=in_specs,
        out_specs=[VMEM] * len(out_shape),
        scratch_shapes=scratch,
        compiler_params=pltpu.CompilerParams(vmem_limit_bytes=(20 if first else 12) * MIB),
        cost_estimate=CHEAP,
        name="section_step",
    )(own, *peers, w_down, operand, gates, *after)
    return outs


def pack_block(source, k, target, at):
    owners = lax.axis_size("dp")
    tokens, width = source.shape
    size = width // owners
    rows = tokens * size // target.shape[1]
    column = pl.multiple_of((lax.axis_index("dp") ^ k) * size, size)
    for q in range(tokens // rows):
        target[at : at + rows, q * size : (q + 1) * size] = source[
            q * rows : (q + 1) * rows, pl.ds(column, size)
        ]
    return rows


def norm_kernel(layer, parts, earlier, owners, passed, handed, kept_ref, *refs):
    arrived = refs[: parts - 1]
    up_ref, in_ref, gain_ref = refs[parts - 1 : parts + 2]
    refs = refs[parts + 2 :]
    earlier_refs, refs = refs[:earlier], refs[earlier:]
    first_ref, pass_refs, refs = refs[0], refs[1 : 1 + passed], refs[1 + passed :]
    out_ref, block_refs, handed_refs = refs[0], refs[1 : len(refs) - len(handed)], refs[len(refs) - len(handed) :]
    segment = lax.axis_index("pipe")

    def cut(source):
        size = source.shape[1] // owners
        for k, ref in enumerate(block_refs, 1):
            at = pl.multiple_of((lax.axis_index("dp") ^ k) * size, size)
            ref[...] = source[:, pl.ds(at, size)]

    @pl.when(segment == layer)
    def _():
        normed = kept_ref[...]
        for ref in arrived:
            normed = normed + ref[...].astype(F32)
        rows_in = in_ref[...].astype(F32)
        inverse_rms = lax.rsqrt(jnp.mean(rows_in * rows_in, axis=-1, keepdims=True) + EPS_NORM)
        scaled = normed * gain_ref[...]
        mean_term = jnp.mean(rows_in * scaled, axis=-1, keepdims=True)
        out_ref[...] = (
            up_ref[...].astype(F32)
            + inverse_rms * scaled
            - rows_in * (inverse_rms * inverse_rms * inverse_rms * mean_term)
        ).astype(BF16)
        cut(out_ref)

    for above, ref in enumerate(earlier_refs):

        @pl.when(segment == layer + earlier - above)
        def _(ref=ref):
            cut(ref)
            if layer == 0:
                out_ref[...] = ref[...]

    sources = iter(pass_refs)
    for recipe, target in zip(handed, handed_refs):
        at = 0
        for piece in recipe:
            if isinstance(piece, int):
                at += pack_block(first_ref, piece, target, at)
            else:
                start, rows = piece
                target[at : at + rows, :] = next(sources)[start : start + rows, :]
                at += rows


def norm_step(layer, kept, arrived, upstream, rows_in, gain, first, earlier=(), owners=1, passed=()):
    parts = len(arrived) + 1
    share, width = upstream.shape
    block = jax.ShapeDtypeStruct((share, width // owners), BF16)
    recipes = [[p if isinstance(p, int) else p[1:] for p in group] for group in passed]
    handed = []
    for group in passed:
        units = passed[0][0][0].shape[1]
        block_rows = share * (width // lax.axis_size("dp")) // units
        rows = sum(block_rows if isinstance(p, int) else p[2] for p in group)
        handed.append(jax.ShapeDtypeStruct((rows, units), BF16))
    passed = [p[0] for group in passed for p in group if not isinstance(p, int)]
    outs = pl.pallas_call(
        functools.partial(norm_kernel, layer, parts, len(earlier), owners, len(passed), recipes),
        out_shape=[jax.ShapeDtypeStruct(upstream.shape, BF16)]
        + [block] * (owners - 1)
        + handed,
        in_specs=[VMEM] * (parts + 4 + len(earlier) + len(passed)),
        out_specs=[VMEM] * (owners + len(handed)),
        compiler_params=pltpu.CompilerParams(vmem_limit_bytes=8 * MIB),
        cost_estimate=CHEAP,
        name="norm_step",
    )(kept, *arrived, upstream, rows_in, gain, *earlier, first, *passed)
    return outs[0], outs[1:owners], outs[owners:]


def collect(upstreams, blocks, packed, after):
    sections = len(upstreams)
    owners = len(blocks) + 1
    share, size = blocks[0].shape
    count = sections + 2 * len(blocks)

    def kernel(*refs):
        out_ref = refs[-1]
        segment = lax.axis_index("pipe")
        at = pl.multiple_of(lax.axis_index("dp") * size, size)
        for s in range(sections):

            @pl.when(segment == sections - 1 - s)
            def _(s=s):
                out_ref[0:share, :] = refs[s][:, pl.ds(at, size)]

        @pl.when(segment < sections - 1)
        def _():
            for k in range(1, owners):
                out_ref[k * share : (k + 1) * share, :] = refs[sections + k - 1][...]

        @pl.when(segment == sections - 1)
        def _():
            for k in range(1, owners):
                source, start = refs[sections + owners + k - 2], packed[k - 1][1]
                pieces = source.shape[1] // size
                rows = share // pieces
                for q in range(pieces):
                    out_ref[k * share + q * rows : k * share + (q + 1) * rows, :] = source[
                        start : start + rows, q * size : (q + 1) * size
                    ]

    return pl.pallas_call(
        kernel,
        out_shape=jax.ShapeDtypeStruct((owners * share, size), BF16),
        in_specs=[VMEM] * count + [pl.BlockSpec(memory_space=pl.ANY)] * len(after),
        out_specs=VMEM,
        compiler_params=pltpu.CompilerParams(vmem_limit_bytes=4 * MIB),
        cost_estimate=CHEAP,
        name="collect",
    )(*upstreams, *blocks, *[array for array, _ in packed], *after)


def adam_update(gradient, current, moment_one, moment_two):
    first = BETA_ONE * moment_one + (1.0 - BETA_ONE) * gradient
    second = BETA_TWO * moment_two + (1.0 - BETA_TWO) * gradient * gradient
    root = second * lax.rsqrt(second)
    scale = math.sqrt(CORRECT_TWO)
    step = (first * (RATE * scale / CORRECT_ONE)) / (root + EPS_ADAM * scale)
    return first, second, (1.0 - RATE * DECAY) * current - step


def adam_kernel(sizes, *refs):
    owners, parts, share, tile, part_rows = sizes
    up_refs = refs[:parts]
    hidden_ref, down_ref, one_ref, two_ref = refs[parts : parts + 4]
    outs = refs[parts + 4 : parts + 7]
    rows_ref, *results, sem = refs[parts + 7 :]
    rows = rows_ref.shape[1]
    me = lax.axis_index("dp")
    part = lax.axis_index("tensor")
    for p in range(parts):
        for k in range(owners):
            at = k * parts + lax.rem(part + p, parts)
            rows_ref[pl.ds(pl.multiple_of(at * share, share), share), :] = up_refs[p][
                k * share : (k + 1) * share, :
            ]
    writes = []
    for i in range(rows // tile):
        turned = rows_ref[:, i * tile : (i + 1) * tile].T
        gradient = jnp.dot(turned, hidden_ref[...], preferred_element_type=F32)
        for j in range(tile // part_rows):
            at = i * tile + j * part_rows
            cut = slice(at, at + part_rows)
            current = down_ref[pl.ds(pl.multiple_of(me * rows + at, part_rows), part_rows), :].astype(F32)
            updates = adam_update(
                gradient[j * part_rows : (j + 1) * part_rows], current, one_ref[cut, :], two_ref[cut, :]
            )
            for q, update in enumerate(updates):
                results[q][cut, :] = update
                writes.append(
                    pltpu.make_async_copy(results[q].at[cut], outs[q].at[cut], sem.at[at // part_rows, q])
                )
                writes[-1].start()
    for write in writes:
        write.wait()


def adam_step(blocks, hidden_all, w_down, moment_one, moment_two, owners, parts):
    rows, units = moment_one.shape
    tokens = hidden_all.shape[0]
    tile = tile_of(rows, 128)
    part_rows = tile_of(tile, 32)
    return pl.pallas_call(
        functools.partial(adam_kernel, (owners, parts, blocks[0].shape[0] // owners, tile, part_rows)),
        out_shape=[jax.ShapeDtypeStruct((rows, units), F32)] * 3,
        in_specs=[VMEM] * (len(blocks) + 4),
        out_specs=[pl.BlockSpec(memory_space=pl.ANY)] * 3,
        scratch_shapes=[pltpu.VMEM((tokens, rows), BF16)]
        + [pltpu.VMEM((rows, units), F32)] * 3
        + [pltpu.SemaphoreType.DMA((rows // part_rows, 3))],
        compiler_params=pltpu.CompilerParams(vmem_limit_bytes=18 * MIB),
        cost_estimate=CHEAP,
        name="adam_step",
    )(*blocks, hidden_all, w_down, moment_one, moment_two)


def stack(order):
    count = len(order)
    total = sum(rows for _, _, rows in order)

    def kernel(*refs):
        out, sem = refs[-2:]
        started = []
        place = 0
        for n, (_, at, rows) in enumerate(order):
            started.append(
                pltpu.make_async_copy(
                    refs[n].at[at : at + rows], out.at[place : place + rows], sem.at[n]
                )
            )
            place += rows
        for copy in started:
            copy.start()
        for copy in started:
            copy.wait()

    return pl.pallas_call(
        kernel,
        out_shape=pltpu.VMEM((total, order[0][0].shape[1]), BF16),
        in_specs=[pl.BlockSpec(memory_space=pl.ANY)] * count,
        out_specs=VMEM,
        scratch_shapes=[pltpu.SemaphoreType.DMA((count,))],
        compiler_params=pltpu.CompilerParams(vmem_limit_bytes=4 * MIB),
        cost_estimate=CHEAP,
        name="stack",
    )(*[array for array, _, _ in order])


def adam_general(upstreams, hidden_all, w_down, moment_one, moment_two):
    owners = lax.axis_size("dp")
    sections = len(upstreams)
    segment = lax.axis_index("pipe")
    own = upstreams[0]
    for s in range(1, sections):
        own = jnp.where(segment == sections - 1 - s, upstreams[s], own)
    mine = lax.all_to_all(own, "dp", split_axis=1, concat_axis=0, tiled=True)
    share, rows = own.shape[0], mine.shape[1]
    turned = lax.all_gather(mine.reshape(owners, share, rows), "tensor", axis=1, tiled=True)
    gradient = lax.dot_general(
        turned.reshape(-1, rows), hidden_all, (((0,), (0,)), ((), ())), preferred_element_type=F32
    )
    at = lax.axis_index("dp") * rows
    current = lax.dynamic_slice_in_dim(w_down, at, rows, 0).astype(F32)
    return adam_update(gradient, current, moment_one, moment_two)


def from_peers(value, axis):
    size = lax.axis_size(axis)
    return [lax.ppermute(value, axis, [((i + k) % size, i) for i in range(size)]) for k in range(1, size)]


def to_peers(values, axis):
    size = lax.axis_size(axis)
    return [
        lax.ppermute(value, axis, [(i, (i + k) % size) for i in range(size)])
        for k, value in enumerate(values, 1)
    ]


def on_device(
    up_weight,
    down_weight,
    gate_act,
    hidden,
    block_input,
    norm_gain,
    loss_grad,
    moment_one,
    moment_two,
):
    sections = lax.axis_size("pipe")
    owners = lax.axis_size("dp")
    parts = lax.axis_size("tensor")
    width, units = down_weight.shape[1:]
    planned = sections == 4 and owners == 4 and width % (128 * owners) == 0 and units % (width // owners) == 0
    planned = planned and loss_grad.shape[0] * (width // owners) % (16 * units) == 0 and parts == 2
    share = loss_grad.shape[0]
    saved = hidden[0]
    half = saved.shape[0] // 2
    w_down, gates, rows_in, loss, *halves = stage(
        [down_weight[0], gate_act[0], block_input[0], loss_grad], [saved] if planned else []
    )
    turned = None
    upstreams = [loss]
    grads = []
    late = ()
    for layer in reversed(range(sections)):
        upstream = upstreams[-1]
        if planned and not layer:
            peers = [lax.all_gather(upstream, "tensor", axis=0, tiled=True)]
        else:
            peers = from_peers(upstream if grads else loss_grad, "tensor")
        if not grads:
            turned, kept, *sent = section_step(layer, upstream, peers, w_down, None, gates, up_weight[0])
        elif planned and len(grads) == 2:
            unit_grad = unit_step(layer, upstream, peers, w_down, gates)
            kept, *sent = width_step(layer, unit_grad, turned, loss_grad.shape[0], late)
        else:
            kept, *sent = section_step(layer, upstream, peers, w_down, turned, gates, after=late)
        if planned and not layer:
            hidden_all = stack(
                [
                    (halves[0], 0, half),
                    (halves[1], 0, half),
                    (along_upper, 0, half),
                    (along_rest, 0, half),
                    (side_rest, 0, half),
                    (side_lower, 0, half),
                    (side_rest, half, half),
                    (along_rest, half, half),
                ]
            )
            packed = [(along_upper, half), (side_lower, half), (corner, 0)]
            own = collect(upstreams, blocks, packed, [kept, hidden_all])
        arrived = to_peers(sent, "tensor")
        window = len(grads)
        moving = ()
        if planned and window == 0:
            moving = [[(halves[0], 0, half), 1], [(halves[1], 0, half), 2]]
        elif planned and window == 1:
            moving = [
                [(halves[1], 0, half), (side_lower, 0, half)],
                [(halves[0], 0, half), (along_upper, 0, half)],
                [3],
            ]
        grad, cuts, handed = norm_step(
            layer,
            kept,
            arrived,
            upstream,
            rows_in,
            norm_gain,
            loss,
            earlier=grads if window >= sections - 2 else (),
            owners=owners if planned and window == 2 else 1,
            passed=moving,
        )
        grads.append(grad)
        if layer:
            upstreams.append(lax.ppermute(grad, "pipe", [(layer, layer - 1)]))
        if planned and layer:
            if window == 2:
                blocks = [
                    lax.ppermute(
                        cut,
                        ("pipe", "dp"),
                        [
                            (s * owners + i, (s - 1) * owners + (i ^ k))
                            for s in range(1, sections)
                            for i in range(owners)
                        ],
                    )
                    for k, cut in enumerate(cuts, 1)
                ]
            if window < 2:
                exchange = [
                    lax.ppermute(piece, "dp", [(i, i ^ k) for i in range(owners)])
                    for k, piece in enumerate(handed[:2], 1)
                ]
            if window == 0:
                along_upper, side_lower = exchange
                moments = stage_in_section(
                    [moment_one[0], moment_two[0]], lambda section: section != sections - 2, (), [grad]
                )
                late = [*exchange, *moments]
            elif window == 1:
                along_rest, side_rest = exchange
                start = (sections - 1) * owners
                corner = lax.ppermute(
                    handed[2], ("pipe", "dp"), [(start + i, start + (i ^ 3)) for i in range(owners)]
                )
                moments = stage_in_section(
                    [moment_one[0], moment_two[0]], lambda section: section == sections - 2, moments, [grad]
                )
                late = [*exchange, *moments]
            else:
                late = ()
    if planned:
        first, second, updated = adam_step(
            [own, *from_peers(own, "tensor")], hidden_all, w_down, *moments, owners, parts
        )
    else:
        hidden_all = lax.all_gather(saved, "dp", axis=0, tiled=True)
        first, second, updated = adam_general(
            upstreams, hidden_all, w_down, moment_one[0], moment_two[0]
        )
    return (grads[-1][None], first[None], second[None], updated[None])


def solution(mesh):
    in_specs = (
        P("pipe", None, "tensor"),
        P("pipe", None, "tensor"),
        P("pipe", "dp", "tensor"),
        P("pipe", "dp", "tensor"),
        P("pipe", ("dp", "tensor"), None),
        P("pipe", None),
        P(("dp", "tensor"), None),
        P("pipe", "dp", "tensor"),
        P("pipe", "dp", "tensor"),
    )
    out_specs = (
        P("pipe", ("dp", "tensor"), None),
        P("pipe", "dp", "tensor"),
        P("pipe", "dp", "tensor"),
        P("pipe", "dp", "tensor"),
    )
    return jax.shard_map(
        on_device, mesh=mesh, in_specs=in_specs, out_specs=out_specs, check_vma=False
    )
```

```python
import functools
import math
import jax
import jax.numpy as jnp
from jax import lax
from jax.experimental import pallas as pl
from jax.experimental.pallas import tpu as pltpu
from jax.sharding import PartitionSpec as P

EPS_NORM = 1e-05
EPS_ADAM = 1e-08
BETA_ONE = 0.9
BETA_TWO = 0.95
RATE = 0.01
DECAY = 0.1
CORRECT_ONE = 1.0 - 0.9**10
CORRECT_TWO = 1.0 - 0.95**10

MIB = 2**20
VMEM = pl.BlockSpec(memory_space=pltpu.VMEM)
CHEAP = pl.CostEstimate(flops=0, bytes_accessed=0, transcendentals=0)
F32 = jnp.float32
BF16 = jnp.bfloat16


def tile_of(extent, most):
    tile = min(extent, most)
    while extent % tile:
        tile //= 2
    return tile


def copies(pairs, sem, chunks):
    started = []
    for n, (source, target) in enumerate(pairs):
        rows = source.shape[0] // chunks
        cut = [slice(c * rows, (c + 1) * rows) for c in range(chunks)]
        started.append(
            [pltpu.make_async_copy(source.at[r], target.at[r], sem.at[n, c]) for c, r in enumerate(cut)]
        )
    for array in started:
        for copy in array:
            copy.start()
    return started


def stage(arrays):
    count = len(arrays)

    def kernel(*refs):
        for array in copies(list(zip(refs[:count], refs[count:-1])), refs[-1], 2):
            for copy in array:
                copy.wait()

    return pl.pallas_call(
        kernel,
        out_shape=[pltpu.VMEM(a.shape, a.dtype) for a in arrays],
        in_specs=[pl.BlockSpec(memory_space=pltpu.HBM)] * count,
        out_specs=[VMEM] * count,
        scratch_shapes=[pltpu.SemaphoreType.DMA((count, 2))],
        compiler_params=pltpu.CompilerParams(vmem_limit_bytes=4 * MIB),
        cost_estimate=pl.CostEstimate(
            flops=0, bytes_accessed=sum(2 * a.size * a.dtype.itemsize for a in arrays), transcendentals=0
        ),
        name="stage",
    )(*[pltpu.with_memory_space_constraint(a, pltpu.HBM) for a in arrays])


def stage_in_section(arrays, wanted, held, after):
    count = len(arrays)

    def kernel(*refs):
        sources, targets, sem = refs[:count], refs[count + len(held) + len(after) : -1], refs[-1]

        @pl.when(wanted(lax.axis_index("pipe")))
        def _():
            for array in copies(list(zip(sources, targets)), sem, 2):
                for copy in array:
                    copy.wait()

    return pl.pallas_call(
        kernel,
        out_shape=[pltpu.VMEM(a.shape, a.dtype) for a in arrays],
        in_specs=[pl.BlockSpec(memory_space=pltpu.HBM)] * count
        + [VMEM] * len(held)
        + [pl.BlockSpec(memory_space=pl.ANY)] * len(after),
        out_specs=[VMEM] * count,
        input_output_aliases={count + n: n for n in range(len(held))},
        scratch_shapes=[pltpu.SemaphoreType.DMA((count, 2))],
        compiler_params=pltpu.CompilerParams(vmem_limit_bytes=4 * MIB),
        cost_estimate=CHEAP,
        name="stage_in_section",
    )(*[pltpu.with_memory_space_constraint(a, pltpu.HBM) for a in arrays], *held, *after)


def unit_grads(parts, share, rows_ref, down_ref, gate_ref, unit_ref):
    me = lax.axis_index("tensor")
    term = jnp.dot(rows_ref[...], down_ref[...], preferred_element_type=F32)
    for k in range(parts):
        at = pl.multiple_of(lax.rem(me + k, parts) * share, share)
        gates = gate_ref[pl.ds(at, share), :].astype(F32)
        unit_ref[k * share : (k + 1) * share, :] = (term[k * share : (k + 1) * share] * gates).astype(BF16)


def hand_out(share, term, cols, kept_ref, sent_refs):
    kept_ref[:, cols] = term[0:share]
    for k, ref in enumerate(sent_refs, 1):
        ref[:, cols] = term[k * share : (k + 1) * share].astype(BF16)


def fill_rows(share, rows_ref, own_ref, peer_refs):
    rows_ref[0:share, :] = own_ref[...]
    parts = rows_ref.shape[0] // share
    me = lax.axis_index("tensor")
    for k in range(1, parts):
        if peer_refs[0].shape[0] > share:
            at = pl.multiple_of(lax.rem(me + k, parts) * share, share)
            rows_ref[k * share : (k + 1) * share, :] = peer_refs[0][pl.ds(at, share), :]
        else:
            rows_ref[k * share : (k + 1) * share, :] = peer_refs[k - 1][...]


def step_kernel(layer, parts, pieces, own_ref, *refs):
    peer_refs, refs = refs[:pieces], refs[pieces:]
    down_ref, turned_ref, gate_ref, kept_ref = refs[:4]
    sent_refs = refs[4 : parts + 3]
    rows_ref, unit_ref = refs[parts + 3 :]
    share = own_ref.shape[0]

    @pl.when(lax.axis_index("pipe") == layer)
    def _():
        fill_rows(share, rows_ref, own_ref, peer_refs)
        unit_grads(parts, share, rows_ref, down_ref, gate_ref, unit_ref)
        term = jnp.dot(unit_ref[...], turned_ref[...], preferred_element_type=F32)
        hand_out(share, term, slice(None), kept_ref, sent_refs)


def unit_kernel(layer, parts, own_ref, *refs):
    peer_refs = refs[: parts - 1]
    down_ref, gate_ref, unit_ref, rows_ref = refs[parts - 1 :]
    share = own_ref.shape[0]

    @pl.when(lax.axis_index("pipe") == layer)
    def _():
        fill_rows(share, rows_ref, own_ref, peer_refs)
        unit_grads(parts, share, rows_ref, down_ref, gate_ref, unit_ref)


def unit_step(layer, own, peers, w_down, gates):
    parts = len(peers) + 1
    rows = own.shape[0] * parts
    return pl.pallas_call(
        functools.partial(unit_kernel, layer, parts),
        out_shape=jax.ShapeDtypeStruct((rows, w_down.shape[1]), BF16),
        in_specs=[VMEM] * (parts + 2),
        out_specs=VMEM,
        scratch_shapes=[pltpu.VMEM((rows, own.shape[1]), BF16)],
        compiler_params=pltpu.CompilerParams(vmem_limit_bytes=12 * MIB),
        cost_estimate=CHEAP,
        name="unit_step",
    )(own, *peers, w_down, gates)


def width_step(layer, unit_grad, turned, share, after):
    width = turned.shape[1]
    parts = unit_grad.shape[0] // share

    def kernel(unit_ref, turned_ref, *refs):
        kept_ref, *sent_refs = refs[len(after) :]

        @pl.when(lax.axis_index("pipe") == layer)
        def _():
            term = jnp.dot(unit_ref[...], turned_ref[...], preferred_element_type=F32)
            hand_out(share, term, slice(None), kept_ref, sent_refs)

    return pl.pallas_call(
        kernel,
        out_shape=[jax.ShapeDtypeStruct((share, width), F32)]
        + [jax.ShapeDtypeStruct((share, width), BF16)] * (parts - 1),
        in_specs=[VMEM, VMEM] + [pl.BlockSpec(memory_space=pl.ANY)] * len(after),
        out_specs=[VMEM] * parts,
        compiler_params=pltpu.CompilerParams(vmem_limit_bytes=12 * MIB),
        cost_estimate=CHEAP,
        name="width_step",
    )(unit_grad, turned, *after)


def first_kernel(layer, parts, pieces, further, own_ref, *refs):
    peer_refs, refs = refs[:pieces], refs[pieces:]
    down_ref, up_ref, gate_ref = refs[:3]
    count = 1 + max((n for n, _ in further), default=-1)
    source_refs, refs = refs[3 : 3 + count], refs[3 + count :]
    turned_ref, kept_ref = refs[:2]
    sent_refs = refs[2 : parts + 1]
    staged_refs = refs[parts + 1 : parts + 1 + len(further)]
    rows_ref, unit_ref, held_ref, sem, further_sem = refs[parts + 1 + len(further) :]
    share = own_ref.shape[0]
    chunks = sem.shape[1]
    size = held_ref.shape[0] // chunks
    (arriving,) = copies([(up_ref, held_ref)], sem, chunks)
    pairs = [(source_refs[n].at[rows], staged) for (n, rows), staged in zip(further, staged_refs)]
    behind = copies(pairs, further_sem, 1)
    starts = lax.axis_index("pipe") == layer

    @pl.when(starts)
    def _():
        fill_rows(share, rows_ref, own_ref, peer_refs)
        unit_grads(parts, share, rows_ref, down_ref, gate_ref, unit_ref)

    for c in range(chunks):
        cols = slice(c * size, (c + 1) * size)
        arriving[c].wait()

        @pl.when(starts)
        def _(cols=cols):
            term = lax.dot_general(
                unit_ref[...], held_ref[cols, :], (((1,), (1,)), ((), ())), preferred_element_type=F32
            )
            hand_out(share, term, cols, kept_ref, sent_refs)

        @pl.when(jnp.logical_not(starts))
        def _(cols=cols):
            turned_ref[:, cols] = held_ref[cols, :].T

    for (copy,) in behind:
        copy.wait()


def first_step(layer, own, peers, w_down, w_up, gates, arrays, split):
    share, width = own.shape
    units = w_down.shape[1]
    parts = lax.axis_size("tensor")
    rows = share * parts
    further = [(n, slice(0, a.shape[0])) for n, a in enumerate(arrays)]
    for n, a in enumerate(split, len(arrays)):
        half = a.shape[0] // 2
        further += [(n, slice(0, half)), (n, slice(half, 2 * half))]
    sources = [*arrays, *split]
    hbm = pl.BlockSpec(memory_space=pltpu.HBM)
    outs = pl.pallas_call(
        functools.partial(first_kernel, layer, parts, len(peers), further),
        out_shape=[pltpu.VMEM((units, width), BF16), jax.ShapeDtypeStruct((share, width), F32)]
        + [jax.ShapeDtypeStruct((share, width), BF16)] * (parts - 1)
        + [pltpu.VMEM((rows.stop - rows.start, sources[n].shape[1]), BF16) for n, rows in further],
        in_specs=[VMEM] * (len(peers) + 2) + [hbm, VMEM] + [hbm] * len(sources),
        out_specs=[VMEM] * (1 + parts + len(further)),
        scratch_shapes=[
            pltpu.VMEM((rows, width), BF16),
            pltpu.VMEM((rows, units), BF16),
            pltpu.VMEM((width, units), BF16),
            pltpu.SemaphoreType.DMA((1, 4)),
            pltpu.SemaphoreType.DMA((len(further), 1)),
        ],
        compiler_params=pltpu.CompilerParams(vmem_limit_bytes=20 * MIB),
        cost_estimate=CHEAP,
        name="first_step",
    )(
        own,
        *peers,
        w_down,
        pltpu.with_memory_space_constraint(w_up, pltpu.HBM),
        gates,
        *[pltpu.with_memory_space_constraint(a, pltpu.HBM) for a in sources],
    )
    return outs[0], outs[1], outs[2 : parts + 1], outs[parts + 1 :]


def section_step(layer, own, peers, w_down, turned, gates, after=()):
    share, width = own.shape
    units = w_down.shape[1]
    pieces = len(peers)
    parts = lax.axis_size("tensor")
    rows = share * parts

    def kernel(*refs):
        step_kernel(layer, parts, pieces, *refs[: pieces + 4], *refs[pieces + 4 + len(after) :])

    return pl.pallas_call(
        kernel,
        out_shape=[jax.ShapeDtypeStruct((share, width), F32)]
        + [jax.ShapeDtypeStruct((share, width), BF16)] * (parts - 1),
        in_specs=[VMEM] * (pieces + 4) + [pl.BlockSpec(memory_space=pl.ANY)] * len(after),
        out_specs=[VMEM] * parts,
        scratch_shapes=[pltpu.VMEM((rows, width), BF16), pltpu.VMEM((rows, units), BF16)],
        compiler_params=pltpu.CompilerParams(vmem_limit_bytes=12 * MIB),
        cost_estimate=CHEAP,
        name="section_step",
    )(own, *peers, w_down, turned, gates, *after)


def pack_block(source, k, target, at):
    owners = lax.axis_size("dp")
    tokens, width = source.shape
    size = width // owners
    rows = tokens * size // target.shape[1]
    column = pl.multiple_of((lax.axis_index("dp") ^ k) * size, size)
    for q in range(tokens // rows):
        target[at : at + rows, q * size : (q + 1) * size] = source[
            q * rows : (q + 1) * rows, pl.ds(column, size)
        ]
    return rows


def norm_kernel(layer, parts, earlier, owners, passed, handed, kept_ref, *refs):
    arrived = refs[: parts - 1]
    up_ref, in_ref, gain_ref = refs[parts - 1 : parts + 2]
    refs = refs[parts + 2 :]
    earlier_refs, refs = refs[:earlier], refs[earlier:]
    first_ref, pass_refs, refs = refs[0], refs[1 : 1 + passed], refs[1 + passed :]
    out_ref, block_refs, handed_refs = refs[0], refs[1 : len(refs) - len(handed)], refs[len(refs) - len(handed) :]
    segment = lax.axis_index("pipe")

    def cut(source):
        size = source.shape[1] // owners
        for k, ref in enumerate(block_refs, 1):
            at = pl.multiple_of((lax.axis_index("dp") ^ k) * size, size)
            ref[...] = source[:, pl.ds(at, size)]

    @pl.when(segment == layer)
    def _():
        normed = kept_ref[...]
        for ref in arrived:
            normed = normed + ref[...].astype(F32)
        rows_in = in_ref[...].astype(F32)
        inverse_rms = lax.rsqrt(jnp.mean(rows_in * rows_in, axis=-1, keepdims=True) + EPS_NORM)
        scaled = normed * gain_ref[...]
        mean_term = jnp.mean(rows_in * scaled, axis=-1, keepdims=True)
        out_ref[...] = (
            up_ref[...].astype(F32)
            + inverse_rms * scaled
            - rows_in * (inverse_rms * inverse_rms * inverse_rms * mean_term)
        ).astype(BF16)
        cut(out_ref)

    for above, ref in enumerate(earlier_refs):

        @pl.when(segment == layer + earlier - above)
        def _(ref=ref):
            cut(ref)
            if layer == 0:
                out_ref[...] = ref[...]

    sources = iter(pass_refs)
    for recipe, target in zip(handed, handed_refs):
        at = 0
        for piece in recipe:
            if isinstance(piece, int):
                at += pack_block(first_ref, piece, target, at)
            else:
                start, rows = piece
                target[at : at + rows, :] = next(sources)[start : start + rows, :]
                at += rows


def norm_step(layer, kept, arrived, upstream, rows_in, gain, first, earlier=(), owners=1, passed=()):
    parts = len(arrived) + 1
    share, width = upstream.shape
    block = jax.ShapeDtypeStruct((share, width // owners), BF16)
    recipes = [[p if isinstance(p, int) else p[1:] for p in group] for group in passed]
    handed = []
    for group in passed:
        units = passed[0][0][0].shape[1]
        block_rows = share * (width // lax.axis_size("dp")) // units
        rows = sum(block_rows if isinstance(p, int) else p[2] for p in group)
        handed.append(jax.ShapeDtypeStruct((rows, units), BF16))
    passed = [p[0] for group in passed for p in group if not isinstance(p, int)]
    outs = pl.pallas_call(
        functools.partial(norm_kernel, layer, parts, len(earlier), owners, len(passed), recipes),
        out_shape=[jax.ShapeDtypeStruct(upstream.shape, BF16)]
        + [block] * (owners - 1)
        + handed,
        in_specs=[VMEM] * (parts + 4 + len(earlier) + len(passed)),
        out_specs=[VMEM] * (owners + len(handed)),
        compiler_params=pltpu.CompilerParams(vmem_limit_bytes=8 * MIB),
        cost_estimate=CHEAP,
        name="norm_step",
    )(kept, *arrived, upstream, rows_in, gain, *earlier, first, *passed)
    return outs[0], outs[1:owners], outs[owners:]


def collect(upstreams, blocks, packed, after):
    sections = len(upstreams)
    owners = len(blocks) + 1
    share, size = blocks[0].shape
    count = sections + 2 * len(blocks)

    def kernel(*refs):
        out_ref = refs[-1]
        segment = lax.axis_index("pipe")
        at = pl.multiple_of(lax.axis_index("dp") * size, size)
        for s in range(sections):

            @pl.when(segment == sections - 1 - s)
            def _(s=s):
                out_ref[0:share, :] = refs[s][:, pl.ds(at, size)]

        @pl.when(segment < sections - 1)
        def _():
            for k in range(1, owners):
                out_ref[k * share : (k + 1) * share, :] = refs[sections + k - 1][...]

        @pl.when(segment == sections - 1)
        def _():
            for k in range(1, owners):
                source, start = refs[sections + owners + k - 2], packed[k - 1][1]
                pieces = source.shape[1] // size
                rows = share // pieces
                for q in range(pieces):
                    out_ref[k * share + q * rows : k * share + (q + 1) * rows, :] = source[
                        start : start + rows, q * size : (q + 1) * size
                    ]

    return pl.pallas_call(
        kernel,
        out_shape=jax.ShapeDtypeStruct((owners * share, size), BF16),
        in_specs=[VMEM] * count + [pl.BlockSpec(memory_space=pl.ANY)] * len(after),
        out_specs=VMEM,
        compiler_params=pltpu.CompilerParams(vmem_limit_bytes=4 * MIB),
        cost_estimate=CHEAP,
        name="collect",
    )(*upstreams, *blocks, *[array for array, _ in packed], *after)


def adam_update(gradient, current, moment_one, moment_two):
    first = BETA_ONE * moment_one + (1.0 - BETA_ONE) * gradient
    second = BETA_TWO * moment_two + (1.0 - BETA_TWO) * gradient * gradient
    root = second * lax.rsqrt(second)
    scale = math.sqrt(CORRECT_TWO)
    step = (first * (RATE * scale / CORRECT_ONE)) / (root + EPS_ADAM * scale)
    return first, second, (1.0 - RATE * DECAY) * current - step


def adam_kernel(sizes, *refs):
    owners, parts, share, tile, part_rows = sizes
    up_refs = refs[:parts]
    hidden_ref, down_ref, one_ref, two_ref = refs[parts : parts + 4]
    outs = refs[parts + 4 : parts + 7]
    rows_ref, *results, sem = refs[parts + 7 :]
    rows = rows_ref.shape[1]
    me = lax.axis_index("dp")
    part = lax.axis_index("tensor")
    for p in range(parts):
        for k in range(owners):
            at = k * parts + lax.rem(part + p, parts)
            rows_ref[pl.ds(pl.multiple_of(at * share, share), share), :] = up_refs[p][
                k * share : (k + 1) * share, :
            ]
    writes = []
    for i in range(rows // tile):
        turned = rows_ref[:, i * tile : (i + 1) * tile].T
        gradient = jnp.dot(turned, hidden_ref[...], preferred_element_type=F32)
        for j in range(tile // part_rows):
            at = i * tile + j * part_rows
            cut = slice(at, at + part_rows)
            current = down_ref[pl.ds(pl.multiple_of(me * rows + at, part_rows), part_rows), :].astype(F32)
            updates = adam_update(
                gradient[j * part_rows : (j + 1) * part_rows], current, one_ref[cut, :], two_ref[cut, :]
            )
            for q, update in enumerate(updates):
                results[q][cut, :] = update
                writes.append(
                    pltpu.make_async_copy(results[q].at[cut], outs[q].at[cut], sem.at[at // part_rows, q])
                )
                writes[-1].start()
    for write in writes:
        write.wait()


def adam_step(blocks, hidden_all, w_down, moment_one, moment_two, owners, parts):
    rows, units = moment_one.shape
    tokens = hidden_all.shape[0]
    tile = tile_of(rows, 128)
    part_rows = tile_of(tile, 64)
    return pl.pallas_call(
        functools.partial(adam_kernel, (owners, parts, blocks[0].shape[0] // owners, tile, part_rows)),
        out_shape=[jax.ShapeDtypeStruct((rows, units), F32)] * 3,
        in_specs=[VMEM] * (len(blocks) + 4),
        out_specs=[pl.BlockSpec(memory_space=pl.ANY)] * 3,
        scratch_shapes=[pltpu.VMEM((tokens, rows), BF16)]
        + [pltpu.VMEM((rows, units), F32)] * 3
        + [pltpu.SemaphoreType.DMA((rows // part_rows, 3))],
        compiler_params=pltpu.CompilerParams(vmem_limit_bytes=18 * MIB),
        cost_estimate=CHEAP,
        name="adam_step",
    )(*blocks, hidden_all, w_down, moment_one, moment_two)


def stack(order):
    count = len(order)
    total = sum(rows for _, _, rows in order)

    def kernel(*refs):
        out, sem = refs[-2:]
        started = []
        place = 0
        for n, (_, at, rows) in enumerate(order):
            started.append(
                pltpu.make_async_copy(
                    refs[n].at[at : at + rows], out.at[place : place + rows], sem.at[n]
                )
            )
            place += rows
        for copy in started:
            copy.start()
        for copy in started:
            copy.wait()

    return pl.pallas_call(
        kernel,
        out_shape=pltpu.VMEM((total, order[0][0].shape[1]), BF16),
        in_specs=[pl.BlockSpec(memory_space=pl.ANY)] * count,
        out_specs=VMEM,
        scratch_shapes=[pltpu.SemaphoreType.DMA((count,))],
        compiler_params=pltpu.CompilerParams(vmem_limit_bytes=4 * MIB),
        cost_estimate=CHEAP,
        name="stack",
    )(*[array for array, _, _ in order])


def adam_general(upstreams, hidden_all, w_down, moment_one, moment_two):
    owners = lax.axis_size("dp")
    sections = len(upstreams)
    segment = lax.axis_index("pipe")
    own = upstreams[0]
    for s in range(1, sections):
        own = jnp.where(segment == sections - 1 - s, upstreams[s], own)
    mine = lax.all_to_all(own, "dp", split_axis=1, concat_axis=0, tiled=True)
    share, rows = own.shape[0], mine.shape[1]
    turned = lax.all_gather(mine.reshape(owners, share, rows), "tensor", axis=1, tiled=True)
    gradient = lax.dot_general(
        turned.reshape(-1, rows), hidden_all, (((0,), (0,)), ((), ())), preferred_element_type=F32
    )
    at = lax.axis_index("dp") * rows
    current = lax.dynamic_slice_in_dim(w_down, at, rows, 0).astype(F32)
    return adam_update(gradient, current, moment_one, moment_two)


def from_peers(value, axis):
    size = lax.axis_size(axis)
    return [lax.ppermute(value, axis, [((i + k) % size, i) for i in range(size)]) for k in range(1, size)]


def to_peers(values, axis):
    size = lax.axis_size(axis)
    return [
        lax.ppermute(value, axis, [(i, (i + k) % size) for i in range(size)])
        for k, value in enumerate(values, 1)
    ]


def on_device(
    up_weight,
    down_weight,
    gate_act,
    hidden,
    block_input,
    norm_gain,
    loss_grad,
    moment_one,
    moment_two,
):
    sections = lax.axis_size("pipe")
    owners = lax.axis_size("dp")
    parts = lax.axis_size("tensor")
    width, units = down_weight.shape[1:]
    planned = sections == 4 and owners == 4 and width % (128 * owners) == 0 and units % (width // owners) == 0
    planned = planned and loss_grad.shape[0] * (width // owners) % (16 * units) == 0 and parts == 2
    share = loss_grad.shape[0]
    saved = hidden[0]
    half = saved.shape[0] // 2
    w_down, gates, loss = stage([down_weight[0], gate_act[0], loss_grad])
    turned = None
    upstreams = [loss]
    grads = []
    late = ()
    for layer in reversed(range(sections)):
        upstream = upstreams[-1]
        if planned and not layer:
            peers = [lax.all_gather(upstream, "tensor", axis=0, tiled=True)]
        else:
            peers = from_peers(upstream if grads else loss_grad, "tensor")
        if not grads:
            turned, kept, sent, (rows_in, *halves) = first_step(
                layer,
                upstream,
                peers,
                w_down,
                up_weight[0],
                gates,
                [block_input[0]],
                [saved] if planned else [],
            )
        elif planned and len(grads) == 2:
            unit_grad = unit_step(layer, upstream, peers, w_down, gates)
            kept, *sent = width_step(layer, unit_grad, turned, loss_grad.shape[0], late)
        else:
            kept, *sent = section_step(layer, upstream, peers, w_down, turned, gates, after=late)
        if planned and not layer:
            hidden_all = stack(
                [
                    (halves[0], 0, half),
                    (halves[1], 0, half),
                    (along_upper, 0, half),
                    (along_rest, 0, half),
                    (side_rest, 0, half),
                    (side_lower, 0, half),
                    (side_rest, half, half),
                    (along_rest, half, half),
                ]
            )
            packed = [(along_upper, half), (side_lower, half), (corner, 0)]
            own = collect(upstreams, blocks, packed, [kept, hidden_all])
        arrived = to_peers(sent, "tensor")
        window = len(grads)
        moving = ()
        if planned and window == 0:
            moving = [[(halves[0], 0, half), 1], [(halves[1], 0, half), 2]]
        elif planned and window == 1:
            moving = [
                [(halves[1], 0, half), (side_lower, 0, half)],
                [(halves[0], 0, half), (along_upper, 0, half)],
                [3],
            ]
        grad, cuts, handed = norm_step(
            layer,
            kept,
            arrived,
            upstream,
            rows_in,
            norm_gain,
            loss,
            earlier=grads if window >= sections - 2 else (),
            owners=owners if planned and window == 2 else 1,
            passed=moving,
        )
        grads.append(grad)
        if layer:
            upstreams.append(lax.ppermute(grad, "pipe", [(layer, layer - 1)]))
        if planned and layer:
            if window == 2:
                blocks = [
                    lax.ppermute(
                        cut,
                        ("pipe", "dp"),
                        [
                            (s * owners + i, (s - 1) * owners + (i ^ k))
                            for s in range(1, sections)
                            for i in range(owners)
                        ],
                    )
                    for k, cut in enumerate(cuts, 1)
                ]
            if window < 2:
                exchange = [
                    lax.ppermute(piece, "dp", [(i, i ^ k) for i in range(owners)])
                    for k, piece in enumerate(handed[:2], 1)
                ]
            if window == 0:
                along_upper, side_lower = exchange
                moments = stage_in_section(
                    [moment_one[0], moment_two[0]], lambda section: section != sections - 2, (), [grad]
                )
                late = [*exchange, *moments]
            elif window == 1:
                along_rest, side_rest = exchange
                start = (sections - 1) * owners
                corner = lax.ppermute(
                    handed[2], ("pipe", "dp"), [(start + i, start + (i ^ 3)) for i in range(owners)]
                )
                moments = stage_in_section(
                    [moment_one[0], moment_two[0]], lambda section: section == sections - 2, moments, [grad]
                )
                late = [*exchange, *moments]
            else:
                late = ()
    if planned:
        first, second, updated = adam_step(
            [own, *from_peers(own, "tensor")], hidden_all, w_down, *moments, owners, parts
        )
    else:
        hidden_all = lax.all_gather(saved, "dp", axis=0, tiled=True)
        first, second, updated = adam_general(
            upstreams, hidden_all, w_down, moment_one[0], moment_two[0]
        )
    return (grads[-1][None], first[None], second[None], updated[None])


def solution(mesh):
    in_specs = (
        P("pipe", None, "tensor"),
        P("pipe", None, "tensor"),
        P("pipe", "dp", "tensor"),
        P("pipe", "dp", "tensor"),
        P("pipe", ("dp", "tensor"), None),
        P("pipe", None),
        P(("dp", "tensor"), None),
        P("pipe", "dp", "tensor"),
        P("pipe", "dp", "tensor"),
    )
    out_specs = (
        P("pipe", ("dp", "tensor"), None),
        P("pipe", "dp", "tensor"),
        P("pipe", "dp", "tensor"),
        P("pipe", "dp", "tensor"),
    )
    return jax.shard_map(
        on_device, mesh=mesh, in_specs=in_specs, out_specs=out_specs, check_vma=False
    )
```

```python
import functools
import math
import jax
import jax.numpy as jnp
from jax import lax
from jax.experimental import pallas as pl
from jax.experimental.pallas import tpu as pltpu
from jax.sharding import PartitionSpec as P

EPS_NORM = 1e-05
EPS_ADAM = 1e-08
BETA_ONE = 0.9
BETA_TWO = 0.95
RATE = 0.01
DECAY = 0.1
CORRECT_ONE = 1.0 - 0.9**10
CORRECT_TWO = 1.0 - 0.95**10

MIB = 2**20
VMEM = pl.BlockSpec(memory_space=pltpu.VMEM)
CHEAP = pl.CostEstimate(flops=0, bytes_accessed=0, transcendentals=0)
F32 = jnp.float32
BF16 = jnp.bfloat16


def tile_of(extent, most):
    tile = min(extent, most)
    while extent % tile:
        tile //= 2
    return tile


def copies(pairs, sem, chunks):
    started = []
    for n, (source, target) in enumerate(pairs):
        rows = source.shape[0] // chunks
        cut = [slice(c * rows, (c + 1) * rows) for c in range(chunks)]
        started.append(
            [pltpu.make_async_copy(source.at[r], target.at[r], sem.at[n, c]) for c, r in enumerate(cut)]
        )
    for array in started:
        for copy in array:
            copy.start()
    return started


def stage(arrays):
    count = len(arrays)

    def kernel(*refs):
        for array in copies(list(zip(refs[:count], refs[count:-1])), refs[-1], 2):
            for copy in array:
                copy.wait()

    return pl.pallas_call(
        kernel,
        out_shape=[pltpu.VMEM(a.shape, a.dtype) for a in arrays],
        in_specs=[pl.BlockSpec(memory_space=pltpu.HBM)] * count,
        out_specs=[VMEM] * count,
        scratch_shapes=[pltpu.SemaphoreType.DMA((count, 2))],
        compiler_params=pltpu.CompilerParams(vmem_limit_bytes=4 * MIB),
        cost_estimate=pl.CostEstimate(
            flops=0, bytes_accessed=sum(2 * a.size * a.dtype.itemsize for a in arrays), transcendentals=0
        ),
        name="stage",
    )(*[pltpu.with_memory_space_constraint(a, pltpu.HBM) for a in arrays])


def stage_in_section(arrays, wanted, held, after):
    count = len(arrays)

    def kernel(*refs):
        sources, targets, sem = refs[:count], refs[count + len(held) + len(after) : -1], refs[-1]

        @pl.when(wanted(lax.axis_index("pipe")))
        def _():
            for array in copies(list(zip(sources, targets)), sem, 2):
                for copy in array:
                    copy.wait()

    return pl.pallas_call(
        kernel,
        out_shape=[pltpu.VMEM(a.shape, a.dtype) for a in arrays],
        in_specs=[pl.BlockSpec(memory_space=pltpu.HBM)] * count
        + [VMEM] * len(held)
        + [pl.BlockSpec(memory_space=pl.ANY)] * len(after),
        out_specs=[VMEM] * count,
        input_output_aliases={count + n: n for n in range(len(held))},
        scratch_shapes=[pltpu.SemaphoreType.DMA((count, 2))],
        compiler_params=pltpu.CompilerParams(vmem_limit_bytes=4 * MIB),
        cost_estimate=CHEAP,
        name="stage_in_section",
    )(*[pltpu.with_memory_space_constraint(a, pltpu.HBM) for a in arrays], *held, *after)


def unit_grads(parts, share, rows_ref, down_ref, gate_ref, unit_ref):
    me = lax.axis_index("tensor")
    term = jnp.dot(rows_ref[...], down_ref[...], preferred_element_type=F32)
    for k in range(parts):
        at = pl.multiple_of(lax.rem(me + k, parts) * share, share)
        gates = gate_ref[pl.ds(at, share), :].astype(F32)
        unit_ref[k * share : (k + 1) * share, :] = (term[k * share : (k + 1) * share] * gates).astype(BF16)


def hand_out(share, term, cols, kept_ref, sent_refs):
    kept_ref[:, cols] = term[0:share]
    for k, ref in enumerate(sent_refs, 1):
        ref[:, cols] = term[k * share : (k + 1) * share].astype(BF16)


def fill_rows(share, rows_ref, own_ref, peer_refs):
    rows_ref[0:share, :] = own_ref[...]
    parts = rows_ref.shape[0] // share
    me = lax.axis_index("tensor")
    for k in range(1, parts):
        if peer_refs[0].shape[0] > share:
            at = pl.multiple_of(lax.rem(me + k, parts) * share, share)
            rows_ref[k * share : (k + 1) * share, :] = peer_refs[0][pl.ds(at, share), :]
        else:
            rows_ref[k * share : (k + 1) * share, :] = peer_refs[k - 1][...]


def step_kernel(layer, parts, pieces, own_ref, *refs):
    peer_refs, refs = refs[:pieces], refs[pieces:]
    down_ref, turned_ref, gate_ref, kept_ref = refs[:4]
    sent_refs = refs[4 : parts + 3]
    rows_ref, unit_ref = refs[parts + 3 :]
    share = own_ref.shape[0]

    @pl.when(lax.axis_index("pipe") == layer)
    def _():
        fill_rows(share, rows_ref, own_ref, peer_refs)
        unit_grads(parts, share, rows_ref, down_ref, gate_ref, unit_ref)
        term = jnp.dot(unit_ref[...], turned_ref[...], preferred_element_type=F32)
        hand_out(share, term, slice(None), kept_ref, sent_refs)


def unit_kernel(layer, parts, own_ref, *refs):
    peer_refs = refs[: parts - 1]
    down_ref, gate_ref, unit_ref, rows_ref = refs[parts - 1 :]
    share = own_ref.shape[0]

    @pl.when(lax.axis_index("pipe") == layer)
    def _():
        fill_rows(share, rows_ref, own_ref, peer_refs)
        unit_grads(parts, share, rows_ref, down_ref, gate_ref, unit_ref)


def unit_step(layer, own, peers, w_down, gates):
    parts = len(peers) + 1
    rows = own.shape[0] * parts
    return pl.pallas_call(
        functools.partial(unit_kernel, layer, parts),
        out_shape=jax.ShapeDtypeStruct((rows, w_down.shape[1]), BF16),
        in_specs=[VMEM] * (parts + 2),
        out_specs=VMEM,
        scratch_shapes=[pltpu.VMEM((rows, own.shape[1]), BF16)],
        compiler_params=pltpu.CompilerParams(vmem_limit_bytes=12 * MIB),
        cost_estimate=CHEAP,
        name="unit_step",
    )(own, *peers, w_down, gates)


def width_step(layer, unit_grad, turned, share, after):
    width = turned.shape[1]
    parts = unit_grad.shape[0] // share

    def kernel(unit_ref, turned_ref, *refs):
        kept_ref, *sent_refs = refs[len(after) :]

        @pl.when(lax.axis_index("pipe") == layer)
        def _():
            term = jnp.dot(unit_ref[...], turned_ref[...], preferred_element_type=F32)
            hand_out(share, term, slice(None), kept_ref, sent_refs)

    return pl.pallas_call(
        kernel,
        out_shape=[jax.ShapeDtypeStruct((share, width), F32)]
        + [jax.ShapeDtypeStruct((share, width), BF16)] * (parts - 1),
        in_specs=[VMEM, VMEM] + [pl.BlockSpec(memory_space=pl.ANY)] * len(after),
        out_specs=[VMEM] * parts,
        compiler_params=pltpu.CompilerParams(vmem_limit_bytes=12 * MIB),
        cost_estimate=CHEAP,
        name="width_step",
    )(unit_grad, turned, *after)


def first_kernel(layer, parts, pieces, further, own_ref, *refs):
    peer_refs, refs = refs[:pieces], refs[pieces:]
    down_ref, up_ref, gate_ref = refs[:3]
    count = 1 + max((n for n, _ in further), default=-1)
    source_refs, refs = refs[3 : 3 + count], refs[3 + count :]
    turned_ref, kept_ref = refs[:2]
    sent_refs = refs[2 : parts + 1]
    staged_refs = refs[parts + 1 : parts + 1 + len(further)]
    rows_ref, unit_ref, held_ref, sem, further_sem = refs[parts + 1 + len(further) :]
    share = own_ref.shape[0]
    chunks = sem.shape[1]
    size = held_ref.shape[0] // chunks
    (arriving,) = copies([(up_ref, held_ref)], sem, chunks)
    pairs = [(source_refs[n].at[rows], staged) for (n, rows), staged in zip(further, staged_refs)]
    behind = copies(pairs, further_sem, 1)
    starts = lax.axis_index("pipe") == layer

    def turn(first, count):
        for c in range(first, first + count):
            arriving[c].wait()
        cols = slice(first * size, (first + count) * size)
        turned_ref[:, cols] = held_ref[cols, :].T

    def product(first, count):
        cols = slice(first * size, (first + count) * size)
        term = jnp.dot(unit_ref[...], turned_ref[:, cols], preferred_element_type=F32)
        hand_out(share, term, cols, kept_ref, sent_refs)

    @pl.when(starts)
    def _():
        fill_rows(share, rows_ref, own_ref, peer_refs)
        unit_grads(parts, share, rows_ref, down_ref, gate_ref, unit_ref)
        turn(0, 2)
        for c in range(2, chunks, 2):
            turn(c, 2)
            product(c - 2, 2)
        product(chunks - 2, 2)

    @pl.when(jnp.logical_not(starts))
    def _():
        for c in range(chunks):
            turn(c, 1)

    for (copy,) in behind:
        copy.wait()


def first_step(layer, own, peers, w_down, w_up, gates, arrays, split):
    share, width = own.shape
    units = w_down.shape[1]
    parts = lax.axis_size("tensor")
    rows = share * parts
    further = [(n, slice(0, a.shape[0])) for n, a in enumerate(arrays)]
    for n, a in enumerate(split, len(arrays)):
        half = a.shape[0] // 2
        further += [(n, slice(0, half)), (n, slice(half, 2 * half))]
    sources = [*arrays, *split]
    hbm = pl.BlockSpec(memory_space=pltpu.HBM)
    outs = pl.pallas_call(
        functools.partial(first_kernel, layer, parts, len(peers), further),
        out_shape=[pltpu.VMEM((units, width), BF16), jax.ShapeDtypeStruct((share, width), F32)]
        + [jax.ShapeDtypeStruct((share, width), BF16)] * (parts - 1)
        + [pltpu.VMEM((rows.stop - rows.start, sources[n].shape[1]), BF16) for n, rows in further],
        in_specs=[VMEM] * (len(peers) + 2) + [hbm, VMEM] + [hbm] * len(sources),
        out_specs=[VMEM] * (1 + parts + len(further)),
        scratch_shapes=[
            pltpu.VMEM((rows, width), BF16),
            pltpu.VMEM((rows, units), BF16),
            pltpu.VMEM((width, units), BF16),
            pltpu.SemaphoreType.DMA((1, 8)),
            pltpu.SemaphoreType.DMA((len(further), 1)),
        ],
        compiler_params=pltpu.CompilerParams(vmem_limit_bytes=20 * MIB),
        cost_estimate=CHEAP,
        name="first_step",
    )(
        own,
        *peers,
        w_down,
        pltpu.with_memory_space_constraint(w_up, pltpu.HBM),
        gates,
        *[pltpu.with_memory_space_constraint(a, pltpu.HBM) for a in sources],
    )
    return outs[0], outs[1], outs[2 : parts + 1], outs[parts + 1 :]


def section_step(layer, own, peers, w_down, turned, gates, after=()):
    share, width = own.shape
    units = w_down.shape[1]
    pieces = len(peers)
    parts = lax.axis_size("tensor")
    rows = share * parts

    def kernel(*refs):
        step_kernel(layer, parts, pieces, *refs[: pieces + 4], *refs[pieces + 4 + len(after) :])

    return pl.pallas_call(
        kernel,
        out_shape=[jax.ShapeDtypeStruct((share, width), F32)]
        + [jax.ShapeDtypeStruct((share, width), BF16)] * (parts - 1),
        in_specs=[VMEM] * (pieces + 4) + [pl.BlockSpec(memory_space=pl.ANY)] * len(after),
        out_specs=[VMEM] * parts,
        scratch_shapes=[pltpu.VMEM((rows, width), BF16), pltpu.VMEM((rows, units), BF16)],
        compiler_params=pltpu.CompilerParams(vmem_limit_bytes=12 * MIB),
        cost_estimate=CHEAP,
        name="section_step",
    )(own, *peers, w_down, turned, gates, *after)


def pack_block(source, k, target, at):
    owners = lax.axis_size("dp")
    tokens, width = source.shape
    size = width // owners
    rows = tokens * size // target.shape[1]
    column = pl.multiple_of((lax.axis_index("dp") ^ k) * size, size)
    for q in range(tokens // rows):
        target[at : at + rows, q * size : (q + 1) * size] = source[
            q * rows : (q + 1) * rows, pl.ds(column, size)
        ]
    return rows


def norm_kernel(layer, parts, earlier, owners, passed, handed, kept_ref, *refs):
    arrived = refs[: parts - 1]
    up_ref, in_ref, gain_ref = refs[parts - 1 : parts + 2]
    refs = refs[parts + 2 :]
    earlier_refs, refs = refs[:earlier], refs[earlier:]
    first_ref, pass_refs, refs = refs[0], refs[1 : 1 + passed], refs[1 + passed :]
    out_ref, block_refs, handed_refs = refs[0], refs[1 : len(refs) - len(handed)], refs[len(refs) - len(handed) :]
    segment = lax.axis_index("pipe")

    def cut(source):
        size = source.shape[1] // owners
        for k, ref in enumerate(block_refs, 1):
            at = pl.multiple_of((lax.axis_index("dp") ^ k) * size, size)
            ref[...] = source[:, pl.ds(at, size)]

    @pl.when(segment == layer)
    def _():
        normed = kept_ref[...]
        for ref in arrived:
            normed = normed + ref[...].astype(F32)
        rows_in = in_ref[...].astype(F32)
        inverse_rms = lax.rsqrt(jnp.mean(rows_in * rows_in, axis=-1, keepdims=True) + EPS_NORM)
        scaled = normed * gain_ref[...]
        mean_term = jnp.mean(rows_in * scaled, axis=-1, keepdims=True)
        out_ref[...] = (
            up_ref[...].astype(F32)
            + inverse_rms * scaled
            - rows_in * (inverse_rms * inverse_rms * inverse_rms * mean_term)
        ).astype(BF16)
        cut(out_ref)

    for above, ref in enumerate(earlier_refs):

        @pl.when(segment == layer + earlier - above)
        def _(ref=ref):
            cut(ref)
            if layer == 0:
                out_ref[...] = ref[...]

    sources = iter(pass_refs)
    for recipe, target in zip(handed, handed_refs):
        at = 0
        for piece in recipe:
            if isinstance(piece, int):
                at += pack_block(first_ref, piece, target, at)
            else:
                start, rows = piece
                target[at : at + rows, :] = next(sources)[start : start + rows, :]
                at += rows


def norm_step(layer, kept, arrived, upstream, rows_in, gain, first, earlier=(), owners=1, passed=()):
    parts = len(arrived) + 1
    share, width = upstream.shape
    block = jax.ShapeDtypeStruct((share, width // owners), BF16)
    recipes = [[p if isinstance(p, int) else p[1:] for p in group] for group in passed]
    handed = []
    for group in passed:
        units = passed[0][0][0].shape[1]
        block_rows = share * (width // lax.axis_size("dp")) // units
        rows = sum(block_rows if isinstance(p, int) else p[2] for p in group)
        handed.append(jax.ShapeDtypeStruct((rows, units), BF16))
    passed = [p[0] for group in passed for p in group if not isinstance(p, int)]
    outs = pl.pallas_call(
        functools.partial(norm_kernel, layer, parts, len(earlier), owners, len(passed), recipes),
        out_shape=[jax.ShapeDtypeStruct(upstream.shape, BF16)]
        + [block] * (owners - 1)
        + handed,
        in_specs=[VMEM] * (parts + 4 + len(earlier) + len(passed)),
        out_specs=[VMEM] * (owners + len(handed)),
        compiler_params=pltpu.CompilerParams(vmem_limit_bytes=8 * MIB),
        cost_estimate=CHEAP,
        name="norm_step",
    )(kept, *arrived, upstream, rows_in, gain, *earlier, first, *passed)
    return outs[0], outs[1:owners], outs[owners:]


def collect(upstreams, blocks, packed, after):
    sections = len(upstreams)
    owners = len(blocks) + 1
    share, size = blocks[0].shape
    count = sections + 2 * len(blocks)

    def kernel(*refs):
        out_ref = refs[-1]
        segment = lax.axis_index("pipe")
        at = pl.multiple_of(lax.axis_index("dp") * size, size)
        for s in range(sections):

            @pl.when(segment == sections - 1 - s)
            def _(s=s):
                out_ref[0:share, :] = refs[s][:, pl.ds(at, size)]

        @pl.when(segment < sections - 1)
        def _():
            for k in range(1, owners):
                out_ref[k * share : (k + 1) * share, :] = refs[sections + k - 1][...]

        @pl.when(segment == sections - 1)
        def _():
            for k in range(1, owners):
                source, start = refs[sections + owners + k - 2], packed[k - 1][1]
                pieces = source.shape[1] // size
                rows = share // pieces
                for q in range(pieces):
                    out_ref[k * share + q * rows : k * share + (q + 1) * rows, :] = source[
                        start : start + rows, q * size : (q + 1) * size
                    ]

    return pl.pallas_call(
        kernel,
        out_shape=jax.ShapeDtypeStruct((owners * share, size), BF16),
        in_specs=[VMEM] * count + [pl.BlockSpec(memory_space=pl.ANY)] * len(after),
        out_specs=VMEM,
        compiler_params=pltpu.CompilerParams(vmem_limit_bytes=4 * MIB),
        cost_estimate=CHEAP,
        name="collect",
    )(*upstreams, *blocks, *[array for array, _ in packed], *after)


def adam_update(gradient, current, moment_one, moment_two):
    first = BETA_ONE * moment_one + (1.0 - BETA_ONE) * gradient
    second = BETA_TWO * moment_two + (1.0 - BETA_TWO) * gradient * gradient
    root = second * lax.rsqrt(second)
    scale = math.sqrt(CORRECT_TWO)
    step = (first * (RATE * scale / CORRECT_ONE)) / (root + EPS_ADAM * scale)
    return first, second, (1.0 - RATE * DECAY) * current - step


def adam_kernel(sizes, *refs):
    owners, parts, share, tile, part_rows = sizes
    up_refs = refs[:parts]
    hidden_ref, down_ref, one_ref, two_ref = refs[parts : parts + 4]
    outs = refs[parts + 4 : parts + 7]
    rows_ref, *results, sem = refs[parts + 7 :]
    rows = rows_ref.shape[1]
    me = lax.axis_index("dp")
    part = lax.axis_index("tensor")
    for p in range(parts):
        for k in range(owners):
            at = k * parts + lax.rem(part + p, parts)
            rows_ref[pl.ds(pl.multiple_of(at * share, share), share), :] = up_refs[p][
                k * share : (k + 1) * share, :
            ]
    writes = []
    for i in range(rows // tile):
        turned = rows_ref[:, i * tile : (i + 1) * tile].T
        gradient = jnp.dot(turned, hidden_ref[...], preferred_element_type=F32)
        for j in range(tile // part_rows):
            at = i * tile + j * part_rows
            cut = slice(at, at + part_rows)
            current = down_ref[pl.ds(pl.multiple_of(me * rows + at, part_rows), part_rows), :].astype(F32)
            updates = adam_update(
                gradient[j * part_rows : (j + 1) * part_rows], current, one_ref[cut, :], two_ref[cut, :]
            )
            for q, update in enumerate(updates):
                results[q][cut, :] = update
                writes.append(
                    pltpu.make_async_copy(results[q].at[cut], outs[q].at[cut], sem.at[at // part_rows, q])
                )
                writes[-1].start()
    for write in writes:
        write.wait()


def adam_step(blocks, hidden_all, w_down, moment_one, moment_two, owners, parts):
    rows, units = moment_one.shape
    tokens = hidden_all.shape[0]
    tile = tile_of(rows, 128)
    part_rows = tile_of(tile, 64)
    return pl.pallas_call(
        functools.partial(adam_kernel, (owners, parts, blocks[0].shape[0] // owners, tile, part_rows)),
        out_shape=[jax.ShapeDtypeStruct((rows, units), F32)] * 3,
        in_specs=[VMEM] * (len(blocks) + 4),
        out_specs=[pl.BlockSpec(memory_space=pl.ANY)] * 3,
        scratch_shapes=[pltpu.VMEM((tokens, rows), BF16)]
        + [pltpu.VMEM((rows, units), F32)] * 3
        + [pltpu.SemaphoreType.DMA((rows // part_rows, 3))],
        compiler_params=pltpu.CompilerParams(vmem_limit_bytes=18 * MIB),
        cost_estimate=CHEAP,
        name="adam_step",
    )(*blocks, hidden_all, w_down, moment_one, moment_two)


def stack(order):
    count = len(order)
    total = sum(rows for _, _, rows in order)

    def kernel(*refs):
        out, sem = refs[-2:]
        started = []
        place = 0
        for n, (_, at, rows) in enumerate(order):
            started.append(
                pltpu.make_async_copy(
                    refs[n].at[at : at + rows], out.at[place : place + rows], sem.at[n]
                )
            )
            place += rows
        for copy in started:
            copy.start()
        for copy in started:
            copy.wait()

    return pl.pallas_call(
        kernel,
        out_shape=pltpu.VMEM((total, order[0][0].shape[1]), BF16),
        in_specs=[pl.BlockSpec(memory_space=pl.ANY)] * count,
        out_specs=VMEM,
        scratch_shapes=[pltpu.SemaphoreType.DMA((count,))],
        compiler_params=pltpu.CompilerParams(vmem_limit_bytes=4 * MIB),
        cost_estimate=CHEAP,
        name="stack",
    )(*[array for array, _, _ in order])


def adam_general(upstreams, hidden_all, w_down, moment_one, moment_two):
    owners = lax.axis_size("dp")
    sections = len(upstreams)
    segment = lax.axis_index("pipe")
    own = upstreams[0]
    for s in range(1, sections):
        own = jnp.where(segment == sections - 1 - s, upstreams[s], own)
    mine = lax.all_to_all(own, "dp", split_axis=1, concat_axis=0, tiled=True)
    share, rows = own.shape[0], mine.shape[1]
    turned = lax.all_gather(mine.reshape(owners, share, rows), "tensor", axis=1, tiled=True)
    gradient = lax.dot_general(
        turned.reshape(-1, rows), hidden_all, (((0,), (0,)), ((), ())), preferred_element_type=F32
    )
    at = lax.axis_index("dp") * rows
    current = lax.dynamic_slice_in_dim(w_down, at, rows, 0).astype(F32)
    return adam_update(gradient, current, moment_one, moment_two)


def from_peers(value, axis):
    size = lax.axis_size(axis)
    return [lax.ppermute(value, axis, [((i + k) % size, i) for i in range(size)]) for k in range(1, size)]


def to_peers(values, axis):
    size = lax.axis_size(axis)
    return [
        lax.ppermute(value, axis, [(i, (i + k) % size) for i in range(size)])
        for k, value in enumerate(values, 1)
    ]


def on_device(
    up_weight,
    down_weight,
    gate_act,
    hidden,
    block_input,
    norm_gain,
    loss_grad,
    moment_one,
    moment_two,
):
    sections = lax.axis_size("pipe")
    owners = lax.axis_size("dp")
    parts = lax.axis_size("tensor")
    width, units = down_weight.shape[1:]
    planned = sections == 4 and owners == 4 and width % (128 * owners) == 0 and units % (width // owners) == 0
    planned = planned and loss_grad.shape[0] * (width // owners) % (16 * units) == 0 and parts == 2
    share = loss_grad.shape[0]
    saved = hidden[0]
    half = saved.shape[0] // 2
    w_down, gates, loss = stage([down_weight[0], gate_act[0], loss_grad])
    turned = None
    upstreams = [loss]
    grads = []
    late = ()
    for layer in reversed(range(sections)):
        upstream = upstreams[-1]
        if planned and not layer:
            peers = [lax.all_gather(upstream, "tensor", axis=0, tiled=True)]
        else:
            peers = from_peers(upstream if grads else loss_grad, "tensor")
        if not grads:
            turned, kept, sent, (rows_in, *halves) = first_step(
                layer,
                upstream,
                peers,
                w_down,
                up_weight[0],
                gates,
                [block_input[0]],
                [saved] if planned else [],
            )
        elif planned and layer:
            unit_grad = unit_step(layer, upstream, peers, w_down, gates)
            kept, *sent = width_step(layer, unit_grad, turned, loss_grad.shape[0], late)
        else:
            kept, *sent = section_step(layer, upstream, peers, w_down, turned, gates, after=late)
        if planned and not layer:
            hidden_all = stack(
                [
                    (halves[0], 0, half),
                    (halves[1], 0, half),
                    (along_upper, 0, half),
                    (along_rest, 0, half),
                    (side_rest, 0, half),
                    (side_lower, 0, half),
                    (side_rest, half, half),
                    (along_rest, half, half),
                ]
            )
            packed = [(along_upper, half), (side_lower, half), (corner, 0)]
            own = collect(upstreams, blocks, packed, [kept, hidden_all])
        arrived = to_peers(sent, "tensor")
        window = len(grads)
        moving = ()
        if planned and window == 0:
            moving = [[(halves[0], 0, half), 1], [(halves[1], 0, half), 2]]
        elif planned and window == 1:
            moving = [
                [(halves[1], 0, half), (side_lower, 0, half)],
                [(halves[0], 0, half), (along_upper, 0, half)],
                [3],
            ]
        grad, cuts, handed = norm_step(
            layer,
            kept,
            arrived,
            upstream,
            rows_in,
            norm_gain,
            loss,
            earlier=grads if window >= sections - 2 else (),
            owners=owners if planned and window == 2 else 1,
            passed=moving,
        )
        grads.append(grad)
        if layer:
            upstreams.append(lax.ppermute(grad, "pipe", [(layer, layer - 1)]))
        if planned and layer:
            if window == 2:
                blocks = [
                    lax.ppermute(
                        cut,
                        ("pipe", "dp"),
                        [
                            (s * owners + i, (s - 1) * owners + (i ^ k))
                            for s in range(1, sections)
                            for i in range(owners)
                        ],
                    )
                    for k, cut in enumerate(cuts, 1)
                ]
            if window < 2:
                exchange = [
                    lax.ppermute(piece, "dp", [(i, i ^ k) for i in range(owners)])
                    for k, piece in enumerate(handed[:2], 1)
                ]
            if window == 0:
                along_upper, side_lower = exchange
                moments = stage_in_section(
                    [moment_one[0], moment_two[0]], lambda section: section != sections - 2, (), [grad]
                )
                late = [*exchange, *moments]
            elif window == 1:
                along_rest, side_rest = exchange
                start = (sections - 1) * owners
                corner = lax.ppermute(
                    handed[2], ("pipe", "dp"), [(start + i, start + (i ^ 3)) for i in range(owners)]
                )
                moments = stage_in_section(
                    [moment_one[0], moment_two[0]], lambda section: section == sections - 2, moments, [grad]
                )
                late = [*exchange, *moments]
            else:
                late = ()
    if planned:
        first, second, updated = adam_step(
            [own, *from_peers(own, "tensor")], hidden_all, w_down, *moments, owners, parts
        )
    else:
        hidden_all = lax.all_gather(saved, "dp", axis=0, tiled=True)
        first, second, updated = adam_general(
            upstreams, hidden_all, w_down, moment_one[0], moment_two[0]
        )
    return (grads[-1][None], first[None], second[None], updated[None])


def solution(mesh):
    in_specs = (
        P("pipe", None, "tensor"),
        P("pipe", None, "tensor"),
        P("pipe", "dp", "tensor"),
        P("pipe", "dp", "tensor"),
        P("pipe", ("dp", "tensor"), None),
        P("pipe", None),
        P(("dp", "tensor"), None),
        P("pipe", "dp", "tensor"),
        P("pipe", "dp", "tensor"),
    )
    out_specs = (
        P("pipe", ("dp", "tensor"), None),
        P("pipe", "dp", "tensor"),
        P("pipe", "dp", "tensor"),
        P("pipe", "dp", "tensor"),
    )
    return jax.shard_map(
        on_device, mesh=mesh, in_specs=in_specs, out_specs=out_specs, check_vma=False
    )
```

```python
import functools
import math
import jax
import jax.numpy as jnp
from jax import lax
from jax.experimental import pallas as pl
from jax.experimental.pallas import tpu as pltpu
from jax.sharding import PartitionSpec as P

EPS_NORM = 1e-05
EPS_ADAM = 1e-08
BETA_ONE = 0.9
BETA_TWO = 0.95
RATE = 0.01
DECAY = 0.1
CORRECT_ONE = 1.0 - 0.9**10
CORRECT_TWO = 1.0 - 0.95**10

MIB = 2**20
VMEM = pl.BlockSpec(memory_space=pltpu.VMEM)
CHEAP = pl.CostEstimate(flops=0, bytes_accessed=0, transcendentals=0)
F32 = jnp.float32
BF16 = jnp.bfloat16


def tile_of(extent, most):
    tile = min(extent, most)
    while extent % tile:
        tile //= 2
    return tile


def copies(pairs, sem, chunks):
    started = []
    for n, (source, target) in enumerate(pairs):
        rows = source.shape[0] // chunks
        cut = [slice(c * rows, (c + 1) * rows) for c in range(chunks)]
        started.append(
            [pltpu.make_async_copy(source.at[r], target.at[r], sem.at[n, c]) for c, r in enumerate(cut)]
        )
    for array in started:
        for copy in array:
            copy.start()
    return started


def stage(arrays):
    count = len(arrays)

    def kernel(*refs):
        for array in copies(list(zip(refs[:count], refs[count:-1])), refs[-1], 2):
            for copy in array:
                copy.wait()

    return pl.pallas_call(
        kernel,
        out_shape=[pltpu.VMEM(a.shape, a.dtype) for a in arrays],
        in_specs=[pl.BlockSpec(memory_space=pltpu.HBM)] * count,
        out_specs=[VMEM] * count,
        scratch_shapes=[pltpu.SemaphoreType.DMA((count, 2))],
        compiler_params=pltpu.CompilerParams(vmem_limit_bytes=4 * MIB),
        cost_estimate=pl.CostEstimate(
            flops=0, bytes_accessed=sum(2 * a.size * a.dtype.itemsize for a in arrays), transcendentals=0
        ),
        name="stage",
    )(*[pltpu.with_memory_space_constraint(a, pltpu.HBM) for a in arrays])


def stage_in_section(arrays, wanted, held, after):
    count = len(arrays)

    def kernel(*refs):
        sources, targets, sem = refs[:count], refs[count + len(held) + len(after) : -1], refs[-1]

        @pl.when(wanted(lax.axis_index("pipe")))
        def _():
            for array in copies(list(zip(sources, targets)), sem, 2):
                for copy in array:
                    copy.wait()

    return pl.pallas_call(
        kernel,
        out_shape=[pltpu.VMEM(a.shape, a.dtype) for a in arrays],
        in_specs=[pl.BlockSpec(memory_space=pltpu.HBM)] * count
        + [VMEM] * len(held)
        + [pl.BlockSpec(memory_space=pl.ANY)] * len(after),
        out_specs=[VMEM] * count,
        input_output_aliases={count + n: n for n in range(len(held))},
        scratch_shapes=[pltpu.SemaphoreType.DMA((count, 2))],
        compiler_params=pltpu.CompilerParams(vmem_limit_bytes=4 * MIB),
        cost_estimate=CHEAP,
        name="stage_in_section",
    )(*[pltpu.with_memory_space_constraint(a, pltpu.HBM) for a in arrays], *held, *after)


def unit_grads(parts, share, rows_ref, down_ref, gate_ref, unit_ref):
    me = lax.axis_index("tensor")
    term = jnp.dot(rows_ref[...], down_ref[...], preferred_element_type=F32)
    for k in range(parts):
        at = pl.multiple_of(lax.rem(me + k, parts) * share, share)
        gates = gate_ref[pl.ds(at, share), :].astype(F32)
        unit_ref[k * share : (k + 1) * share, :] = (term[k * share : (k + 1) * share] * gates).astype(BF16)


def hand_out(share, term, cols, kept_ref, sent_refs):
    kept_ref[:, cols] = term[0:share]
    for k, ref in enumerate(sent_refs, 1):
        ref[:, cols] = term[k * share : (k + 1) * share].astype(BF16)


def fill_rows(share, rows_ref, own_ref, peer_refs):
    rows_ref[0:share, :] = own_ref[...]
    parts = rows_ref.shape[0] // share
    me = lax.axis_index("tensor")
    for k in range(1, parts):
        if peer_refs[0].shape[0] > share:
            at = pl.multiple_of(lax.rem(me + k, parts) * share, share)
            rows_ref[k * share : (k + 1) * share, :] = peer_refs[0][pl.ds(at, share), :]
        else:
            rows_ref[k * share : (k + 1) * share, :] = peer_refs[k - 1][...]


def step_kernel(layer, parts, pieces, own_ref, *refs):
    peer_refs, refs = refs[:pieces], refs[pieces:]
    down_ref, turned_ref, gate_ref, kept_ref = refs[:4]
    sent_refs = refs[4 : parts + 3]
    rows_ref, unit_ref = refs[parts + 3 :]
    share = own_ref.shape[0]

    @pl.when(lax.axis_index("pipe") == layer)
    def _():
        fill_rows(share, rows_ref, own_ref, peer_refs)
        unit_grads(parts, share, rows_ref, down_ref, gate_ref, unit_ref)
        term = jnp.dot(unit_ref[...], turned_ref[...], preferred_element_type=F32)
        hand_out(share, term, slice(None), kept_ref, sent_refs)


def unit_kernel(layer, parts, own_ref, *refs):
    peer_refs = refs[: parts - 1]
    down_ref, gate_ref, unit_ref, rows_ref = refs[parts - 1 :]
    share = own_ref.shape[0]

    @pl.when(lax.axis_index("pipe") == layer)
    def _():
        fill_rows(share, rows_ref, own_ref, peer_refs)
        unit_grads(parts, share, rows_ref, down_ref, gate_ref, unit_ref)


def unit_step(layer, own, peers, w_down, gates):
    parts = len(peers) + 1
    rows = own.shape[0] * parts
    return pl.pallas_call(
        functools.partial(unit_kernel, layer, parts),
        out_shape=jax.ShapeDtypeStruct((rows, w_down.shape[1]), BF16),
        in_specs=[VMEM] * (parts + 2),
        out_specs=VMEM,
        scratch_shapes=[pltpu.VMEM((rows, own.shape[1]), BF16)],
        compiler_params=pltpu.CompilerParams(vmem_limit_bytes=12 * MIB),
        cost_estimate=CHEAP,
        name="unit_step",
    )(own, *peers, w_down, gates)


def width_step(layer, unit_grad, turned, share, after):
    width = turned.shape[1]
    parts = unit_grad.shape[0] // share

    def kernel(unit_ref, turned_ref, *refs):
        kept_ref, *sent_refs = refs[len(after) :]

        @pl.when(lax.axis_index("pipe") == layer)
        def _():
            term = jnp.dot(unit_ref[...], turned_ref[...], preferred_element_type=F32)
            hand_out(share, term, slice(None), kept_ref, sent_refs)

    return pl.pallas_call(
        kernel,
        out_shape=[jax.ShapeDtypeStruct((share, width), F32)]
        + [jax.ShapeDtypeStruct((share, width), BF16)] * (parts - 1),
        in_specs=[VMEM, VMEM] + [pl.BlockSpec(memory_space=pl.ANY)] * len(after),
        out_specs=[VMEM] * parts,
        compiler_params=pltpu.CompilerParams(vmem_limit_bytes=12 * MIB),
        cost_estimate=CHEAP,
        name="width_step",
    )(unit_grad, turned, *after)


def first_kernel(layer, parts, pieces, further, own_ref, *refs):
    peer_refs, refs = refs[:pieces], refs[pieces:]
    down_ref, up_ref, gate_ref = refs[:3]
    count = 1 + max((n for n, _ in further), default=-1)
    source_refs, refs = refs[3 : 3 + count], refs[3 + count :]
    turned_ref, kept_ref = refs[:2]
    sent_refs = refs[2 : parts + 1]
    staged_refs = refs[parts + 1 : parts + 1 + len(further)]
    rows_ref, unit_ref, held_ref, sem, further_sem = refs[parts + 1 + len(further) :]
    share = own_ref.shape[0]
    chunks = sem.shape[1]
    size = held_ref.shape[0] // chunks
    (arriving,) = copies([(up_ref, held_ref)], sem, chunks)
    pairs = [(source_refs[n].at[rows], staged) for (n, rows), staged in zip(further, staged_refs)]
    behind = copies(pairs, further_sem, 1)
    starts = lax.axis_index("pipe") == layer

    def turn(first, count):
        for c in range(first, first + count):
            arriving[c].wait()
        cols = slice(first * size, (first + count) * size)
        turned_ref[:, cols] = held_ref[cols, :].T

    def product(first, count):
        cols = slice(first * size, (first + count) * size)
        term = jnp.dot(unit_ref[...], turned_ref[:, cols], preferred_element_type=F32)
        hand_out(share, term, cols, kept_ref, sent_refs)

    @pl.when(starts)
    def _():
        fill_rows(share, rows_ref, own_ref, peer_refs)
        unit_grads(parts, share, rows_ref, down_ref, gate_ref, unit_ref)
        turn(0, 2)
        for c in range(2, chunks, 2):
            turn(c, 2)
            product(c - 2, 2)
        product(chunks - 2, 2)

    @pl.when(jnp.logical_not(starts))
    def _():
        for c in range(chunks):
            turn(c, 1)

    for (copy,) in behind:
        copy.wait()


def first_step(layer, own, peers, w_down, w_up, gates, arrays, split):
    share, width = own.shape
    units = w_down.shape[1]
    parts = lax.axis_size("tensor")
    rows = share * parts
    further = [(n, slice(0, a.shape[0])) for n, a in enumerate(arrays)]
    for n, a in enumerate(split, len(arrays)):
        half = a.shape[0] // 2
        further += [(n, slice(0, half)), (n, slice(half, 2 * half))]
    sources = [*arrays, *split]
    hbm = pl.BlockSpec(memory_space=pltpu.HBM)
    outs = pl.pallas_call(
        functools.partial(first_kernel, layer, parts, len(peers), further),
        out_shape=[pltpu.VMEM((units, width), BF16), jax.ShapeDtypeStruct((share, width), F32)]
        + [jax.ShapeDtypeStruct((share, width), BF16)] * (parts - 1)
        + [pltpu.VMEM((rows.stop - rows.start, sources[n].shape[1]), BF16) for n, rows in further],
        in_specs=[VMEM] * (len(peers) + 2) + [hbm, VMEM] + [hbm] * len(sources),
        out_specs=[VMEM] * (1 + parts + len(further)),
        scratch_shapes=[
            pltpu.VMEM((rows, width), BF16),
            pltpu.VMEM((rows, units), BF16),
            pltpu.VMEM((width, units), BF16),
            pltpu.SemaphoreType.DMA((1, 8)),
            pltpu.SemaphoreType.DMA((len(further), 1)),
        ],
        compiler_params=pltpu.CompilerParams(vmem_limit_bytes=20 * MIB),
        cost_estimate=CHEAP,
        name="first_step",
    )(
        own,
        *peers,
        w_down,
        pltpu.with_memory_space_constraint(w_up, pltpu.HBM),
        gates,
        *[pltpu.with_memory_space_constraint(a, pltpu.HBM) for a in sources],
    )
    return outs[0], outs[1], outs[2 : parts + 1], outs[parts + 1 :]


def section_step(layer, own, peers, w_down, turned, gates, after=()):
    share, width = own.shape
    units = w_down.shape[1]
    pieces = len(peers)
    parts = lax.axis_size("tensor")
    rows = share * parts

    def kernel(*refs):
        step_kernel(layer, parts, pieces, *refs[: pieces + 4], *refs[pieces + 4 + len(after) :])

    return pl.pallas_call(
        kernel,
        out_shape=[jax.ShapeDtypeStruct((share, width), F32)]
        + [jax.ShapeDtypeStruct((share, width), BF16)] * (parts - 1),
        in_specs=[VMEM] * (pieces + 4) + [pl.BlockSpec(memory_space=pl.ANY)] * len(after),
        out_specs=[VMEM] * parts,
        scratch_shapes=[pltpu.VMEM((rows, width), BF16), pltpu.VMEM((rows, units), BF16)],
        compiler_params=pltpu.CompilerParams(vmem_limit_bytes=12 * MIB),
        cost_estimate=CHEAP,
        name="section_step",
    )(own, *peers, w_down, turned, gates, *after)


def pack_block(source, k, target, at):
    owners = lax.axis_size("dp")
    tokens, width = source.shape
    size = width // owners
    rows = tokens * size // target.shape[1]
    column = pl.multiple_of((lax.axis_index("dp") ^ k) * size, size)
    for q in range(tokens // rows):
        target[at : at + rows, q * size : (q + 1) * size] = source[
            q * rows : (q + 1) * rows, pl.ds(column, size)
        ]
    return rows


def norm_kernel(layer, parts, earlier, owners, passed, handed, kept_ref, *refs):
    arrived = refs[: parts - 1]
    up_ref, in_ref, gain_ref = refs[parts - 1 : parts + 2]
    refs = refs[parts + 2 :]
    earlier_refs, refs = refs[:earlier], refs[earlier:]
    first_ref, pass_refs, refs = refs[0], refs[1 : 1 + passed], refs[1 + passed :]
    out_ref, block_refs, handed_refs = refs[0], refs[1 : len(refs) - len(handed)], refs[len(refs) - len(handed) :]
    segment = lax.axis_index("pipe")

    def cut(source):
        size = source.shape[1] // owners
        for k, ref in enumerate(block_refs, 1):
            at = pl.multiple_of((lax.axis_index("dp") ^ k) * size, size)
            ref[...] = source[:, pl.ds(at, size)]

    @pl.when(segment == layer)
    def _():
        normed = kept_ref[...]
        for ref in arrived:
            normed = normed + ref[...].astype(F32)
        rows_in = in_ref[...].astype(F32)
        inverse_rms = lax.rsqrt(jnp.mean(rows_in * rows_in, axis=-1, keepdims=True) + EPS_NORM)
        scaled = normed * gain_ref[...]
        mean_term = jnp.mean(rows_in * scaled, axis=-1, keepdims=True)
        out_ref[...] = (
            up_ref[...].astype(F32)
            + inverse_rms * scaled
            - rows_in * (inverse_rms * inverse_rms * inverse_rms * mean_term)
        ).astype(BF16)
        cut(out_ref)

    for above, ref in enumerate(earlier_refs):

        @pl.when(segment == layer + earlier - above)
        def _(ref=ref):
            cut(ref)
            if layer == 0:
                out_ref[...] = ref[...]

    sources = iter(pass_refs)
    for recipe, target in zip(handed, handed_refs):
        at = 0
        for piece in recipe:
            if isinstance(piece, int):
                at += pack_block(first_ref, piece, target, at)
            else:
                start, rows = piece
                target[at : at + rows, :] = next(sources)[start : start + rows, :]
                at += rows


def norm_step(layer, kept, arrived, upstream, rows_in, gain, first, earlier=(), owners=1, passed=()):
    parts = len(arrived) + 1
    share, width = upstream.shape
    block = jax.ShapeDtypeStruct((share, width // owners), BF16)
    recipes = [[p if isinstance(p, int) else p[1:] for p in group] for group in passed]
    handed = []
    for group in passed:
        units = passed[0][0][0].shape[1]
        block_rows = share * (width // lax.axis_size("dp")) // units
        rows = sum(block_rows if isinstance(p, int) else p[2] for p in group)
        handed.append(jax.ShapeDtypeStruct((rows, units), BF16))
    passed = [p[0] for group in passed for p in group if not isinstance(p, int)]
    outs = pl.pallas_call(
        functools.partial(norm_kernel, layer, parts, len(earlier), owners, len(passed), recipes),
        out_shape=[jax.ShapeDtypeStruct(upstream.shape, BF16)]
        + [block] * (owners - 1)
        + handed,
        in_specs=[VMEM] * (parts + 4 + len(earlier) + len(passed)),
        out_specs=[VMEM] * (owners + len(handed)),
        compiler_params=pltpu.CompilerParams(vmem_limit_bytes=8 * MIB),
        cost_estimate=CHEAP,
        name="norm_step",
    )(kept, *arrived, upstream, rows_in, gain, *earlier, first, *passed)
    return outs[0], outs[1:owners], outs[owners:]


def collect(upstreams, blocks, packed, after):
    sections = len(upstreams)
    owners = len(blocks) + 1
    share, size = blocks[0].shape
    count = sections + 2 * len(blocks)

    def kernel(*refs):
        block_refs = refs[: owners - 1][::-1]
        refs = [*refs[owners - 1 : owners - 1 + sections], *block_refs, *refs[owners - 1 + sections :]]
        out_ref = refs[-1]
        segment = lax.axis_index("pipe")
        at = pl.multiple_of(lax.axis_index("dp") * size, size)
        for s in range(sections):

            @pl.when(segment == sections - 1 - s)
            def _(s=s):
                out_ref[0:share, :] = refs[s][:, pl.ds(at, size)]

        @pl.when(segment < sections - 1)
        def _():
            for k in range(1, owners):
                out_ref[k * share : (k + 1) * share, :] = refs[sections + k - 1][...]

        @pl.when(segment == sections - 1)
        def _():
            for k in range(1, owners):
                source, start = refs[sections + owners + k - 2], packed[k - 1][1]
                pieces = source.shape[1] // size
                rows = share // pieces
                for q in range(pieces):
                    out_ref[k * share + q * rows : k * share + (q + 1) * rows, :] = source[
                        start : start + rows, q * size : (q + 1) * size
                    ]

    return pl.pallas_call(
        kernel,
        out_shape=jax.ShapeDtypeStruct((owners * share, size), BF16),
        in_specs=[VMEM] * count + [pl.BlockSpec(memory_space=pl.ANY)] * len(after),
        out_specs=VMEM,
        compiler_params=pltpu.CompilerParams(vmem_limit_bytes=4 * MIB),
        cost_estimate=CHEAP,
        name="collect",
    )(*blocks[::-1], *upstreams, *[array for array, _ in packed], *after)


def adam_update(gradient, current, moment_one, moment_two):
    first = BETA_ONE * moment_one + (1.0 - BETA_ONE) * gradient
    second = BETA_TWO * moment_two + (1.0 - BETA_TWO) * gradient * gradient
    root = second * lax.rsqrt(second)
    scale = math.sqrt(CORRECT_TWO)
    step = (first * (RATE * scale / CORRECT_ONE)) / (root + EPS_ADAM * scale)
    return first, second, (1.0 - RATE * DECAY) * current - step


def adam_kernel(sizes, *refs):
    owners, parts, share, tile, part_rows = sizes
    up_refs = refs[:parts]
    refs = refs[parts:]
    done_ref, hidden_ref, down_ref, one_ref, two_ref = refs[:5]
    outs, done_out = refs[5:8], refs[8]
    rows_ref, *results, sem, done_sem = refs[9:]
    writing = pltpu.make_async_copy(done_ref, done_out, done_sem)
    writing.start()
    rows = rows_ref.shape[1]
    me = lax.axis_index("dp")
    part = lax.axis_index("tensor")
    for p in range(parts):
        for k in range(owners):
            at = k * parts + lax.rem(part + p, parts)
            rows_ref[pl.ds(pl.multiple_of(at * share, share), share), :] = up_refs[p][
                k * share : (k + 1) * share, :
            ]
    writes = []
    for i in range(rows // tile):
        turned = rows_ref[:, i * tile : (i + 1) * tile].T
        gradient = jnp.dot(turned, hidden_ref[...], preferred_element_type=F32)
        for j in range(tile // part_rows):
            at = i * tile + j * part_rows
            cut = slice(at, at + part_rows)
            current = down_ref[pl.ds(pl.multiple_of(me * rows + at, part_rows), part_rows), :].astype(F32)
            updates = adam_update(
                gradient[j * part_rows : (j + 1) * part_rows], current, one_ref[cut, :], two_ref[cut, :]
            )
            for q, update in enumerate(updates):
                results[q][cut, :] = update
                writes.append(
                    pltpu.make_async_copy(results[q].at[cut], outs[q].at[cut], sem.at[at // part_rows, q])
                )
                writes[-1].start()
    for write in writes:
        write.wait()
    writing.wait()


def adam_step(blocks, done, hidden_all, w_down, moment_one, moment_two, owners, parts):
    rows, units = moment_one.shape
    tokens = hidden_all.shape[0]
    tile = tile_of(rows, 128)
    part_rows = tile_of(tile, 64)
    return pl.pallas_call(
        functools.partial(adam_kernel, (owners, parts, blocks[0].shape[0] // owners, tile, part_rows)),
        out_shape=[jax.ShapeDtypeStruct((rows, units), F32)] * 3
        + [jax.ShapeDtypeStruct(done.shape, done.dtype)],
        in_specs=[VMEM] * (len(blocks) + 5),
        out_specs=[pl.BlockSpec(memory_space=pl.ANY)] * 4,
        scratch_shapes=[pltpu.VMEM((tokens, rows), BF16)]
        + [pltpu.VMEM((rows, units), F32)] * 3
        + [pltpu.SemaphoreType.DMA((rows // part_rows, 3)), pltpu.SemaphoreType.DMA(())],
        compiler_params=pltpu.CompilerParams(vmem_limit_bytes=18 * MIB),
        cost_estimate=CHEAP,
        name="adam_step",
    )(*blocks, done, hidden_all, w_down, moment_one, moment_two)


def stack(order):
    count = len(order)
    total = sum(rows for _, _, rows in order)

    def kernel(*refs):
        out, sem = refs[-2:]
        started = []
        place = 0
        for n, (_, at, rows) in enumerate(order):
            started.append(
                pltpu.make_async_copy(
                    refs[n].at[at : at + rows], out.at[place : place + rows], sem.at[n]
                )
            )
            place += rows
        for copy in started:
            copy.start()
        for copy in started:
            copy.wait()

    return pl.pallas_call(
        kernel,
        out_shape=pltpu.VMEM((total, order[0][0].shape[1]), BF16),
        in_specs=[pl.BlockSpec(memory_space=pl.ANY)] * count,
        out_specs=VMEM,
        scratch_shapes=[pltpu.SemaphoreType.DMA((count,))],
        compiler_params=pltpu.CompilerParams(vmem_limit_bytes=4 * MIB),
        cost_estimate=CHEAP,
        name="stack",
    )(*[array for array, _, _ in order])


def adam_general(upstreams, hidden_all, w_down, moment_one, moment_two):
    owners = lax.axis_size("dp")
    sections = len(upstreams)
    segment = lax.axis_index("pipe")
    own = upstreams[0]
    for s in range(1, sections):
        own = jnp.where(segment == sections - 1 - s, upstreams[s], own)
    mine = lax.all_to_all(own, "dp", split_axis=1, concat_axis=0, tiled=True)
    share, rows = own.shape[0], mine.shape[1]
    turned = lax.all_gather(mine.reshape(owners, share, rows), "tensor", axis=1, tiled=True)
    gradient = lax.dot_general(
        turned.reshape(-1, rows), hidden_all, (((0,), (0,)), ((), ())), preferred_element_type=F32
    )
    at = lax.axis_index("dp") * rows
    current = lax.dynamic_slice_in_dim(w_down, at, rows, 0).astype(F32)
    return adam_update(gradient, current, moment_one, moment_two)


def from_peers(value, axis):
    size = lax.axis_size(axis)
    return [lax.ppermute(value, axis, [((i + k) % size, i) for i in range(size)]) for k in range(1, size)]


def to_peers(values, axis):
    size = lax.axis_size(axis)
    return [
        lax.ppermute(value, axis, [(i, (i + k) % size) for i in range(size)])
        for k, value in enumerate(values, 1)
    ]


def on_device(
    up_weight,
    down_weight,
    gate_act,
    hidden,
    block_input,
    norm_gain,
    loss_grad,
    moment_one,
    moment_two,
):
    sections = lax.axis_size("pipe")
    owners = lax.axis_size("dp")
    parts = lax.axis_size("tensor")
    width, units = down_weight.shape[1:]
    planned = sections == 4 and owners == 4 and width % (128 * owners) == 0 and units % (width // owners) == 0
    planned = planned and loss_grad.shape[0] * (width // owners) % (16 * units) == 0 and parts == 2
    share = loss_grad.shape[0]
    saved = hidden[0]
    half = saved.shape[0] // 2
    w_down, gates, loss = stage([down_weight[0], gate_act[0], loss_grad])
    turned = None
    upstreams = [loss]
    grads = []
    late = ()
    for layer in reversed(range(sections)):
        upstream = upstreams[-1]
        if planned and not layer:
            peers = [lax.all_gather(upstream, "tensor", axis=0, tiled=True)]
        else:
            peers = from_peers(upstream if grads else loss_grad, "tensor")
        if not grads:
            turned, kept, sent, (rows_in, *halves) = first_step(
                layer,
                upstream,
                peers,
                w_down,
                up_weight[0],
                gates,
                [block_input[0]],
                [saved] if planned else [],
            )
        elif planned and layer:
            unit_grad = unit_step(layer, upstream, peers, w_down, gates)
            kept, *sent = width_step(layer, unit_grad, turned, loss_grad.shape[0], late)
        else:
            kept, *sent = section_step(layer, upstream, peers, w_down, turned, gates, after=late)
        if planned and not layer:
            hidden_all = stack(
                [
                    (halves[0], 0, half),
                    (halves[1], 0, half),
                    (along_upper, 0, half),
                    (along_rest, 0, half),
                    (side_rest, 0, half),
                    (side_lower, 0, half),
                    (side_rest, half, half),
                    (along_rest, half, half),
                ]
            )
            packed = [(along_upper, half), (side_lower, half), (corner, 0)]
            own = collect(upstreams, blocks, packed, [kept, hidden_all])
        arrived = to_peers(sent, "tensor")
        window = len(grads)
        moving = ()
        if planned and window == 0:
            moving = [[(halves[0], 0, half), 1], [(halves[1], 0, half), 2]]
        elif planned and window == 1:
            moving = [
                [(halves[1], 0, half), (side_lower, 0, half)],
                [(halves[0], 0, half), (along_upper, 0, half)],
                [3],
            ]
        grad, cuts, handed = norm_step(
            layer,
            kept,
            arrived,
            upstream,
            rows_in,
            norm_gain,
            loss,
            earlier=grads if window >= sections - 2 else (),
            owners=owners if planned and window == 2 else 1,
            passed=moving,
        )
        grads.append(grad)
        if layer:
            upstreams.append(lax.ppermute(grad, "pipe", [(layer, layer - 1)]))
        if planned and layer:
            if window == 2:
                blocks = [
                    lax.ppermute(
                        cut,
                        ("pipe", "dp"),
                        [
                            (s * owners + i, (s - 1) * owners + (i ^ k))
                            for s in range(1, sections)
                            for i in range(owners)
                        ],
                    )
                    for k, cut in enumerate(cuts, 1)
                ]
            if window < 2:
                exchange = [
                    lax.ppermute(piece, "dp", [(i, i ^ k) for i in range(owners)])
                    for k, piece in enumerate(handed[:2], 1)
                ]
            if window == 0:
                along_upper, side_lower = exchange
                moments = stage_in_section(
                    [moment_one[0], moment_two[0]], lambda section: section != sections - 2, (), [grad]
                )
                late = [*exchange, *moments]
            elif window == 1:
                along_rest, side_rest = exchange
                start = (sections - 1) * owners
                corner = lax.ppermute(
                    handed[2], ("pipe", "dp"), [(start + i, start + (i ^ 3)) for i in range(owners)]
                )
                moments = stage_in_section(
                    [moment_one[0], moment_two[0]], lambda section: section == sections - 2, moments, [grad]
                )
                late = [*exchange, *moments]
            else:
                late = ()
    if planned:
        first, second, updated, grads[-1] = adam_step(
            [own, *from_peers(own, "tensor")], grads[-1], hidden_all, w_down, *moments, owners, parts
        )
    else:
        hidden_all = lax.all_gather(saved, "dp", axis=0, tiled=True)
        first, second, updated = adam_general(
            upstreams, hidden_all, w_down, moment_one[0], moment_two[0]
        )
    return (grads[-1][None], first[None], second[None], updated[None])


def solution(mesh):
    in_specs = (
        P("pipe", None, "tensor"),
        P("pipe", None, "tensor"),
        P("pipe", "dp", "tensor"),
        P("pipe", "dp", "tensor"),
        P("pipe", ("dp", "tensor"), None),
        P("pipe", None),
        P(("dp", "tensor"), None),
        P("pipe", "dp", "tensor"),
        P("pipe", "dp", "tensor"),
    )
    out_specs = (
        P("pipe", ("dp", "tensor"), None),
        P("pipe", "dp", "tensor"),
        P("pipe", "dp", "tensor"),
        P("pipe", "dp", "tensor"),
    )
    return jax.shard_map(
        on_device, mesh=mesh, in_specs=in_specs, out_specs=out_specs, check_vma=False
    )
```

```python
import functools
import math
import jax
import jax.numpy as jnp
from jax import lax
from jax.experimental import pallas as pl
from jax.experimental.pallas import tpu as pltpu
from jax.sharding import PartitionSpec as P

EPS_NORM = 1e-05
EPS_ADAM = 1e-08
BETA_ONE = 0.9
BETA_TWO = 0.95
RATE = 0.01
DECAY = 0.1
CORRECT_ONE = 1.0 - 0.9**10
CORRECT_TWO = 1.0 - 0.95**10

MIB = 2**20
VMEM = pl.BlockSpec(memory_space=pltpu.VMEM)
CHEAP = pl.CostEstimate(flops=0, bytes_accessed=0, transcendentals=0)
F32 = jnp.float32
BF16 = jnp.bfloat16


def tile_of(extent, most):
    tile = min(extent, most)
    while extent % tile:
        tile //= 2
    return tile


def copies(pairs, sem, chunks):
    started = []
    for n, (source, target) in enumerate(pairs):
        rows = source.shape[0] // chunks
        cut = [slice(c * rows, (c + 1) * rows) for c in range(chunks)]
        started.append(
            [pltpu.make_async_copy(source.at[r], target.at[r], sem.at[n, c]) for c, r in enumerate(cut)]
        )
    for array in started:
        for copy in array:
            copy.start()
    return started


def stage(arrays):
    count = len(arrays)

    def kernel(*refs):
        for array in copies(list(zip(refs[:count], refs[count:-1])), refs[-1], 2):
            for copy in array:
                copy.wait()

    return pl.pallas_call(
        kernel,
        out_shape=[pltpu.VMEM(a.shape, a.dtype) for a in arrays],
        in_specs=[pl.BlockSpec(memory_space=pltpu.HBM)] * count,
        out_specs=[VMEM] * count,
        scratch_shapes=[pltpu.SemaphoreType.DMA((count, 2))],
        compiler_params=pltpu.CompilerParams(vmem_limit_bytes=4 * MIB),
        cost_estimate=pl.CostEstimate(
            flops=0, bytes_accessed=sum(2 * a.size * a.dtype.itemsize for a in arrays), transcendentals=0
        ),
        name="stage",
    )(*[pltpu.with_memory_space_constraint(a, pltpu.HBM) for a in arrays])


def stage_in_section(arrays, wanted, held, after):
    count = len(arrays)

    def kernel(*refs):
        sources, targets, sem = refs[:count], refs[count + len(held) + len(after) : -1], refs[-1]

        @pl.when(wanted(lax.axis_index("pipe")))
        def _():
            for array in copies(list(zip(sources, targets)), sem, 2):
                for copy in array:
                    copy.wait()

    return pl.pallas_call(
        kernel,
        out_shape=[pltpu.VMEM(a.shape, a.dtype) for a in arrays],
        in_specs=[pl.BlockSpec(memory_space=pltpu.HBM)] * count
        + [VMEM] * len(held)
        + [pl.BlockSpec(memory_space=pl.ANY)] * len(after),
        out_specs=[VMEM] * count,
        input_output_aliases={count + n: n for n in range(len(held))},
        scratch_shapes=[pltpu.SemaphoreType.DMA((count, 2))],
        compiler_params=pltpu.CompilerParams(vmem_limit_bytes=4 * MIB),
        cost_estimate=CHEAP,
        name="stage_in_section",
    )(*[pltpu.with_memory_space_constraint(a, pltpu.HBM) for a in arrays], *held, *after)


def unit_grads(parts, share, rows_ref, down_ref, gate_ref, unit_ref):
    me = lax.axis_index("tensor")
    term = jnp.dot(rows_ref[...], down_ref[...], preferred_element_type=F32)
    for k in range(parts):
        at = pl.multiple_of(lax.rem(me + k, parts) * share, share)
        gates = gate_ref[pl.ds(at, share), :].astype(F32)
        unit_ref[k * share : (k + 1) * share, :] = (term[k * share : (k + 1) * share] * gates).astype(BF16)


def hand_out(share, term, cols, kept_ref, sent_refs):
    kept_ref[:, cols] = term[0:share]
    for k, ref in enumerate(sent_refs, 1):
        ref[:, cols] = term[k * share : (k + 1) * share].astype(BF16)


def fill_rows(share, rows_ref, own_ref, peer_refs):
    rows_ref[0:share, :] = own_ref[...]
    parts = rows_ref.shape[0] // share
    me = lax.axis_index("tensor")
    for k in range(1, parts):
        if peer_refs[0].shape[0] > share:
            at = pl.multiple_of(lax.rem(me + k, parts) * share, share)
            rows_ref[k * share : (k + 1) * share, :] = peer_refs[0][pl.ds(at, share), :]
        else:
            rows_ref[k * share : (k + 1) * share, :] = peer_refs[k - 1][...]


def step_kernel(layer, parts, pieces, own_ref, *refs):
    peer_refs, refs = refs[:pieces], refs[pieces:]
    down_ref, turned_ref, gate_ref, kept_ref = refs[:4]
    sent_refs = refs[4 : parts + 3]
    rows_ref, unit_ref = refs[parts + 3 :]
    share = own_ref.shape[0]

    @pl.when(lax.axis_index("pipe") == layer)
    def _():
        fill_rows(share, rows_ref, own_ref, peer_refs)
        unit_grads(parts, share, rows_ref, down_ref, gate_ref, unit_ref)
        term = jnp.dot(unit_ref[...], turned_ref[...], preferred_element_type=F32)
        hand_out(share, term, slice(None), kept_ref, sent_refs)


def unit_kernel(layer, parts, own_ref, *refs):
    peer_refs = refs[: parts - 1]
    down_ref, gate_ref, unit_ref, rows_ref = refs[parts - 1 :]
    share = own_ref.shape[0]

    @pl.when(lax.axis_index("pipe") == layer)
    def _():
        fill_rows(share, rows_ref, own_ref, peer_refs)
        unit_grads(parts, share, rows_ref, down_ref, gate_ref, unit_ref)


def unit_step(layer, own, peers, w_down, gates):
    parts = len(peers) + 1
    rows = own.shape[0] * parts
    return pl.pallas_call(
        functools.partial(unit_kernel, layer, parts),
        out_shape=jax.ShapeDtypeStruct((rows, w_down.shape[1]), BF16),
        in_specs=[VMEM] * (parts + 2),
        out_specs=VMEM,
        scratch_shapes=[pltpu.VMEM((rows, own.shape[1]), BF16)],
        compiler_params=pltpu.CompilerParams(vmem_limit_bytes=12 * MIB),
        cost_estimate=CHEAP,
        name="unit_step",
    )(own, *peers, w_down, gates)


def width_step(layer, unit_grad, turned, share, after):
    width = turned.shape[1]
    parts = unit_grad.shape[0] // share

    def kernel(unit_ref, turned_ref, *refs):
        kept_ref, *sent_refs = refs[len(after) :]

        @pl.when(lax.axis_index("pipe") == layer)
        def _():
            term = jnp.dot(unit_ref[...], turned_ref[...], preferred_element_type=F32)
            hand_out(share, term, slice(None), kept_ref, sent_refs)

    return pl.pallas_call(
        kernel,
        out_shape=[jax.ShapeDtypeStruct((share, width), F32)]
        + [jax.ShapeDtypeStruct((share, width), BF16)] * (parts - 1),
        in_specs=[VMEM, VMEM] + [pl.BlockSpec(memory_space=pl.ANY)] * len(after),
        out_specs=[VMEM] * parts,
        compiler_params=pltpu.CompilerParams(vmem_limit_bytes=12 * MIB),
        cost_estimate=CHEAP,
        name="width_step",
    )(unit_grad, turned, *after)


def first_kernel(layer, parts, pieces, further, own_ref, *refs):
    peer_refs, refs = refs[:pieces], refs[pieces:]
    down_ref, up_ref, gate_ref = refs[:3]
    count = 1 + max((n for n, _ in further), default=-1)
    source_refs, refs = refs[3 : 3 + count], refs[3 + count :]
    turned_ref, kept_ref = refs[:2]
    sent_refs = refs[2 : parts + 1]
    staged_refs = refs[parts + 1 : parts + 1 + len(further)]
    rows_ref, unit_ref, held_ref, sem, further_sem = refs[parts + 1 + len(further) :]
    share = own_ref.shape[0]
    chunks = sem.shape[1]
    size = held_ref.shape[0] // chunks
    (arriving,) = copies([(up_ref, held_ref)], sem, chunks)
    pairs = [(source_refs[n].at[rows], staged) for (n, rows), staged in zip(further, staged_refs)]
    behind = copies(pairs, further_sem, 1)
    starts = lax.axis_index("pipe") == layer

    def turn(first, count):
        for c in range(first, first + count):
            arriving[c].wait()
        cols = slice(first * size, (first + count) * size)
        turned_ref[:, cols] = held_ref[cols, :].T

    def product(first, count):
        cols = slice(first * size, (first + count) * size)
        term = jnp.dot(unit_ref[...], turned_ref[:, cols], preferred_element_type=F32)
        hand_out(share, term, cols, kept_ref, sent_refs)

    @pl.when(starts)
    def _():
        fill_rows(share, rows_ref, own_ref, peer_refs)
        unit_grads(parts, share, rows_ref, down_ref, gate_ref, unit_ref)
        turn(0, 2)
        for c in range(2, chunks, 2):
            turn(c, 2)
            product(c - 2, 2)
        product(chunks - 2, 2)

    @pl.when(jnp.logical_not(starts))
    def _():
        for c in range(chunks):
            turn(c, 1)

    for (copy,) in behind:
        copy.wait()


def first_step(layer, own, peers, w_down, w_up, gates, arrays, split):
    share, width = own.shape
    units = w_down.shape[1]
    parts = lax.axis_size("tensor")
    rows = share * parts
    further = [(n, slice(0, a.shape[0])) for n, a in enumerate(arrays)]
    for n, a in enumerate(split, len(arrays)):
        half = a.shape[0] // 2
        further += [(n, slice(0, half)), (n, slice(half, 2 * half))]
    sources = [*arrays, *split]
    hbm = pl.BlockSpec(memory_space=pltpu.HBM)
    outs = pl.pallas_call(
        functools.partial(first_kernel, layer, parts, len(peers), further),
        out_shape=[pltpu.VMEM((units, width), BF16), jax.ShapeDtypeStruct((share, width), F32)]
        + [jax.ShapeDtypeStruct((share, width), BF16)] * (parts - 1)
        + [pltpu.VMEM((rows.stop - rows.start, sources[n].shape[1]), BF16) for n, rows in further],
        in_specs=[VMEM] * (len(peers) + 2) + [hbm, VMEM] + [hbm] * len(sources),
        out_specs=[VMEM] * (1 + parts + len(further)),
        scratch_shapes=[
            pltpu.VMEM((rows, width), BF16),
            pltpu.VMEM((rows, units), BF16),
            pltpu.VMEM((width, units), BF16),
            pltpu.SemaphoreType.DMA((1, 8)),
            pltpu.SemaphoreType.DMA((len(further), 1)),
        ],
        compiler_params=pltpu.CompilerParams(vmem_limit_bytes=20 * MIB),
        cost_estimate=CHEAP,
        name="first_step",
    )(
        own,
        *peers,
        w_down,
        pltpu.with_memory_space_constraint(w_up, pltpu.HBM),
        gates,
        *[pltpu.with_memory_space_constraint(a, pltpu.HBM) for a in sources],
    )
    return outs[0], outs[1], outs[2 : parts + 1], outs[parts + 1 :]


def section_step(layer, own, peers, w_down, turned, gates, after=()):
    share, width = own.shape
    units = w_down.shape[1]
    pieces = len(peers)
    parts = lax.axis_size("tensor")
    rows = share * parts

    def kernel(*refs):
        step_kernel(layer, parts, pieces, *refs[: pieces + 4], *refs[pieces + 4 + len(after) :])

    return pl.pallas_call(
        kernel,
        out_shape=[jax.ShapeDtypeStruct((share, width), F32)]
        + [jax.ShapeDtypeStruct((share, width), BF16)] * (parts - 1),
        in_specs=[VMEM] * (pieces + 4) + [pl.BlockSpec(memory_space=pl.ANY)] * len(after),
        out_specs=[VMEM] * parts,
        scratch_shapes=[pltpu.VMEM((rows, width), BF16), pltpu.VMEM((rows, units), BF16)],
        compiler_params=pltpu.CompilerParams(vmem_limit_bytes=12 * MIB),
        cost_estimate=CHEAP,
        name="section_step",
    )(own, *peers, w_down, turned, gates, *after)


def pack_block(source, k, target, at):
    owners = lax.axis_size("dp")
    tokens, width = source.shape
    size = width // owners
    rows = tokens * size // target.shape[1]
    column = pl.multiple_of((lax.axis_index("dp") ^ k) * size, size)
    for q in range(tokens // rows):
        target[at : at + rows, q * size : (q + 1) * size] = source[
            q * rows : (q + 1) * rows, pl.ds(column, size)
        ]
    return rows


def norm_kernel(layer, parts, earlier, owners, passed, handed, kept_ref, *refs):
    arrived = refs[: parts - 1]
    up_ref, in_ref, gain_ref = refs[parts - 1 : parts + 2]
    refs = refs[parts + 2 :]
    earlier_refs, refs = refs[:earlier], refs[earlier:]
    first_ref, pass_refs, refs = refs[0], refs[1 : 1 + passed], refs[1 + passed :]
    out_ref, block_refs, handed_refs = refs[0], refs[1 : len(refs) - len(handed)], refs[len(refs) - len(handed) :]
    segment = lax.axis_index("pipe")

    def cut(source):
        size = source.shape[1] // owners
        for k, ref in enumerate(block_refs, 1):
            at = pl.multiple_of((lax.axis_index("dp") ^ k) * size, size)
            ref[...] = source[:, pl.ds(at, size)]

    @pl.when(segment == layer)
    def _():
        normed = kept_ref[...]
        for ref in arrived:
            normed = normed + ref[...].astype(F32)
        rows_in = in_ref[...].astype(F32)
        inverse_rms = lax.rsqrt(jnp.mean(rows_in * rows_in, axis=-1, keepdims=True) + EPS_NORM)
        scaled = normed * gain_ref[...]
        mean_term = jnp.mean(rows_in * scaled, axis=-1, keepdims=True)
        out_ref[...] = (
            up_ref[...].astype(F32)
            + inverse_rms * scaled
            - rows_in * (inverse_rms * inverse_rms * inverse_rms * mean_term)
        ).astype(BF16)
        cut(out_ref)

    for above, ref in enumerate(earlier_refs):

        @pl.when(segment == layer + earlier - above)
        def _(ref=ref):
            cut(ref)
            if layer == 0:
                out_ref[...] = ref[...]

    sources = iter(pass_refs)
    for recipe, target in zip(handed, handed_refs):
        at = 0
        for piece in recipe:
            if isinstance(piece, int):
                at += pack_block(first_ref, piece, target, at)
            else:
                start, rows = piece
                target[at : at + rows, :] = next(sources)[start : start + rows, :]
                at += rows


def norm_step(layer, kept, arrived, upstream, rows_in, gain, first, earlier=(), owners=1, passed=()):
    parts = len(arrived) + 1
    share, width = upstream.shape
    block = jax.ShapeDtypeStruct((share, width // owners), BF16)
    recipes = [[p if isinstance(p, int) else p[1:] for p in group] for group in passed]
    handed = []
    for group in passed:
        units = passed[0][0][0].shape[1]
        block_rows = share * (width // lax.axis_size("dp")) // units
        rows = sum(block_rows if isinstance(p, int) else p[2] for p in group)
        handed.append(jax.ShapeDtypeStruct((rows, units), BF16))
    passed = [p[0] for group in passed for p in group if not isinstance(p, int)]
    outs = pl.pallas_call(
        functools.partial(norm_kernel, layer, parts, len(earlier), owners, len(passed), recipes),
        out_shape=[jax.ShapeDtypeStruct(upstream.shape, BF16)]
        + [block] * (owners - 1)
        + handed,
        in_specs=[VMEM] * (parts + 4 + len(earlier) + len(passed)),
        out_specs=[VMEM] * (owners + len(handed)),
        compiler_params=pltpu.CompilerParams(vmem_limit_bytes=8 * MIB),
        cost_estimate=CHEAP,
        name="norm_step",
    )(kept, *arrived, upstream, rows_in, gain, *earlier, first, *passed)
    return outs[0], outs[1:owners], outs[owners:]


def collect(upstreams, blocks, packed, after):
    sections = len(upstreams)
    owners = len(blocks) + 1
    share, size = blocks[0].shape
    count = sections + 2 * len(blocks)

    def kernel(*refs):
        block_refs = refs[: owners - 1][::-1]
        refs = [*refs[owners - 1 : owners - 1 + sections], *block_refs, *refs[owners - 1 + sections :]]
        out_ref = refs[-1]
        segment = lax.axis_index("pipe")
        at = pl.multiple_of(lax.axis_index("dp") * size, size)
        for s in range(sections):

            @pl.when(segment == sections - 1 - s)
            def _(s=s):
                out_ref[0:share, :] = refs[s][:, pl.ds(at, size)]

        @pl.when(segment < sections - 1)
        def _():
            for k in range(1, owners):
                out_ref[k * share : (k + 1) * share, :] = refs[sections + k - 1][...]

        @pl.when(segment == sections - 1)
        def _():
            for k in range(1, owners):
                source, start = refs[sections + owners + k - 2], packed[k - 1][1]
                pieces = source.shape[1] // size
                rows = share // pieces
                for q in range(pieces):
                    out_ref[k * share + q * rows : k * share + (q + 1) * rows, :] = source[
                        start : start + rows, q * size : (q + 1) * size
                    ]

    return pl.pallas_call(
        kernel,
        out_shape=jax.ShapeDtypeStruct((owners * share, size), BF16),
        in_specs=[VMEM] * count + [pl.BlockSpec(memory_space=pl.ANY)] * len(after),
        out_specs=VMEM,
        compiler_params=pltpu.CompilerParams(vmem_limit_bytes=4 * MIB),
        cost_estimate=CHEAP,
        name="collect",
    )(*blocks[::-1], *upstreams, *[array for array, _ in packed], *after)


def adam_update(gradient, current, moment_one, moment_two):
    first = BETA_ONE * moment_one + (1.0 - BETA_ONE) * gradient
    second = BETA_TWO * moment_two + (1.0 - BETA_TWO) * gradient * gradient
    root = second * lax.rsqrt(second)
    scale = math.sqrt(CORRECT_TWO)
    step = (first * (RATE * scale / CORRECT_ONE)) / (root + EPS_ADAM * scale)
    return first, second, (1.0 - RATE * DECAY) * current - step


def adam_kernel(sizes, *refs):
    owners, parts, share, tile, part_rows = sizes
    up_refs = refs[:parts]
    refs = refs[parts:]
    done_ref, hidden_ref, down_ref, one_ref, two_ref = refs[:5]
    outs, done_out = refs[5:8], refs[8]
    rows_ref, *results, sem, done_sem = refs[9:]
    writing = pltpu.make_async_copy(done_ref, done_out, done_sem)
    writing.start()
    rows = rows_ref.shape[1]
    me = lax.axis_index("dp")
    part = lax.axis_index("tensor")
    for p in range(parts):
        for k in range(owners):
            at = k * parts + lax.rem(part + p, parts)
            rows_ref[pl.ds(pl.multiple_of(at * share, share), share), :] = up_refs[p][
                k * share : (k + 1) * share, :
            ]
    writes = []
    for i in range(rows // tile):
        turned = rows_ref[:, i * tile : (i + 1) * tile].T
        gradient = jnp.dot(turned, hidden_ref[...], preferred_element_type=F32)
        extents = [part_rows] * (tile // part_rows)
        if i == 0:
            extents[:1] = [part_rows // 2] * 2
        if i == rows // tile - 1:
            extents[-1:] = [part_rows // 2] * 2
        at = i * tile
        for extent in extents:
            cut = slice(at, at + extent)
            base = at - i * tile
            current = down_ref[pl.ds(pl.multiple_of(me * rows + at, extent), extent), :].astype(F32)
            updates = adam_update(
                gradient[base : base + extent], current, one_ref[cut, :], two_ref[cut, :]
            )
            for q, update in enumerate(updates):
                results[q][cut, :] = update
                writes.append(
                    pltpu.make_async_copy(results[q].at[cut], outs[q].at[cut], sem.at[len(writes) // 3, q])
                )
                writes[-1].start()
            at += extent
    for write in writes:
        write.wait()
    writing.wait()


def adam_step(blocks, done, hidden_all, w_down, moment_one, moment_two, owners, parts):
    rows, units = moment_one.shape
    tokens = hidden_all.shape[0]
    tile = tile_of(rows, 128)
    part_rows = tile_of(tile, 64)
    return pl.pallas_call(
        functools.partial(adam_kernel, (owners, parts, blocks[0].shape[0] // owners, tile, part_rows)),
        out_shape=[jax.ShapeDtypeStruct((rows, units), F32)] * 3
        + [jax.ShapeDtypeStruct(done.shape, done.dtype)],
        in_specs=[VMEM] * (len(blocks) + 5),
        out_specs=[pl.BlockSpec(memory_space=pl.ANY)] * 4,
        scratch_shapes=[pltpu.VMEM((tokens, rows), BF16)]
        + [pltpu.VMEM((rows, units), F32)] * 3
        + [pltpu.SemaphoreType.DMA((rows // part_rows + 2, 3)), pltpu.SemaphoreType.DMA(())],
        compiler_params=pltpu.CompilerParams(vmem_limit_bytes=18 * MIB),
        cost_estimate=CHEAP,
        name="adam_step",
    )(*blocks, done, hidden_all, w_down, moment_one, moment_two)


def stack(order):
    count = len(order)
    total = sum(rows for _, _, rows in order)

    def kernel(*refs):
        out, sem = refs[-2:]
        started = []
        place = 0
        for n, (_, at, rows) in enumerate(order):
            started.append(
                pltpu.make_async_copy(
                    refs[n].at[at : at + rows], out.at[place : place + rows], sem.at[n]
                )
            )
            place += rows
        for copy in started:
            copy.start()
        for copy in started:
            copy.wait()

    return pl.pallas_call(
        kernel,
        out_shape=pltpu.VMEM((total, order[0][0].shape[1]), BF16),
        in_specs=[pl.BlockSpec(memory_space=pl.ANY)] * count,
        out_specs=VMEM,
        scratch_shapes=[pltpu.SemaphoreType.DMA((count,))],
        compiler_params=pltpu.CompilerParams(vmem_limit_bytes=4 * MIB),
        cost_estimate=CHEAP,
        name="stack",
    )(*[array for array, _, _ in order])


def adam_general(upstreams, hidden_all, w_down, moment_one, moment_two):
    owners = lax.axis_size("dp")
    sections = len(upstreams)
    segment = lax.axis_index("pipe")
    own = upstreams[0]
    for s in range(1, sections):
        own = jnp.where(segment == sections - 1 - s, upstreams[s], own)
    mine = lax.all_to_all(own, "dp", split_axis=1, concat_axis=0, tiled=True)
    share, rows = own.shape[0], mine.shape[1]
    turned = lax.all_gather(mine.reshape(owners, share, rows), "tensor", axis=1, tiled=True)
    gradient = lax.dot_general(
        turned.reshape(-1, rows), hidden_all, (((0,), (0,)), ((), ())), preferred_element_type=F32
    )
    at = lax.axis_index("dp") * rows
    current = lax.dynamic_slice_in_dim(w_down, at, rows, 0).astype(F32)
    return adam_update(gradient, current, moment_one, moment_two)


def from_peers(value, axis):
    size = lax.axis_size(axis)
    return [lax.ppermute(value, axis, [((i + k) % size, i) for i in range(size)]) for k in range(1, size)]


def to_peers(values, axis):
    size = lax.axis_size(axis)
    return [
        lax.ppermute(value, axis, [(i, (i + k) % size) for i in range(size)])
        for k, value in enumerate(values, 1)
    ]


def on_device(
    up_weight,
    down_weight,
    gate_act,
    hidden,
    block_input,
    norm_gain,
    loss_grad,
    moment_one,
    moment_two,
):
    sections = lax.axis_size("pipe")
    owners = lax.axis_size("dp")
    parts = lax.axis_size("tensor")
    width, units = down_weight.shape[1:]
    planned = sections == 4 and owners == 4 and width % (128 * owners) == 0 and units % (width // owners) == 0
    planned = planned and loss_grad.shape[0] * (width // owners) % (16 * units) == 0 and parts == 2
    share = loss_grad.shape[0]
    saved = hidden[0]
    half = saved.shape[0] // 2
    w_down, gates, loss = stage([down_weight[0], gate_act[0], loss_grad])
    turned = None
    upstreams = [loss]
    grads = []
    late = ()
    for layer in reversed(range(sections)):
        upstream = upstreams[-1]
        if planned and not layer:
            peers = [lax.all_gather(upstream, "tensor", axis=0, tiled=True)]
        else:
            peers = from_peers(upstream if grads else loss_grad, "tensor")
        if not grads:
            turned, kept, sent, (rows_in, *halves) = first_step(
                layer,
                upstream,
                peers,
                w_down,
                up_weight[0],
                gates,
                [block_input[0]],
                [saved] if planned else [],
            )
        elif planned and layer:
            unit_grad = unit_step(layer, upstream, peers, w_down, gates)
            kept, *sent = width_step(layer, unit_grad, turned, loss_grad.shape[0], late)
        else:
            kept, *sent = section_step(layer, upstream, peers, w_down, turned, gates, after=late)
        if planned and not layer:
            hidden_all = stack(
                [
                    (halves[0], 0, half),
                    (halves[1], 0, half),
                    (along_upper, 0, half),
                    (along_rest, 0, half),
                    (side_rest, 0, half),
                    (side_lower, 0, half),
                    (side_rest, half, half),
                    (along_rest, half, half),
                ]
            )
            packed = [(along_upper, half), (side_lower, half), (corner, 0)]
            own = collect(upstreams, blocks, packed, [kept, hidden_all])
        arrived = to_peers(sent, "tensor")
        window = len(grads)
        moving = ()
        if planned and window == 0:
            moving = [[(halves[0], 0, half), 1], [(halves[1], 0, half), 2]]
        elif planned and window == 1:
            moving = [
                [(halves[1], 0, half), (side_lower, 0, half)],
                [(halves[0], 0, half), (along_upper, 0, half)],
                [3],
            ]
        grad, cuts, handed = norm_step(
            layer,
            kept,
            arrived,
            upstream,
            rows_in,
            norm_gain,
            loss,
            earlier=grads if window >= sections - 2 else (),
            owners=owners if planned and window == 2 else 1,
            passed=moving,
        )
        grads.append(grad)
        if layer:
            upstreams.append(lax.ppermute(grad, "pipe", [(layer, layer - 1)]))
        if planned and layer:
            if window == 2:
                blocks = [
                    lax.ppermute(
                        cut,
                        ("pipe", "dp"),
                        [
                            (s * owners + i, (s - 1) * owners + (i ^ k))
                            for s in range(1, sections)
                            for i in range(owners)
                        ],
                    )
                    for k, cut in enumerate(cuts, 1)
                ]
            if window < 2:
                exchange = [
                    lax.ppermute(piece, "dp", [(i, i ^ k) for i in range(owners)])
                    for k, piece in enumerate(handed[:2], 1)
                ]
            if window == 0:
                along_upper, side_lower = exchange
                moments = stage_in_section(
                    [moment_one[0], moment_two[0]], lambda section: section != sections - 2, (), [grad]
                )
                late = [*exchange, *moments]
            elif window == 1:
                along_rest, side_rest = exchange
                start = (sections - 1) * owners
                corner = lax.ppermute(
                    handed[2], ("pipe", "dp"), [(start + i, start + (i ^ 3)) for i in range(owners)]
                )
                moments = stage_in_section(
                    [moment_one[0], moment_two[0]], lambda section: section == sections - 2, moments, [grad]
                )
                late = [*exchange, *moments]
            else:
                late = ()
    if planned:
        first, second, updated, grads[-1] = adam_step(
            [own, *from_peers(own, "tensor")], grads[-1], hidden_all, w_down, *moments, owners, parts
        )
    else:
        hidden_all = lax.all_gather(saved, "dp", axis=0, tiled=True)
        first, second, updated = adam_general(
            upstreams, hidden_all, w_down, moment_one[0], moment_two[0]
        )
    return (grads[-1][None], first[None], second[None], updated[None])


def solution(mesh):
    in_specs = (
        P("pipe", None, "tensor"),
        P("pipe", None, "tensor"),
        P("pipe", "dp", "tensor"),
        P("pipe", "dp", "tensor"),
        P("pipe", ("dp", "tensor"), None),
        P("pipe", None),
        P(("dp", "tensor"), None),
        P("pipe", "dp", "tensor"),
        P("pipe", "dp", "tensor"),
    )
    out_specs = (
        P("pipe", ("dp", "tensor"), None),
        P("pipe", "dp", "tensor"),
        P("pipe", "dp", "tensor"),
        P("pipe", "dp", "tensor"),
    )
    return jax.shard_map(
        on_device, mesh=mesh, in_specs=in_specs, out_specs=out_specs, check_vma=False
    )
```

```python
import functools
import math
import jax
import jax.numpy as jnp
from jax import lax
from jax.experimental import pallas as pl
from jax.experimental.pallas import tpu as pltpu
from jax.sharding import PartitionSpec as P

EPS_NORM = 1e-05
EPS_ADAM = 1e-08
BETA_ONE = 0.9
BETA_TWO = 0.95
RATE = 0.01
DECAY = 0.1
CORRECT_ONE = 1.0 - 0.9**10
CORRECT_TWO = 1.0 - 0.95**10

MIB = 2**20
VMEM = pl.BlockSpec(memory_space=pltpu.VMEM)
CHEAP = pl.CostEstimate(flops=0, bytes_accessed=0, transcendentals=0)
F32 = jnp.float32
BF16 = jnp.bfloat16


def tile_of(extent, most):
    tile = min(extent, most)
    while extent % tile:
        tile //= 2
    return tile


def copies(pairs, sem, chunks):
    started = []
    for n, (source, target) in enumerate(pairs):
        rows = source.shape[0] // chunks
        cut = [slice(c * rows, (c + 1) * rows) for c in range(chunks)]
        started.append(
            [pltpu.make_async_copy(source.at[r], target.at[r], sem.at[n, c]) for c, r in enumerate(cut)]
        )
    for array in started:
        for copy in array:
            copy.start()
    return started


def stage(arrays):
    count = len(arrays)

    def kernel(*refs):
        for array in copies(list(zip(refs[:count], refs[count:-1])), refs[-1], 2):
            for copy in array:
                copy.wait()

    return pl.pallas_call(
        kernel,
        out_shape=[pltpu.VMEM(a.shape, a.dtype) for a in arrays],
        in_specs=[pl.BlockSpec(memory_space=pltpu.HBM)] * count,
        out_specs=[VMEM] * count,
        scratch_shapes=[pltpu.SemaphoreType.DMA((count, 2))],
        compiler_params=pltpu.CompilerParams(vmem_limit_bytes=4 * MIB),
        cost_estimate=pl.CostEstimate(
            flops=0, bytes_accessed=sum(2 * a.size * a.dtype.itemsize for a in arrays), transcendentals=0
        ),
        name="stage",
    )(*[pltpu.with_memory_space_constraint(a, pltpu.HBM) for a in arrays])


def stage_in_section(arrays, wanted, held, after):
    count = len(arrays)

    def kernel(*refs):
        sources, targets, sem = refs[:count], refs[count + len(held) + len(after) : -1], refs[-1]

        @pl.when(wanted(lax.axis_index("pipe")))
        def _():
            for array in copies(list(zip(sources, targets)), sem, 2):
                for copy in array:
                    copy.wait()

    return pl.pallas_call(
        kernel,
        out_shape=[pltpu.VMEM(a.shape, a.dtype) for a in arrays],
        in_specs=[pl.BlockSpec(memory_space=pltpu.HBM)] * count
        + [VMEM] * len(held)
        + [pl.BlockSpec(memory_space=pl.ANY)] * len(after),
        out_specs=[VMEM] * count,
        input_output_aliases={count + n: n for n in range(len(held))},
        scratch_shapes=[pltpu.SemaphoreType.DMA((count, 2))],
        compiler_params=pltpu.CompilerParams(vmem_limit_bytes=4 * MIB),
        cost_estimate=CHEAP,
        name="stage_in_section",
    )(*[pltpu.with_memory_space_constraint(a, pltpu.HBM) for a in arrays], *held, *after)


def unit_grads(parts, share, rows_ref, down_ref, gate_ref, unit_ref):
    me = lax.axis_index("tensor")
    term = jnp.dot(rows_ref[...], down_ref[...], preferred_element_type=F32)
    for k in range(parts):
        at = pl.multiple_of(lax.rem(me + k, parts) * share, share)
        gates = gate_ref[pl.ds(at, share), :].astype(F32)
        unit_ref[k * share : (k + 1) * share, :] = (term[k * share : (k + 1) * share] * gates).astype(BF16)


def hand_out(share, term, cols, kept_ref, sent_refs):
    kept_ref[:, cols] = term[0:share]
    for k, ref in enumerate(sent_refs, 1):
        ref[:, cols] = term[k * share : (k + 1) * share].astype(BF16)


def fill_rows(share, rows_ref, own_ref, peer_refs):
    rows_ref[0:share, :] = own_ref[...]
    parts = rows_ref.shape[0] // share
    me = lax.axis_index("tensor")
    for k in range(1, parts):
        if peer_refs[0].shape[0] > share:
            at = pl.multiple_of(lax.rem(me + k, parts) * share, share)
            rows_ref[k * share : (k + 1) * share, :] = peer_refs[0][pl.ds(at, share), :]
        else:
            rows_ref[k * share : (k + 1) * share, :] = peer_refs[k - 1][...]


def step_kernel(layer, parts, pieces, own_ref, *refs):
    peer_refs, refs = refs[:pieces], refs[pieces:]
    down_ref, turned_ref, gate_ref, kept_ref = refs[:4]
    sent_refs = refs[4 : parts + 3]
    rows_ref, unit_ref = refs[parts + 3 :]
    share = own_ref.shape[0]

    @pl.when(lax.axis_index("pipe") == layer)
    def _():
        fill_rows(share, rows_ref, own_ref, peer_refs)
        unit_grads(parts, share, rows_ref, down_ref, gate_ref, unit_ref)
        term = jnp.dot(unit_ref[...], turned_ref[...], preferred_element_type=F32)
        hand_out(share, term, slice(None), kept_ref, sent_refs)


def unit_kernel(layer, parts, own_ref, *refs):
    peer_refs = refs[: parts - 1]
    down_ref, gate_ref, unit_ref, rows_ref = refs[parts - 1 :]
    share = own_ref.shape[0]

    @pl.when(lax.axis_index("pipe") == layer)
    def _():
        fill_rows(share, rows_ref, own_ref, peer_refs)
        unit_grads(parts, share, rows_ref, down_ref, gate_ref, unit_ref)


def unit_step(layer, own, peers, w_down, gates):
    parts = len(peers) + 1
    rows = own.shape[0] * parts
    return pl.pallas_call(
        functools.partial(unit_kernel, layer, parts),
        out_shape=jax.ShapeDtypeStruct((rows, w_down.shape[1]), BF16),
        in_specs=[VMEM] * (parts + 2),
        out_specs=VMEM,
        scratch_shapes=[pltpu.VMEM((rows, own.shape[1]), BF16)],
        compiler_params=pltpu.CompilerParams(vmem_limit_bytes=12 * MIB),
        cost_estimate=CHEAP,
        name="unit_step",
    )(own, *peers, w_down, gates)


def width_step(layer, unit_grad, turned, share, after):
    width = turned.shape[1]
    parts = unit_grad.shape[0] // share

    def kernel(unit_ref, turned_ref, *refs):
        kept_ref, *sent_refs = refs[len(after) :]

        @pl.when(lax.axis_index("pipe") == layer)
        def _():
            term = jnp.dot(unit_ref[...], turned_ref[...], preferred_element_type=F32)
            hand_out(share, term, slice(None), kept_ref, sent_refs)

    return pl.pallas_call(
        kernel,
        out_shape=[jax.ShapeDtypeStruct((share, width), F32)]
        + [jax.ShapeDtypeStruct((share, width), BF16)] * (parts - 1),
        in_specs=[VMEM, VMEM] + [pl.BlockSpec(memory_space=pl.ANY)] * len(after),
        out_specs=[VMEM] * parts,
        compiler_params=pltpu.CompilerParams(vmem_limit_bytes=12 * MIB),
        cost_estimate=CHEAP,
        name="width_step",
    )(unit_grad, turned, *after)


def first_kernel(layer, parts, pieces, further, own_ref, *refs):
    peer_refs, refs = refs[:pieces], refs[pieces:]
    down_ref, up_ref, gate_ref = refs[:3]
    count = 1 + max((n for n, _ in further), default=-1)
    source_refs, refs = refs[3 : 3 + count], refs[3 + count :]
    turned_ref, kept_ref = refs[:2]
    sent_refs = refs[2 : parts + 1]
    staged_refs = refs[parts + 1 : parts + 1 + len(further)]
    rows_ref, unit_ref, held_ref, sem, further_sem = refs[parts + 1 + len(further) :]
    share = own_ref.shape[0]
    chunks = sem.shape[1]
    size = held_ref.shape[0] // chunks
    (arriving,) = copies([(up_ref, held_ref)], sem, chunks)
    pairs = [(source_refs[n].at[rows], staged) for (n, rows), staged in zip(further, staged_refs)]
    behind = copies(pairs, further_sem, 1)
    starts = lax.axis_index("pipe") == layer

    def turn(first, count):
        for c in range(first, first + count):
            arriving[c].wait()
        cols = slice(first * size, (first + count) * size)
        turned_ref[:, cols] = held_ref[cols, :].T

    def product(first, count):
        cols = slice(first * size, (first + count) * size)
        term = jnp.dot(unit_ref[...], turned_ref[:, cols], preferred_element_type=F32)
        hand_out(share, term, cols, kept_ref, sent_refs)

    @pl.when(starts)
    def _():
        fill_rows(share, rows_ref, own_ref, peer_refs)
        unit_grads(parts, share, rows_ref, down_ref, gate_ref, unit_ref)
        turn(0, 2)
        for c in range(2, chunks, 2):
            turn(c, 2)
            product(c - 2, 2)
        product(chunks - 2, 2)

    @pl.when(jnp.logical_not(starts))
    def _():
        for c in range(chunks):
            turn(c, 1)

    for (copy,) in behind:
        copy.wait()


def first_step(layer, own, peers, w_down, w_up, gates, arrays, split):
    share, width = own.shape
    units = w_down.shape[1]
    parts = lax.axis_size("tensor")
    rows = share * parts
    further = [(n, slice(0, a.shape[0])) for n, a in enumerate(arrays)]
    for n, a in enumerate(split, len(arrays)):
        half = a.shape[0] // 2
        further += [(n, slice(0, half)), (n, slice(half, 2 * half))]
    sources = [*arrays, *split]
    hbm = pl.BlockSpec(memory_space=pltpu.HBM)
    outs = pl.pallas_call(
        functools.partial(first_kernel, layer, parts, len(peers), further),
        out_shape=[pltpu.VMEM((units, width), BF16), jax.ShapeDtypeStruct((share, width), F32)]
        + [jax.ShapeDtypeStruct((share, width), BF16)] * (parts - 1)
        + [pltpu.VMEM((rows.stop - rows.start, sources[n].shape[1]), BF16) for n, rows in further],
        in_specs=[VMEM] * (len(peers) + 2) + [hbm, VMEM] + [hbm] * len(sources),
        out_specs=[VMEM] * (1 + parts + len(further)),
        scratch_shapes=[
            pltpu.VMEM((rows, width), BF16),
            pltpu.VMEM((rows, units), BF16),
            pltpu.VMEM((width, units), BF16),
            pltpu.SemaphoreType.DMA((1, 8)),
            pltpu.SemaphoreType.DMA((len(further), 1)),
        ],
        compiler_params=pltpu.CompilerParams(vmem_limit_bytes=20 * MIB),
        cost_estimate=CHEAP,
        name="first_step",
    )(
        own,
        *peers,
        w_down,
        pltpu.with_memory_space_constraint(w_up, pltpu.HBM),
        gates,
        *[pltpu.with_memory_space_constraint(a, pltpu.HBM) for a in sources],
    )
    return outs[0], outs[1], outs[2 : parts + 1], outs[parts + 1 :]


def section_step(layer, own, peers, w_down, turned, gates, after=()):
    share, width = own.shape
    units = w_down.shape[1]
    pieces = len(peers)
    parts = lax.axis_size("tensor")
    rows = share * parts

    def kernel(*refs):
        step_kernel(layer, parts, pieces, *refs[: pieces + 4], *refs[pieces + 4 + len(after) :])

    return pl.pallas_call(
        kernel,
        out_shape=[jax.ShapeDtypeStruct((share, width), F32)]
        + [jax.ShapeDtypeStruct((share, width), BF16)] * (parts - 1),
        in_specs=[VMEM] * (pieces + 4) + [pl.BlockSpec(memory_space=pl.ANY)] * len(after),
        out_specs=[VMEM] * parts,
        scratch_shapes=[pltpu.VMEM((rows, width), BF16), pltpu.VMEM((rows, units), BF16)],
        compiler_params=pltpu.CompilerParams(vmem_limit_bytes=12 * MIB),
        cost_estimate=CHEAP,
        name="section_step",
    )(own, *peers, w_down, turned, gates, *after)


def pack_block(source, k, target, at):
    owners = lax.axis_size("dp")
    tokens, width = source.shape
    size = width // owners
    rows = tokens * size // target.shape[1]
    column = pl.multiple_of((lax.axis_index("dp") ^ k) * size, size)
    for q in range(tokens // rows):
        target[at : at + rows, q * size : (q + 1) * size] = source[
            q * rows : (q + 1) * rows, pl.ds(column, size)
        ]
    return rows


def norm_kernel(layer, parts, earlier, owners, passed, handed, kept_ref, *refs):
    arrived = refs[: parts - 1]
    up_ref, in_ref, gain_ref = refs[parts - 1 : parts + 2]
    refs = refs[parts + 2 :]
    earlier_refs, refs = refs[:earlier], refs[earlier:]
    first_ref, pass_refs, refs = refs[0], refs[1 : 1 + passed], refs[1 + passed :]
    out_ref, block_refs, handed_refs = refs[0], refs[1 : len(refs) - len(handed)], refs[len(refs) - len(handed) :]
    segment = lax.axis_index("pipe")

    def cut(source):
        size = source.shape[1] // owners
        for k, ref in enumerate(block_refs, 1):
            at = pl.multiple_of((lax.axis_index("dp") ^ k) * size, size)
            ref[...] = source[:, pl.ds(at, size)]

    @pl.when(segment == layer)
    def _():
        normed = kept_ref[...]
        for ref in arrived:
            normed = normed + ref[...].astype(F32)
        rows_in = in_ref[...].astype(F32)
        inverse_rms = lax.rsqrt(jnp.mean(rows_in * rows_in, axis=-1, keepdims=True) + EPS_NORM)
        scaled = normed * gain_ref[...]
        mean_term = jnp.mean(rows_in * scaled, axis=-1, keepdims=True)
        out_ref[...] = (
            up_ref[...].astype(F32)
            + inverse_rms * scaled
            - rows_in * (inverse_rms * inverse_rms * inverse_rms * mean_term)
        ).astype(BF16)
        cut(out_ref)

    for above, ref in enumerate(earlier_refs):

        @pl.when(segment == layer + earlier - above)
        def _(ref=ref):
            cut(ref)
            if layer == 0:
                out_ref[...] = ref[...]

    sources = iter(pass_refs)
    for recipe, target in zip(handed, handed_refs):
        at = 0
        for piece in recipe:
            if isinstance(piece, int):
                at += pack_block(first_ref, piece, target, at)
            else:
                start, rows = piece
                target[at : at + rows, :] = next(sources)[start : start + rows, :]
                at += rows


def norm_step(layer, kept, arrived, upstream, rows_in, gain, first, earlier=(), owners=1, passed=()):
    parts = len(arrived) + 1
    share, width = upstream.shape
    block = jax.ShapeDtypeStruct((share, width // owners), BF16)
    recipes = [[p if isinstance(p, int) else p[1:] for p in group] for group in passed]
    handed = []
    for group in passed:
        units = passed[0][0][0].shape[1]
        block_rows = share * (width // lax.axis_size("dp")) // units
        rows = sum(block_rows if isinstance(p, int) else p[2] for p in group)
        handed.append(jax.ShapeDtypeStruct((rows, units), BF16))
    passed = [p[0] for group in passed for p in group if not isinstance(p, int)]
    outs = pl.pallas_call(
        functools.partial(norm_kernel, layer, parts, len(earlier), owners, len(passed), recipes),
        out_shape=[jax.ShapeDtypeStruct(upstream.shape, BF16)]
        + [block] * (owners - 1)
        + handed,
        in_specs=[VMEM] * (parts + 4 + len(earlier) + len(passed)),
        out_specs=[VMEM] * (owners + len(handed)),
        compiler_params=pltpu.CompilerParams(vmem_limit_bytes=8 * MIB),
        cost_estimate=CHEAP,
        name="norm_step",
    )(kept, *arrived, upstream, rows_in, gain, *earlier, first, *passed)
    return outs[0], outs[1:owners], outs[owners:]


def collect(upstreams, blocks, packed, after):
    sections = len(upstreams)
    owners = len(blocks) + 1
    share, size = blocks[0].shape
    count = sections + 2 * len(blocks)

    def kernel(*refs):
        block_refs = refs[: owners - 1][::-1]
        refs = [*refs[owners - 1 : owners - 1 + sections], *block_refs, *refs[owners - 1 + sections :]]
        out_ref = refs[-1]
        segment = lax.axis_index("pipe")
        at = pl.multiple_of(lax.axis_index("dp") * size, size)
        for s in range(sections):

            @pl.when(segment == sections - 1 - s)
            def _(s=s):
                out_ref[0:share, :] = refs[s][:, pl.ds(at, size)]

        @pl.when(segment < sections - 1)
        def _():
            for k in range(1, owners):
                out_ref[k * share : (k + 1) * share, :] = refs[sections + k - 1][...]

        @pl.when(segment == sections - 1)
        def _():
            for k in range(1, owners):
                source, start = refs[sections + owners + k - 2], packed[k - 1][1]
                pieces = source.shape[1] // size
                rows = share // pieces
                for q in range(pieces):
                    out_ref[k * share + q * rows : k * share + (q + 1) * rows, :] = source[
                        start : start + rows, q * size : (q + 1) * size
                    ]

    return pl.pallas_call(
        kernel,
        out_shape=jax.ShapeDtypeStruct((owners * share, size), BF16),
        in_specs=[VMEM] * count + [pl.BlockSpec(memory_space=pl.ANY)] * len(after),
        out_specs=VMEM,
        compiler_params=pltpu.CompilerParams(vmem_limit_bytes=4 * MIB),
        cost_estimate=CHEAP,
        name="collect",
    )(*blocks[::-1], *upstreams, *[array for array, _ in packed], *after)


def adam_update(gradient, current, moment_one, moment_two):
    first = BETA_ONE * moment_one + (1.0 - BETA_ONE) * gradient
    second = BETA_TWO * moment_two + (1.0 - BETA_TWO) * gradient * gradient
    root = second * lax.rsqrt(second)
    scale = math.sqrt(CORRECT_TWO)
    step = (first * (RATE * scale / CORRECT_ONE)) / (root + EPS_ADAM * scale)
    return first, second, (1.0 - RATE * DECAY) * current - step


def adam_kernel(sizes, *refs):
    owners, parts, share, tile, part_rows = sizes
    up_refs = refs[:parts]
    refs = refs[parts:]
    done_ref, hidden_ref, down_ref, one_ref, two_ref = refs[:5]
    outs, done_out = refs[5:8], refs[8]
    rows_ref, *results, sem, done_sem = refs[9:]
    writing = pltpu.make_async_copy(done_ref, done_out, done_sem)
    writing.start()
    rows = rows_ref.shape[1]
    me = lax.axis_index("dp")
    part = lax.axis_index("tensor")
    for p in range(parts):
        for k in range(owners):
            at = k * parts + lax.rem(part + p, parts)
            rows_ref[pl.ds(pl.multiple_of(at * share, share), share), :] = up_refs[p][
                k * share : (k + 1) * share, :
            ]
    writes = []
    for i in range(rows // tile):
        turned = rows_ref[:, i * tile : (i + 1) * tile].T
        gradient = jnp.dot(turned, hidden_ref[...], preferred_element_type=F32)
        extents = [part_rows] * (tile // part_rows)
        if i == 0:
            extents[:1] = [part_rows // 2] * 2
        if i == rows // tile - 1:
            extents[-1:] = [part_rows // 2] * 2
        at = i * tile
        for extent in extents:
            cut = slice(at, at + extent)
            base = at - i * tile
            current = down_ref[pl.ds(pl.multiple_of(me * rows + at, extent), extent), :].astype(F32)
            updates = adam_update(
                gradient[base : base + extent], current, one_ref[cut, :], two_ref[cut, :]
            )
            for q, update in enumerate(updates):
                results[q][cut, :] = update
                writes.append(
                    pltpu.make_async_copy(results[q].at[cut], outs[q].at[cut], sem.at[len(writes) // 3, q])
                )
                writes[-1].start()
            at += extent
    for write in writes:
        write.wait()
    writing.wait()


def adam_step(blocks, done, hidden_all, w_down, moment_one, moment_two, owners, parts):
    rows, units = moment_one.shape
    tokens = hidden_all.shape[0]
    tile = tile_of(rows, 128)
    part_rows = tile_of(tile, 64)
    return pl.pallas_call(
        functools.partial(adam_kernel, (owners, parts, blocks[0].shape[0] // owners, tile, part_rows)),
        out_shape=[jax.ShapeDtypeStruct((rows, units), F32)] * 3
        + [jax.ShapeDtypeStruct(done.shape, done.dtype)],
        in_specs=[VMEM] * (len(blocks) + 5),
        out_specs=[pl.BlockSpec(memory_space=pl.ANY)] * 4,
        scratch_shapes=[pltpu.VMEM((tokens, rows), BF16)]
        + [pltpu.VMEM((rows, units), F32)] * 3
        + [pltpu.SemaphoreType.DMA((rows // part_rows + 2, 3)), pltpu.SemaphoreType.DMA(())],
        compiler_params=pltpu.CompilerParams(vmem_limit_bytes=18 * MIB),
        cost_estimate=CHEAP,
        name="adam_step",
    )(*blocks, done, hidden_all, w_down, moment_one, moment_two)


def stack(order):
    count = len(order)
    total = sum(rows for _, _, rows in order)

    def kernel(*refs):
        out, sem = refs[-2:]
        started = []
        place = 0
        for n, (_, at, rows) in enumerate(order):
            started.append(
                pltpu.make_async_copy(
                    refs[n].at[at : at + rows], out.at[place : place + rows], sem.at[n]
                )
            )
            place += rows
        for copy in started:
            copy.start()
        for copy in started:
            copy.wait()

    return pl.pallas_call(
        kernel,
        out_shape=pltpu.VMEM((total, order[0][0].shape[1]), BF16),
        in_specs=[pl.BlockSpec(memory_space=pl.ANY)] * count,
        out_specs=VMEM,
        scratch_shapes=[pltpu.SemaphoreType.DMA((count,))],
        compiler_params=pltpu.CompilerParams(vmem_limit_bytes=4 * MIB),
        cost_estimate=CHEAP,
        name="stack",
    )(*[array for array, _, _ in order])


def adam_general(upstreams, hidden_all, w_down, moment_one, moment_two):
    owners = lax.axis_size("dp")
    sections = len(upstreams)
    segment = lax.axis_index("pipe")
    own = upstreams[0]
    for s in range(1, sections):
        own = jnp.where(segment == sections - 1 - s, upstreams[s], own)
    mine = lax.all_to_all(own, "dp", split_axis=1, concat_axis=0, tiled=True)
    share, rows = own.shape[0], mine.shape[1]
    turned = lax.all_gather(mine.reshape(owners, share, rows), "tensor", axis=1, tiled=True)
    gradient = lax.dot_general(
        turned.reshape(-1, rows), hidden_all, (((0,), (0,)), ((), ())), preferred_element_type=F32
    )
    at = lax.axis_index("dp") * rows
    current = lax.dynamic_slice_in_dim(w_down, at, rows, 0).astype(F32)
    return adam_update(gradient, current, moment_one, moment_two)


def from_peers(value, axis):
    size = lax.axis_size(axis)
    return [lax.ppermute(value, axis, [((i + k) % size, i) for i in range(size)]) for k in range(1, size)]


def to_peers(values, axis):
    size = lax.axis_size(axis)
    return [
        lax.ppermute(value, axis, [(i, (i + k) % size) for i in range(size)])
        for k, value in enumerate(values, 1)
    ]


def on_device(
    up_weight,
    down_weight,
    gate_act,
    hidden,
    block_input,
    norm_gain,
    loss_grad,
    moment_one,
    moment_two,
):
    sections = lax.axis_size("pipe")
    owners = lax.axis_size("dp")
    parts = lax.axis_size("tensor")
    width, units = down_weight.shape[1:]
    planned = sections == 4 and owners == 4 and width % (128 * owners) == 0 and units % (width // owners) == 0
    planned = planned and loss_grad.shape[0] * (width // owners) % (16 * units) == 0 and parts == 2
    share = loss_grad.shape[0]
    saved = hidden[0]
    half = saved.shape[0] // 2
    w_down, gates, loss = stage([down_weight[0], gate_act[0], loss_grad])
    turned = None
    upstreams = [loss]
    grads = []
    late = ()
    for layer in reversed(range(sections)):
        upstream = upstreams[-1]
        if planned and not layer:
            peers = [lax.all_gather(upstream, "tensor", axis=0, tiled=True)]
        else:
            peers = from_peers(upstream if grads else loss_grad, "tensor")
        if not grads:
            turned, kept, sent, (rows_in, *halves) = first_step(
                layer,
                upstream,
                peers,
                w_down,
                up_weight[0],
                gates,
                [block_input[0]],
                [saved] if planned else [],
            )
        elif planned and layer:
            unit_grad = unit_step(layer, upstream, peers, w_down, gates)
            kept, *sent = width_step(layer, unit_grad, turned, loss_grad.shape[0], late)
        else:
            kept, *sent = section_step(layer, upstream, peers, w_down, turned, gates, after=late)
        if planned and not layer:
            hidden_all = stack(
                [
                    (halves[0], 0, half),
                    (halves[1], 0, half),
                    (along_upper, 0, half),
                    (along_rest, 0, half),
                    (side_rest, 0, half),
                    (side_lower, 0, half),
                    (side_rest, half, half),
                    (along_rest, half, half),
                ]
            )
            packed = [(along_upper, half), (side_lower, half), (corner, 0)]
            own = collect(upstreams, blocks, packed, [kept, hidden_all])
        arrived = to_peers(sent, "tensor")
        window = len(grads)
        moving = ()
        if planned and window == 0:
            moving = [[(halves[0], 0, half), 1], [(halves[1], 0, half), 2]]
        elif planned and window == 1:
            moving = [
                [(halves[1], 0, half), (side_lower, 0, half)],
                [(halves[0], 0, half), (along_upper, 0, half)],
                [3],
            ]
        grad, cuts, handed = norm_step(
            layer,
            kept,
            arrived,
            upstream,
            rows_in,
            norm_gain,
            loss,
            earlier=grads if window >= sections - 2 else (),
            owners=owners if planned and window == 2 else 1,
            passed=moving,
        )
        grads.append(grad)
        if layer:
            upstreams.append(lax.ppermute(grad, "pipe", [(layer, layer - 1)]))
        if planned and layer:
            if window == 2:
                blocks = [
                    lax.ppermute(
                        cut,
                        ("pipe", "dp"),
                        [
                            (s * owners + i, (s - 1) * owners + (i ^ k))
                            for s in range(1, sections)
                            for i in range(owners)
                        ],
                    )
                    for k, cut in enumerate(cuts, 1)
                ]
            if window < 2:
                exchange = [
                    lax.ppermute(piece, "dp", [(i, i ^ k) for i in range(owners)])
                    for k, piece in enumerate(handed[:2], 1)
                ]
            if window == 0:
                along_upper, side_lower = exchange
                moments = stage_in_section(
                    [moment_one[0], moment_two[0]], lambda section: section != sections - 2, (), [grad]
                )
                late = [*exchange, *moments]
            elif window == 1:
                along_rest, side_rest = exchange
                start = (sections - 1) * owners
                corner = lax.ppermute(
                    handed[2], ("pipe", "dp"), [(start + i, start + (i ^ 3)) for i in range(owners)]
                )
                moments = stage_in_section(
                    [moment_one[0], moment_two[0]], lambda section: section == sections - 2, moments, [grad]
                )
                late = [*exchange, *moments, corner]
            else:
                late = ()
    if planned:
        first, second, updated, grads[-1] = adam_step(
            [own, *from_peers(own, "tensor")], grads[-1], hidden_all, w_down, *moments, owners, parts
        )
    else:
        hidden_all = lax.all_gather(saved, "dp", axis=0, tiled=True)
        first, second, updated = adam_general(
            upstreams, hidden_all, w_down, moment_one[0], moment_two[0]
        )
    return (grads[-1][None], first[None], second[None], updated[None])


def solution(mesh):
    in_specs = (
        P("pipe", None, "tensor"),
        P("pipe", None, "tensor"),
        P("pipe", "dp", "tensor"),
        P("pipe", "dp", "tensor"),
        P("pipe", ("dp", "tensor"), None),
        P("pipe", None),
        P(("dp", "tensor"), None),
        P("pipe", "dp", "tensor"),
        P("pipe", "dp", "tensor"),
    )
    out_specs = (
        P("pipe", ("dp", "tensor"), None),
        P("pipe", "dp", "tensor"),
        P("pipe", "dp", "tensor"),
        P("pipe", "dp", "tensor"),
    )
    return jax.shard_map(
        on_device, mesh=mesh, in_specs=in_specs, out_specs=out_specs, check_vma=False
    )
```
